128 devices in a mesh: dp: 64 (over y, x, z), tensor: 2 (over core).
Axes of the slice: x: 4, y: 4, z: 4, core: 2. Of those that a mesh axis runs over, the one named last changes fastest.
Arguments:
- tokens: bfloat16 [65536, 768], P(('dp', 'tensor')), may hold values from -6 to 6
- segment_ids: int32 [65536], P('dp'), may hold values from 0 to 2, as said below
- cotangent: bfloat16 [65536, 768], P(('dp', 'tensor')), may hold values from -6 to 6
- norm_gains: float32 [2, 768], replicated, may hold values from 0.1 to 1.9
- gains_moment: float32 [2, 768], replicated, may hold values from -1536 to 1536
- inbound: float32 [3, 768, 768], P(None, 'dp', 'tensor'), may hold values from -0.21875 to 0.21875
- outbound: float32 [768, 768], P('tensor', 'dp'), may hold values from -1.75 to 1.75
- expand: float32 [2, 768, 3072], P(None, 'dp', 'tensor'), may hold values from -0.21875 to 0.21875
- shrink: float32 [3072, 768], P('tensor', 'dp'), may hold values from -0.15625 to 0.15625
- inbound_moment: float32 [3, 768, 768], P(None, 'dp', 'tensor'), may hold values from -1.25 to 1.25
- outbound_moment: float32 [768, 768], P('tensor', 'dp'), may hold values from -0.25 to 0.25
- expand_moment: float32 [2, 768, 3072], P(None, 'dp', 'tensor'), may hold values from -0.625 to 0.625
- shrink_moment: float32 [3072, 768], P('tensor', 'dp'), may hold values from -0.625 to 0.625
- inbound_error: float32 [64, 3, 768, 768], P('dp', None, None, 'tensor'), may hold values from -96 to 96
- outbound_error: float32 [64, 768, 768], P('dp', 'tensor'), may hold values from -20 to 20
- expand_error: float32 [64, 2, 768, 3072], P('dp', None, None, 'tensor'), may hold values from -48 to 48
- shrink_error: float32 [64, 3072, 768], P('dp', 'tensor'), may hold values from -96 to 96
- inbound_start: float32 [3, 768, 8], P(None, 'tensor'), may hold values from -6 to 6
- outbound_start: float32 [768, 8], replicated, may hold values from -6 to 6
- expand_start: float32 [2, 3072, 8], P(None, 'tensor'), may hold values from -6 to 6
- shrink_start: float32 [768, 8], replicated, may hold values from -6 to 6
Outputs:
- layer_output: bfloat16 [65536, 768], P(('dp', 'tensor'))
- input_grad: bfloat16 [65536, 768], P(('dp', 'tensor'))
- gains_momentum: float32 [2, 768], replicated
- gains_updated: float32 [2, 768], replicated
- inbound_momentum: float32 [3, 768, 768], P(None, 'dp', 'tensor')
- outbound_momentum: float32 [768, 768], P('tensor', 'dp')
- expand_momentum: float32 [2, 768, 3072], P(None, 'dp', 'tensor')
- shrink_momentum: float32 [3072, 768], P('tensor', 'dp')
- inbound_updated: float32 [3, 768, 768], P(None, 'dp', 'tensor')
- outbound_updated: float32 [768, 768], P('tensor', 'dp')
- expand_updated: float32 [2, 768, 3072], P(None, 'dp', 'tensor')
- shrink_updated: float32 [3072, 768], P('tensor', 'dp')
- inbound_residue: float32 [64, 3, 768, 768], P('dp', None, None, 'tensor')
- outbound_residue: float32 [64, 768, 768], P('dp', 'tensor')
- expand_residue: float32 [64, 2, 768, 3072], P('dp', None, None, 'tensor')
- shrink_residue: float32 [64, 3072, 768], P('dp', 'tensor')
- inbound_left: float32 [3, 768, 8], replicated
- inbound_right: float32 [3, 768, 8], P(None, 'tensor')
- outbound_left: float32 [768, 8], P('tensor')
- outbound_right: float32 [768, 8], replicated
- expand_left: float32 [2, 768, 8], replicated
- expand_right: float32 [2, 3072, 8], P(None, 'tensor')
- shrink_left: float32 [3072, 8], P('tensor')
- shrink_right: float32 [768, 8], replicated
The draws below stay inside these ranges and needn't reach their ends.
Inputs may be any that keep to these rules, and one draw needn't show every extreme that they name: `segment_ids`: within each sequence of 1024 rows the ids never fall and take each of 0, 1 and 2; documents 0 and 2 hold 128 positions or more, and document 1 covers positions 511 and 512.
All inputs are finite; a program needn't handle non-finite values.
Results may differ from the reference program's by a relative error of at most 0.018.
Values may be sent and summed in bfloat16 or wider, within the bound.
No kernel may reach another device: no remote copies, remote signals or barrier semaphores. Data moves between devices by JAX's collectives and lax.ppermute only.
A program may use at most 256 MiB of HBM per device.

```python
import jax
import jax.numpy as jnp
from jax import lax

D = 768
HEADS = 12
HEAD_DIM = 64
FF = 3072
RANK = 8
BLOCK = 256
SEQ = 1024
TOKENS = 65536
N_DP = 64


def draw_segment_ids(key, part):
    key = jax.random.fold_in(key, 17)
    sequences = TOKENS // SEQ
    first_key, second_key = jax.random.split(key)
    middle = SEQ // 2
    first_cut = jax.random.randint(first_key, (sequences, 1), middle // 4, middle // 2 + 1)
    second_cut = jax.random.randint(second_key, (sequences, 1), middle + middle // 2, SEQ - middle // 4 + 1)
    positions = jnp.arange(SEQ, dtype=jnp.int32)[None, :]
    labels = (positions >= first_cut).astype(jnp.int32) + (positions >= second_cut).astype(jnp.int32)
    return labels.reshape(TOKENS)


def steps_of(stream_key, dims, cuts, smallest, top_value):
    gain, own = 1.0, jax.random.fold_in(stream_key, 6)
    for dim, parts in cuts:
        heights = jnp.exp(jax.random.uniform(jax.random.fold_in(own, dim), (parts,), jnp.float32, smallest / len(cuts), top_value / len(cuts)))
        gain = gain * jnp.repeat(heights, dims[dim] // parts).reshape([-1 if axis == dim else 1 for axis in range(len(dims))])
    return gain


def gaussian(stream_key, shape, spread, reach, pieces=(), kind=jnp.bfloat16):
    values = jax.random.normal(stream_key, shape, jnp.float32) * spread
    if len(pieces) > 0:
        values = steps_of(stream_key, shape, pieces, -0.22, 0.18) * values
    return jnp.clip(values, min=-reach, max=reach).astype(kind)


def setup_inputs(seed: int = 0) -> dict:
    splits = jax.random.split(jax.random.key(seed), 22)
    return {
        "tokens": gaussian(splits[0], (TOKENS, D), 1.0, 6.0, ((0, 128),)),
        "segment_ids": draw_segment_ids(jax.random.fold_in(splits[21], 71), 0),
        "cotangent": gaussian(splits[2], (TOKENS, D), 1.0, 6.0, ((0, 128),)),
        "norm_gains": jnp.clip(1.0 + 0.18 * jax.random.normal(splits[3], (2, D), jnp.float32), 0.1, 1.9),
        "gains_moment": gaussian(splits[4], (2, D), (TOKENS ** 0.5), 1536.0, (), jnp.float32),
        "inbound": gaussian(splits[5], (3, D, D), D ** -0.5, 0.21875, ((1, 64), (2, 2)), jnp.float32),
        "outbound": gaussian(splits[6], (D, D), (max(D // 64, 4)) ** -0.5, 1.75, ((0, 2), (1, 64)), jnp.float32),
        "expand": gaussian(splits[7], (2, D, FF), D ** -0.5, 0.21875, ((1, 64), (2, 2)), jnp.float32),
        "shrink": gaussian(splits[8], (FF, D), (FF // 2) ** -0.5, 0.15625, ((0, 2), (1, 64)), jnp.float32),
        "inbound_moment": gaussian(splits[9], (3, D, D), (0.5 * (SEQ * RANK) ** 0.5 * (D * N_DP) ** -0.5), 1.25, ((1, 64), (2, 2)), jnp.float32),
        "outbound_moment": gaussian(splits[10], (D, D), (0.1 * (SEQ * RANK) ** 0.5 * (D * N_DP) ** -0.5), 0.25, ((0, 2), (1, 64)), jnp.float32),
        "expand_moment": gaussian(splits[11], (2, D, FF), (0.25 * (SEQ * RANK) ** 0.5 * (D * N_DP) ** -0.5), 0.625, ((1, 64), (2, 2)), jnp.float32),
        "shrink_moment": gaussian(splits[12], (FF, D), (0.5 * (SEQ * RANK) ** 0.5 * (FF * N_DP) ** -0.5), 0.625, ((0, 2), (1, 64)), jnp.float32),
        "inbound_error": gaussian(splits[13], (N_DP, 3, D, D), (0.5 * SEQ ** 0.5), 96.0, ((0, 64), (3, 2)), jnp.float32),
        "outbound_error": gaussian(splits[14], (N_DP, D, D), (0.1 * SEQ ** 0.5), 20.0, ((0, 64), (1, 2)), jnp.float32),
        "expand_error": gaussian(splits[15], (N_DP, 2, D, FF), (0.25 * SEQ ** 0.5), 48.0, ((0, 64), (3, 2)), jnp.float32),
        "shrink_error": gaussian(splits[16], (N_DP, FF, D), (0.5 * SEQ ** 0.5), 96.0, ((0, 64), (1, 2)), jnp.float32),
        "inbound_start": gaussian(splits[17], (3, D, RANK), 1.0, 6.0, ((1, 2),), jnp.float32),
        "outbound_start": gaussian(splits[18], (D, RANK), 1.0, 6.0, (), jnp.float32),
        "expand_start": gaussian(splits[19], (2, FF, RANK), 1.0, 6.0, ((1, 2),), jnp.float32),
        "shrink_start": gaussian(splits[20], (D, RANK), 1.0, 6.0, (), jnp.float32),
    }


@jax.custom_vjp
def low(v):
    return lax.optimization_barrier(v.astype(jnp.bfloat16)).astype(jnp.float32)

@jax.custom_vjp
def low_back(v):
    return v

def low_keep(v):
    return (low(v), None)

def low_pass(kept, grad):
    return (grad,)

def back_keep(v):
    return (v, None)

def back_low(kept, grad):
    return (low(grad),)
low.defvjp(low_keep, low_pass)
low_back.defvjp(back_keep, back_low)
norm_epsilon = 1e-06
factor_epsilon = 1e-06
momentum_decay = 0.9
rate_inbound = 0.2
rate_outbound = 6.0
rate_expand = 0.3
rate_shrink = 0.25
rate_gains = 0.0005
rope_base = 10000.0
highest = lax.Precision.HIGHEST

def rotate(inputs, cos_table, sin_table):
    middle = inputs.shape[-1] // 2
    turned = jnp.concatenate([-inputs[..., middle:], inputs[..., :middle]], axis=-1)
    return inputs * cos_table[:, None, :] + turned * sin_table[:, None, :]

def rope_tables(segment_row):
    length = segment_row.shape[0]
    before = lax.optimization_barrier(jnp.sum((segment_row[None, :] < segment_row[:, None]).astype(jnp.int32), axis=1))
    places = (jnp.arange(length, dtype=jnp.int32) - before).astype(jnp.float32)
    inverse = rope_base ** (-(jnp.arange(HEAD_DIM // 2, dtype=jnp.float32) * 2.0) / HEAD_DIM)
    angles = places[:, None] * inverse[None, :]
    angles = jnp.concatenate([angles, angles], axis=1)
    return (jnp.cos(angles), jnp.sin(angles))

def allowed_pairs(segment_row):
    block_ids = jnp.arange(segment_row.shape[0], dtype=jnp.int32) // BLOCK
    return (segment_row[:, None] == segment_row[None, :]) & (block_ids[:, None] >= block_ids[None, :])

def decoder_layer(residual, gains, inbound, outbound, expand, shrink, cos_table, sin_table, allowed):
    seq_len = residual.shape[0]
    head_shape = (seq_len, HEADS, HEAD_DIM)
    score_scale = HEAD_DIM ** (-0.5)
    inverse_first = lax.rsqrt(lax.optimization_barrier(jnp.mean(residual * residual, axis=-1, keepdims=True)) + norm_epsilon)
    normed = low(residual * inverse_first * gains[0])
    projected = low_back(jnp.einsum('sd,cde->cse', normed, low(inbound), precision=highest))
    queries = low(rotate(projected[0].reshape(head_shape), cos_table, sin_table))
    key_rows = low(rotate(projected[1].reshape(head_shape), cos_table, sin_table))
    value_rows = low(projected[2].reshape(head_shape))
    block_rows = min(512, seq_len)
    blocks = seq_len // block_rows

    def one_block(inputs_pair):
        query_block, allowed_block = inputs_pair
        scores = low_back(jnp.einsum('qhd,khd->hqk', query_block, key_rows, precision=highest) * score_scale)
        scores = jnp.where(allowed_block[None], scores, -1e+30)
        largest = lax.optimization_barrier(jnp.max(scores, axis=-1, keepdims=True))
        weights = jnp.exp(scores - largest)
        shares = low(weights / lax.optimization_barrier(jnp.sum(weights, axis=-1, keepdims=True)))
        return jnp.einsum('hqk,khd->qhd', shares, value_rows, precision=highest)
    attended = lax.map(jax.checkpoint(one_block), (queries.reshape(blocks, block_rows, HEADS, HEAD_DIM), allowed.reshape(blocks, block_rows, seq_len)))
    attended = low(low_back(attended.reshape(seq_len, HEADS * HEAD_DIM)))
    middle = residual + low_back(jnp.dot(attended, low(outbound), precision=highest))
    inverse_second = lax.rsqrt(lax.optimization_barrier(jnp.mean(middle * middle, axis=-1, keepdims=True)) + norm_epsilon)
    second = low(middle * inverse_second * gains[1])
    gate_up = low_back(jnp.einsum('sd,cdf->csf', second, low(expand), precision=highest))
    hidden = low(gate_up[0] * lax.logistic(gate_up[0]) * gate_up[1])
    return middle + low_back(jnp.dot(hidden, low(shrink), precision=highest))

def gram_schmidt(factor):
    columns = []
    for column_index in range(factor.shape[-1]):
        column = factor[..., column_index]
        if column_index > 0:
            finished = jnp.stack(columns, axis=-1)
            coeffs = jnp.einsum('...mr,...m->...r', finished, column, precision=highest)
            column = column - jnp.einsum('...mr,...r->...m', finished, coeffs, precision=highest)
        length = lax.optimization_barrier(jnp.sum(column * column, axis=-1))
        columns.append(column * lax.rsqrt(length + factor_epsilon)[..., None])
    return jnp.stack(columns, axis=-1)

def reference(tokens, segment_ids, cotangent, norm_gains, gains_moment, inbound, outbound, expand, shrink, inbound_moment, outbound_moment, expand_moment, shrink_moment, inbound_error, outbound_error, expand_error, shrink_error, inbound_start, outbound_start, expand_start, shrink_start):
    replica_rows = tokens.reshape(N_DP, SEQ, D)
    replica_back = cotangent.reshape(N_DP, SEQ, D)
    replica_ids = segment_ids.reshape(N_DP, SEQ)

    def replica(inputs_all):
        rows_in, rows_back, segment_row, error_in, error_out, error_expand, error_shrink = inputs_all
        cos_table, sin_table = rope_tables(segment_row)
        allowed = allowed_pairs(segment_row)

        def forward(residual, gains, weight_in, weight_out, weight_expand, weight_shrink):
            return decoder_layer(residual, gains, weight_in, weight_out, weight_expand, weight_shrink, cos_table, sin_table, allowed)
        result, pullback = jax.vjp(forward, rows_in.astype(jnp.float32), norm_gains, inbound, outbound, expand, shrink)
        gradients = pullback(rows_back.astype(jnp.float32))
        return (result.astype(jnp.bfloat16), gradients[0].astype(jnp.bfloat16), gradients[1], gradients[2] + error_in, gradients[3] + error_out, gradients[4] + error_expand, gradients[5] + error_shrink)
    outputs_all = lax.map(replica, (replica_rows, replica_back, replica_ids, inbound_error, outbound_error, expand_error, shrink_error))
    layer_output = outputs_all[0].reshape(TOKENS, D)
    input_grad = outputs_all[1].reshape(TOKENS, D)
    gains_total = lax.optimization_barrier(jnp.sum(outputs_all[2], axis=0))
    inbound_sum = outputs_all[3]
    outbound_sum = outputs_all[4]
    expand_sum = outputs_all[5]
    shrink_sum = outputs_all[6]
    inbound_left = gram_schmidt(jnp.einsum('ncde,cer->cdr', inbound_sum, inbound_start, precision=highest))
    outbound_left = gram_schmidt(jnp.einsum('nde,er->dr', outbound_sum, outbound_start, precision=highest))
    expand_left = gram_schmidt(jnp.einsum('ncdf,cfr->cdr', expand_sum, expand_start, precision=highest))
    shrink_left = gram_schmidt(jnp.einsum('nfd,dr->fr', shrink_sum, shrink_start, precision=highest))
    inbound_right = jnp.einsum('ncde,cdr->cer', inbound_sum, inbound_left, precision=highest) / N_DP
    outbound_right = jnp.einsum('nde,dr->er', outbound_sum, outbound_left, precision=highest) / N_DP
    expand_right = jnp.einsum('ncdf,cdr->cfr', expand_sum, expand_left, precision=highest) / N_DP
    shrink_right = jnp.einsum('nfd,fr->dr', shrink_sum, shrink_left, precision=highest) / N_DP
    inbound_approx = jnp.einsum('cdr,cer->cde', inbound_left, inbound_right, precision=highest)
    outbound_approx = jnp.einsum('dr,er->de', outbound_left, outbound_right, precision=highest)
    expand_approx = jnp.einsum('cdr,cfr->cdf', expand_left, expand_right, precision=highest)
    shrink_approx = jnp.einsum('fr,dr->fd', shrink_left, shrink_right, precision=highest)
    inbound_residue = inbound_sum - inbound_approx[None]
    outbound_residue = outbound_sum - outbound_approx[None]
    expand_residue = expand_sum - expand_approx[None]
    shrink_residue = shrink_sum - shrink_approx[None]
    inbound_momentum = momentum_decay * inbound_moment + inbound_approx
    outbound_momentum = momentum_decay * outbound_moment + outbound_approx
    expand_momentum = momentum_decay * expand_moment + expand_approx
    shrink_momentum = momentum_decay * shrink_moment + shrink_approx
    gains_momentum = momentum_decay * gains_moment + gains_total
    return (layer_output, input_grad, gains_momentum, norm_gains - rate_gains * gains_momentum, inbound_momentum, outbound_momentum, expand_momentum, shrink_momentum, inbound - rate_inbound * inbound_momentum, outbound - rate_outbound * outbound_momentum, expand - rate_expand * expand_momentum, shrink - rate_shrink * shrink_momentum, inbound_residue, outbound_residue, expand_residue, shrink_residue, inbound_left, inbound_right, outbound_left, outbound_right, expand_left, expand_right, shrink_left, shrink_right)
```

```python
import functools

import jax
import jax.numpy as jnp
from jax import lax
from jax.experimental import pallas as pl
from jax.experimental.pallas import tpu as pltpu
from jax.sharding import Mesh
from jax.sharding import PartitionSpec as P

Y, X, Z, T = "dp_0", "dp_1", "dp_2", "tensor"
DP = (Y, X, Z)
DP_TENSOR = (Y, X, Z, T)
F32, BF = jnp.float32, jnp.bfloat16

SEQ = 1024
D = 768
HEAD_DIM = 64
HALF = 384
FF = 1536
RANK = 8
BLOCK = 256
SHARD = 12
CHUNK = 256
CHUNKS = FF // CHUNK
REL = (0, 3, 1, 2)
EPS = 1e-06
MASKED = -1e30

momentum_decay = 0.9
rate_inbound = 0.2
rate_outbound = 6.0
rate_expand = 0.3
rate_shrink = 0.25
rate_gains = 0.0005
rope_base = 10000.0

ANY = pl.BlockSpec(memory_space=pl.ANY)
SMEM = pl.BlockSpec(memory_space=pltpu.SMEM)


def nn(a, b):
    return jnp.dot(a, b, preferred_element_type=F32)


def nt(a, b):
    return lax.dot_general(a, b, (((1,), (1,)), ((), ())), preferred_element_type=F32)


def tn(a, b):
    return lax.dot_general(a, b, (((0,), (0,)), ((), ())), preferred_element_type=F32)


def params(mib=56):
    return pltpu.CompilerParams(vmem_limit_bytes=mib * 2**20)


def cost(flops, moved):
    return pl.CostEstimate(flops=flops, bytes_accessed=moved, transcendentals=0)


def full(shape):
    return pl.BlockSpec(shape, lambda *_: (0,) * len(shape))


def like(shape, dtype):
    return jax.ShapeDtypeStruct(shape, dtype)


def shift(v, axis, d):
    n = lax.axis_size(axis)
    return lax.ppermute(v, axis, [(i, (i + d) % n) for i in range(n)])


def swap(v):
    return lax.ppermute(v, T, [(0, 1), (1, 0)])


def sum_over_ring(v, axis):
    one, back, two = shift(v, axis, 1), shift(v, axis, 3), shift(v, axis, 2)
    return (v + two) + (one + back)


def sum_over_dp(v):
    for axis in (Z, X, Y):
        v = sum_over_ring(v, axis)
    return v


def rows_of_column(shard, z):
    own, one, two, back = shard, shift(shard, Z, 1), shift(shard, Z, 2), shift(shard, Z, 3)
    ring = jnp.stack([own, back, two, one, own, back, two, one])
    start = lax.rem(4 - z, 4)
    block = lax.dynamic_slice_in_dim(ring, start, 4, 0)
    return block.reshape(4 * SHARD, shard.shape[1])


def neighbours(v, axis):
    return shift(v, axis, 1), shift(v, axis, 3)


def opposite(ahead, behind, axis, cut):
    return shift(ahead[..., :cut], axis, 1), shift(behind[..., cut:], axis, 3)


def collect_first(v, axis, cut):
    one, back = neighbours(v, axis)
    left, right = opposite(one, back, axis, cut)
    return jnp.stack([v, one, back, jnp.concatenate([left, right], axis=-1)])


def place_pieces(pieces, widths, target, sems, place, inner_x):
    y0, x0 = place[0], place[1]
    copies = []
    spots = [(REL[0], 0), (REL[1], 0), (REL[2], 0)]
    at = 0
    for w in widths[3:]:
        spots.append((REL[3], at))
        at += w
    for s, (piece, w) in enumerate(zip(pieces, widths)):
        outer, col = spots[s]
        for i in range(4):
            if inner_x:
                yy, xx = lax.rem(y0 + outer, 4), lax.rem(x0 + REL[i], 4)
            else:
                yy, xx = lax.rem(y0 + REL[i], 4), lax.rem(x0 + outer, 4)
            row = pl.multiple_of(yy * 192 + xx * 48, 16)
            copies.append(
                pltpu.make_async_copy(
                    piece.at[i],
                    target.at[pl.ds(row, 48), pl.ds(col, w)],
                    sems.at[s * 4 + i],
                )
            )
    return copies


def turn_lanes(v, cos, low, high):
    n = v.shape[1]
    return v * cos + pltpu.roll(v, n - 32, 1) * low + pltpu.roll(v, 32, 1) * high


def project_kernel(place, x, gain, cos, low, high, *refs):
    pieces, (normed, q, k, v, weights, sems) = refs[:4], refs[4:]
    i = pl.program_id(0)

    @pl.when(i == 0)
    def _():
        copies = place_pieces(pieces, (1152,) * 4, weights, sems, place, True)
        for c in copies:
            c.start()
        for c in copies:
            c.wait()

    xb = x[...].astype(F32)
    inverse = lax.rsqrt(jnp.mean(xb * xb, axis=1, keepdims=True) + EPS)
    n = (xb * inverse * gain[...]).astype(BF)
    normed[...] = n
    c3 = jnp.concatenate([cos[...]] * 3, axis=1)
    l3 = jnp.concatenate([low[...]] * 3, axis=1)
    h3 = jnp.concatenate([high[...]] * 3, axis=1)
    pq = nn(n, weights[:, 0:384])
    q[...] = (turn_lanes(pq, c3, l3, h3).astype(BF).astype(F32) * 0.125).astype(BF)
    pk = nn(n, weights[:, 384:768])
    k[...] = turn_lanes(pk, c3, l3, h3).astype(BF)
    v[...] = nn(n, weights[:, 768:1152]).astype(BF)


def project(place, x, gain, tables, pieces):
    rows = lambda w: pl.BlockSpec((256, w), lambda i: (i, 0))
    return pl.pallas_call(
        project_kernel,
        grid=(4,),
        in_specs=[SMEM, rows(D), full((1, D)), rows(128), rows(128), rows(128)] + [ANY] * 4,
        out_specs=[rows(D), rows(HALF), rows(HALF), rows(HALF)],
        out_shape=[like((SEQ, D), BF)] + [like((SEQ, HALF), BF)] * 3,
        scratch_shapes=[pltpu.VMEM((D, 1152), BF), pltpu.SemaphoreType.DMA((16,))],
        compiler_params=params(),
        cost_estimate=cost(2 * SEQ * D * 1152, 8 * 2**20),
    )(place, x, gain, *tables, *pieces)


def head_lanes(rows, h):
    lane = lax.broadcasted_iota(jnp.int32, (rows, 128), 1)
    return (lane < 64) if h == 0 else (lane >= 64)


def three_terms(v):
    one = v.astype(BF).astype(F32)
    two = (v - one).astype(BF).astype(F32)
    return one, two, v - one - two


def attend_kernel(q, k, v, fq, fk, out, fq_out):
    keys = jnp.concatenate([k[...], fk[...]], axis=1)
    zero = jnp.zeros((), BF)
    lane = lax.broadcasted_iota(jnp.int32, (256, 128), 1)
    vals = [jnp.where(head_lanes(SEQ, h), v[...], zero) for h in range(2)]
    for b in range(4):
        rows = slice(b * 256, (b + 1) * 256)
        count = (b + 1) * 256
        total = None
        for h in range(2):
            qa = jnp.concatenate(
                [jnp.where(head_lanes(256, h), q[rows, :], zero), fq[rows, :]], axis=1
            )
            s = nt(qa, keys[:count])
            largest = jnp.max(s, axis=1, keepdims=True)
            e = jnp.exp(s - largest)
            sums = jnp.sum(e, axis=1, keepdims=True)
            o = nn(e.astype(BF), vals[h][:count]) * (1.0 / sums)
            total = o if total is None else total + o
            one, two, three = three_terms(-(largest + jnp.log(sums)))
            extra = jnp.where(lane == 3, one, jnp.where(lane == 4, two, three)).astype(BF)
            fq_out[h, rows, :] = jnp.where((lane >= 3) & (lane < 6), extra, fq[rows, :])
        out[rows, :] = total.astype(BF)


def attend(q, k, v, fq, fk):
    pair = pl.BlockSpec((SEQ, 128), lambda j: (0, j))
    return pl.pallas_call(
        attend_kernel,
        grid=(3,),
        in_specs=[pair, pair, pair, full((SEQ, 128)), full((SEQ, 128))],
        out_specs=[pair, pl.BlockSpec((2, SEQ, 128), lambda j: (j, 0, 0))],
        out_shape=[like((SEQ, HALF), BF), like((6, SEQ, 128), BF)],
        compiler_params=params(),
        cost_estimate=cost(8 * 10**9, 4 * 2**20),
    )(q, k, v, fq, fk)


def middle_kernel(place, x, att, att_other, gain, *refs):
    pieces, (middle, second, weights, sems) = refs[:4], refs[4:]
    i = pl.program_id(0)

    @pl.when(i == 0)
    def _():
        copies = place_pieces(pieces, (768,) * 4, weights, sems, place, False)
        for c in copies:
            c.start()
        for c in copies:
            c.wait()

    m = (
        x[...].astype(F32)
        + nt(att[...], weights[:, 0:384])
        + nt(att_other[...], weights[:, 384:768])
    )
    middle[...] = m
    inverse = lax.rsqrt(jnp.mean(m * m, axis=1, keepdims=True) + EPS)
    second[...] = (m * inverse * gain[...]).astype(BF)


def middle_rows(place, x, att, att_other, gain, pieces):
    rows = lambda w: pl.BlockSpec((256, w), lambda i: (i, 0))
    return pl.pallas_call(
        middle_kernel,
        grid=(4,),
        in_specs=[SMEM, rows(D), rows(HALF), rows(HALF), full((1, D))] + [ANY] * 4,
        out_specs=[rows(D), rows(D)],
        out_shape=[like((SEQ, D), F32), like((SEQ, D), BF)],
        scratch_shapes=[pltpu.VMEM((D, 768), BF), pltpu.SemaphoreType.DMA((16,))],
        compiler_params=params(),
        cost_estimate=cost(2 * SEQ * D * D, 8 * 2**20),
    )(place, x, att, att_other, gain, *pieces)


def two_terms(v):
    one = v.astype(BF).astype(F32)
    return jnp.concatenate([one, v - one], axis=0).astype(BF)


def folded(v):
    return v[0:8] + v[8:16]


def feed_kernel(place, second, cot, middle, err_e, err_s, start_e, start_s, *refs):
    pieces_a, pieces_b = refs[0:5], refs[5:10]
    (sum_e, sum_s, left_e, left_s, grad_out, own_out, send_out) = refs[10:17]
    (weights, sems, turned, hid, dgate, dup, grad_acc, out_acc) = refs[17:]
    j = pl.program_id(0)
    wide = (2304, 2304, 2304, 1152, 1152)
    copies_a = place_pieces(pieces_a, wide, weights.at[0], sems.at[0], place, True)
    copies_b = place_pieces(pieces_b, wide, weights.at[1], sems.at[1], place, False)

    @pl.when(j == 0)
    def _():
        for c in copies_a + copies_b:
            c.start()
        turned[...] = second[...].T
        grad_acc[...] = jnp.zeros_like(grad_acc)
        out_acc[...] = jnp.zeros_like(out_acc)
        left_e[...] = jnp.zeros_like(left_e)
        for c in copies_a:
            c.wait()

    @pl.when(j == CHUNKS // 2)
    def _():
        for c in copies_b:
            c.wait()

    half = j // (CHUNKS // 2)
    at = pl.multiple_of(lax.rem(j, CHUNKS // 2) * CHUNK, CHUNK)
    wg = weights[half, :, pl.ds(at, CHUNK)]
    wu = weights[half, :, pl.ds(pl.multiple_of(768 + at, CHUNK), CHUNK)]
    ws = weights[half, :, pl.ds(pl.multiple_of(1536 + at, CHUNK), CHUNK)]
    for b in range(4):
        rows = slice(b * 256, (b + 1) * 256)
        n, c = second[rows, :], cot[rows, :]
        g, u, hg = nn(n, wg), nn(n, wu), nn(c, ws)
        sig = 0.5 * jnp.tanh(0.5 * g) + 0.5
        act = g * sig
        hb = (act * u).astype(BF)
        dg = (hg * u * (sig + act * (1.0 - sig))).astype(BF)
        du = (hg * act).astype(BF)
        hid[rows, :] = hb
        dgate[rows, :] = dg
        dup[rows, :] = du
        out_acc[rows, :] += nt(hb, ws)
        grad_acc[rows, :] += nt(dg, wg) + nt(du, wu)
    starts = two_terms(start_s[...])
    ss = tn(hid[...], cot[...]) + err_s[0]
    low = ss.astype(BF)
    sum_s[...] = low
    left_s[...] = folded(nt(starts, low))
    for c, grads in enumerate((dgate, dup)):
        se = nn(turned[...], grads[...]) + err_e[0, c]
        low = se.astype(BF)
        sum_e[c] = low
        left_e[c] += folded(nt(two_terms(start_e[c]), low))

    @pl.when(j == CHUNKS - 1)
    def _():
        t = place[3]
        grad_out[...] = grad_acc[...].astype(BF)
        mine = pl.ds(pl.multiple_of(t * 512, 512), 512)
        other = pl.ds(pl.multiple_of((1 - t) * 512, 512), 512)
        own_out[...] = out_acc[mine, :] + middle[mine, :]
        send_out[...] = out_acc[other, :].astype(BF)


def feed(place, second, cot, middle, err_e, err_s, start_e, start_s, pieces_a, pieces_b):
    return pl.pallas_call(
        feed_kernel,
        grid=(CHUNKS,),
        in_specs=[
            SMEM,
            full((SEQ, D)),
            full((SEQ, D)),
            full((SEQ, D)),
            pl.BlockSpec((1, 2, D, CHUNK), lambda j: (0, 0, 0, j)),
            pl.BlockSpec((1, CHUNK, D), lambda j: (0, j, 0)),
            pl.BlockSpec((2, RANK, CHUNK), lambda j: (0, 0, j)),
            full((RANK, D)),
        ]
        + [ANY] * 10,
        out_specs=[
            pl.BlockSpec((2, D, CHUNK), lambda j: (0, 0, j)),
            pl.BlockSpec((CHUNK, D), lambda j: (j, 0)),
            full((2, RANK, D)),
            pl.BlockSpec((RANK, CHUNK), lambda j: (0, j)),
            full((SEQ, D)),
            full((512, D)),
            full((512, D)),
        ],
        out_shape=[
            like((2, D, FF), BF),
            like((FF, D), BF),
            like((2, RANK, D), F32),
            like((RANK, FF), F32),
            like((SEQ, D), BF),
            like((512, D), F32),
            like((512, D), BF),
        ],
        scratch_shapes=[
            pltpu.VMEM((2, D, 2304), BF),
            pltpu.SemaphoreType.DMA((2, 20)),
            pltpu.VMEM((D, SEQ), BF),
            pltpu.VMEM((SEQ, CHUNK), BF),
            pltpu.VMEM((SEQ, CHUNK), BF),
            pltpu.VMEM((SEQ, CHUNK), BF),
            pltpu.VMEM((SEQ, D), F32),
            pltpu.VMEM((SEQ, D), F32),
        ],
        compiler_params=params(60),
        cost_estimate=cost(18 * SEQ * D * FF, 40 * 2**20),
    )(place, second, cot, middle, err_e, err_s, start_e, start_s, *pieces_a, *pieces_b)


def by_eight(v):
    return jnp.sum(v.reshape(-1, 8, v.shape[1]), axis=0)


def branch_kernel(place, cot, grad, grad_other, middle, gain, att, err, start, *refs):
    pieces = refs[:4]
    middle_grad, att_grad, gain_sum, sums, left, weights, sems, acc = refs[4:]
    i = pl.program_id(0)

    @pl.when(i == 0)
    def _():
        copies = place_pieces(pieces, (768,) * 4, weights, sems, place, False)
        for c in copies:
            c.start()
        acc[...] = jnp.zeros_like(acc)
        gain_sum[...] = jnp.zeros_like(gain_sum)
        for c in copies:
            c.wait()

    m = middle[...]
    inverse = lax.rsqrt(jnp.mean(m * m, axis=1, keepdims=True) + EPS)
    unit = m * inverse
    w = grad[...].astype(F32) + grad_other[...].astype(F32)
    a = w * gain[...]
    mg = cot[...].astype(F32) + inverse * (a - unit * jnp.mean(a * unit, axis=1, keepdims=True))
    branch = mg.astype(BF)
    att_grad[...] = nn(branch, weights[:, 0:384]).astype(BF)
    acc[...] += tn(att[...], branch)

    @pl.when(i // 2 == place[3])
    def _():
        middle_grad[...] = mg
        gain_sum[...] += by_eight(w * unit)

    @pl.when(i == 3)
    def _():
        low = (acc[...] + err[0]).astype(BF)
        sums[...] = low
        left[...] = folded(nt(two_terms(start[...]), low))


def branch_rows(place, cot, grad, grad_other, middle, gain, att, err, start, pieces):
    rows = lambda w: pl.BlockSpec((256, w), lambda i, p: (i, 0))
    fixed = lambda shape: pl.BlockSpec(shape, lambda i, p: (0,) * len(shape))
    own = pl.BlockSpec((256, D), lambda i, p: (jnp.clip(i - 2 * p[3], 0, 1), 0))
    return pl.pallas_call(
        branch_kernel,
        grid_spec=pltpu.PrefetchScalarGridSpec(
            num_scalar_prefetch=1,
            grid=(4,),
            in_specs=[
                rows(D),
                rows(D),
                rows(D),
                rows(D),
                fixed((1, D)),
                rows(HALF),
                fixed((1, HALF, D)),
                fixed((RANK, D)),
            ]
            + [ANY] * 4,
            out_specs=[
                own,
                rows(HALF),
                fixed((8, D)),
                fixed((HALF, D)),
                fixed((RANK, HALF)),
            ],
            scratch_shapes=[
                pltpu.VMEM((D, 768), BF),
                pltpu.SemaphoreType.DMA((16,)),
                pltpu.VMEM((HALF, D), F32),
            ],
        ),
        out_shape=[
            like((512, D), F32),
            like((SEQ, HALF), BF),
            like((8, D), F32),
            like((HALF, D), BF),
            like((RANK, HALF), F32),
        ],
        compiler_params=params(),
        cost_estimate=cost(4 * SEQ * D * HALF, 14 * 2**20),
    )(place, cot, grad, grad_other, middle, gain, att, err, start, *pieces)


def attend_back_kernel(q, k, v, att, grad, fq, fk, cos, low, high, out, kt, dk_acc, dv_acc):
    zero = jnp.zeros((), BF)
    lane = lax.broadcasted_iota(jnp.int32, (256, 128), 1)
    ones = jnp.where(lax.broadcasted_iota(jnp.int32, (SEQ, 128), 1) < 3, 1.0, 0.0).astype(BF)
    keys = jnp.concatenate([k[...], fk[...]], axis=1)
    vals = jnp.concatenate([v[...], ones], axis=1)
    for h in range(2):
        kt[h] = jnp.where(head_lanes(SEQ, h), k[...], zero).T
    dk_acc[...] = jnp.zeros_like(dk_acc)
    dv_acc[...] = jnp.zeros_like(dv_acc)
    for b in range(4):
        rows = slice(b * 256, (b + 1) * 256)
        count = (b + 1) * 256
        dq = None
        for h in range(2):
            mine = head_lanes(256, h)
            qm = jnp.where(mine, q[rows, :], zero)
            gm = jnp.where(mine, grad[rows, :], zero)
            centre = jnp.sum(gm.astype(F32) * att[rows, :].astype(F32), axis=1, keepdims=True)
            one, two, three = three_terms(-centre)
            extra = jnp.where(lane == 0, one, jnp.where(lane == 1, two, three))
            fg = jnp.where(lane < 3, extra, 0.0).astype(BF)
            soft = jnp.exp(nt(keys[:count], jnp.concatenate([qm, fq[h, rows, :]], axis=1)))
            shares = soft.astype(BF)
            ds = (soft * nt(vals[:count], jnp.concatenate([gm, fg], axis=1))).astype(BF)
            dv_acc[:count, :] += nn(shares, gm)
            dk_acc[:count, :] += nn(ds, qm)
            part = nn(kt[h, :, :count], ds)
            dq = part if dq is None else dq + part
        turned = dq.T * 0.125
        out[0, rows, :] = turn_lanes(turned, cos[rows, :], -low[rows, :], -high[rows, :]).astype(BF)
    out[1] = turn_lanes(dk_acc[...], cos[...], -low[...], -high[...]).astype(BF)
    out[2] = dv_acc[...].astype(BF)


def attend_back(q, k, v, att, grad, fq, fk, tables):
    pair = pl.BlockSpec((SEQ, 128), lambda j: (0, j))
    return pl.pallas_call(
        attend_back_kernel,
        grid=(3,),
        in_specs=[pair] * 5
        + [pl.BlockSpec((2, SEQ, 128), lambda j: (j, 0, 0))]
        + [full((SEQ, 128))] * 4,
        out_specs=pl.BlockSpec((3, SEQ, 128), lambda j: (0, 0, j)),
        out_shape=like((3, SEQ, HALF), BF),
        scratch_shapes=[
            pltpu.VMEM((2, 128, SEQ), BF),
            pltpu.VMEM((SEQ, 128), F32),
            pltpu.VMEM((SEQ, 128), F32),
        ],
        compiler_params=params(),
        cost_estimate=cost(16 * 10**9, 8 * 2**20),
    )(q, k, v, att, grad, fq, fk, *tables)


def keep_and_send(v, t):
    first, rest = v[:, :HALF], v[:, HALF:]
    return jnp.where(t == 0, first, rest), jnp.where(t == 0, rest, first)


def inbound_kernel(place, normed, dproj, err, start, sums, keep, send, turned):
    c = pl.program_id(0)

    @pl.when(c == 0)
    def _():
        turned[...] = normed[...].T

    low = (nn(turned[...], dproj[0]) + err[0, 0]).astype(BF)
    sums[0] = low
    keep[...], send[...] = keep_and_send(folded(nt(two_terms(start[0]), low)), place[3])


def inbound_sums(place, normed, dproj, err, start):
    lanes = pl.BlockSpec((RANK, HALF), lambda c: (0, c))
    return pl.pallas_call(
        inbound_kernel,
        grid=(3,),
        in_specs=[
            SMEM,
            full((SEQ, D)),
            pl.BlockSpec((1, SEQ, HALF), lambda c: (c, 0, 0)),
            pl.BlockSpec((1, 1, D, HALF), lambda c: (0, c, 0, 0)),
            pl.BlockSpec((1, RANK, HALF), lambda c: (c, 0, 0)),
        ],
        out_specs=[pl.BlockSpec((1, D, HALF), lambda c: (c, 0, 0)), lanes, lanes],
        out_shape=[
            like((3, D, HALF), BF),
            like((RANK, 3 * HALF), F32),
            like((RANK, 3 * HALF), F32),
        ],
        scratch_shapes=[pltpu.VMEM((D, SEQ), BF)],
        compiler_params=params(),
        cost_estimate=cost(2 * SEQ * D * 1152, 12 * 2**20),
    )(place, normed, dproj, err, start)


def first_grad_kernel(place, dproj, *refs):
    pieces, (own, send, weights, sems, acc) = refs[:4], refs[4:]
    c = pl.program_id(0)

    @pl.when(c == 0)
    def _():
        copies = place_pieces(pieces, (1152,) * 4, weights, sems, place, True)
        for x in copies:
            x.start()
        acc[...] = jnp.zeros_like(acc)
        for x in copies:
            x.wait()

    at = pl.multiple_of(c * HALF, HALF)
    acc[...] += nt(dproj[0], weights[:, pl.ds(at, HALF)])

    @pl.when(c == 2)
    def _():
        t = place[3]
        own[...] = acc[pl.ds(pl.multiple_of(t * 512, 512), 512), :]
        send[...] = acc[pl.ds(pl.multiple_of((1 - t) * 512, 512), 512), :].astype(BF)


def first_grad_rows(place, dproj, pieces):
    return pl.pallas_call(
        first_grad_kernel,
        grid=(3,),
        in_specs=[SMEM, pl.BlockSpec((1, SEQ, HALF), lambda c: (c, 0, 0))] + [ANY] * 4,
        out_specs=[full((512, D)), full((512, D))],
        out_shape=[like((512, D), F32), like((512, D), BF)],
        scratch_shapes=[
            pltpu.VMEM((D, 1152), BF),
            pltpu.SemaphoreType.DMA((16,)),
            pltpu.VMEM((SEQ, D), F32),
        ],
        compiler_params=params(),
        cost_estimate=cost(2 * SEQ * D * 1152, 8 * 2**20),
    )(place, dproj, *pieces)


def input_grad_kernel(place, x, gain, middle_grad, own, other, gain_second, out, keep, send):
    xb = x[...].astype(F32)
    inverse = lax.rsqrt(jnp.mean(xb * xb, axis=1, keepdims=True) + EPS)
    unit = xb * inverse
    w = own[...] + other[...].astype(F32)
    a = w * gain[...]
    back = inverse * (a - unit * jnp.mean(a * unit, axis=1, keepdims=True))
    out[...] = (middle_grad[...] + back).astype(BF)
    t = place[3]
    keep_one, send_one = keep_and_send(by_eight(w * unit), t)
    keep_two, send_two = keep_and_send(gain_second[...], t)
    keep[...] = jnp.concatenate([keep_one, keep_two], axis=1)
    send[...] = jnp.concatenate([send_one, send_two], axis=1)


def input_grad_rows(place, x, gain, middle_grad, own, other, gain_second):
    shapes = [(512, D), (1, D), (512, D), (512, D), (512, D), (8, D)]
    return pl.pallas_call(
        input_grad_kernel,
        in_specs=[SMEM] + [full(s) for s in shapes],
        out_specs=[full((512, D)), full((8, D)), full((8, D))],
        out_shape=[like((512, D), BF), like((8, D), F32), like((8, D), F32)],
        compiler_params=params(),
        cost_estimate=cost(10**7, 6 * 2**20),
    )(place, x, gain, middle_grad, own, other, gain_second)


def orthonormal(factors):
    done = [jnp.zeros_like(f) for f in factors]
    for k in range(RANK):
        for m, f in enumerate(factors):
            row = f[k : k + 1]
            if k > 0:
                coeffs = jnp.sum(done[m] * row, axis=1, keepdims=True)
                row = row - jnp.sum(coeffs * done[m], axis=0, keepdims=True)
            length = jnp.sum(row * row, axis=1, keepdims=True)
            row = row * lax.rsqrt(length + EPS)
            here = lax.broadcasted_iota(jnp.int32, f.shape, 0) == k
            done[m] = jnp.where(here, row, done[m])
    return done


def joined(mine, other, t):
    return jnp.concatenate(
        [jnp.where(t == 0, mine, other), jnp.where(t == 0, other, mine)], axis=1
    )


def feed_left_kernel(place, mine, other, left_e, left_s, own_s):
    t = place[3]
    a, b = mine[...], other[...]
    e0 = jnp.where(t == 0, a[:, :D], b[:, :D])
    e1 = jnp.where(t == 0, b[:, :D], a[:, :D])
    s = joined(a[:, D:], b[:, D:], t)
    e0, e1, s = orthonormal([e0, e1, s])
    left_e[0] = e0
    left_e[1] = e1
    left_s[...] = s
    own_s[...] = jnp.where(t == 0, s[:, :FF], s[:, FF:])


def feed_left(place, mine, other):
    n = D + FF
    return pl.pallas_call(
        feed_left_kernel,
        in_specs=[SMEM, full((RANK, n)), full((RANK, n))],
        out_specs=[full((2, RANK, D)), full((RANK, 2 * FF)), full((RANK, FF))],
        out_shape=[like((2, RANK, D), F32), like((RANK, 2 * FF), F32), like((RANK, FF), F32)],
        compiler_params=params(),
        cost_estimate=cost(10**7, 2**18),
    )(place, mine, other)


def feed_right_kernel(place, left_e, left_s, sum_e, sum_s, right_e, keep, send, acc):
    j = pl.program_id(0)
    for c in range(2):
        right_e[:, c, :] = folded(nn(two_terms(left_e[c]), sum_e[c]))
    part = folded(nn(two_terms(left_s[...]), sum_s[...]))

    @pl.when(j == 0)
    def _():
        acc[...] = part

    @pl.when(j > 0)
    def _():
        acc[...] += part

    @pl.when(j == CHUNKS // 2 - 1)
    def _():
        keep[...], send[...] = keep_and_send(acc[...], place[3])


def feed_right(place, left_e, own_s, sum_e, sum_s):
    wide = 2 * CHUNK
    return pl.pallas_call(
        feed_right_kernel,
        grid=(CHUNKS // 2,),
        in_specs=[
            SMEM,
            full((2, RANK, D)),
            pl.BlockSpec((RANK, wide), lambda j: (0, j)),
            pl.BlockSpec((2, D, wide), lambda j: (0, 0, j)),
            pl.BlockSpec((wide, D), lambda j: (j, 0)),
        ],
        out_specs=[
            pl.BlockSpec((RANK, 2, wide), lambda j: (0, 0, j)),
            full((RANK, HALF)),
            full((RANK, HALF)),
        ],
        out_shape=[like((RANK, 2, FF), F32), like((RANK, HALF), F32), like((RANK, HALF), F32)],
        scratch_shapes=[pltpu.VMEM((RANK, D), F32)],
        compiler_params=params(),
        cost_estimate=cost(10**8, 10 * 2**20),
    )(place, left_e, own_s, sum_e, sum_s)


def left_terms(v):
    one = v.astype(BF).astype(F32)
    two = v - one
    return jnp.concatenate([one, one, two, two], axis=0).astype(BF)


def right_terms(v):
    one = v.astype(BF).astype(F32)
    two = v - one
    return jnp.concatenate([one, two, one, two], axis=0).astype(BF)


def own_rows(terms, place):
    dp = (place[0] * 4 + place[1]) * 4 + place[2]
    row = lax.broadcasted_iota(jnp.int32, (16, D), 0)
    col = lax.broadcasted_iota(jnp.int32, (16, D), 1)
    pick = jnp.where((row < SHARD) & (col == row + SHARD * dp), 1.0, 0.0).astype(BF)
    return nt(pick, terms).astype(BF)


def feed_last_kernel(place, left_e, own_s, right_e, right_s, sum_e, sum_s, res_e, res_s, own_e, own_sh):
    scale = 1.0 / 64
    for c in range(2):
        lt, rt = left_terms(left_e[c]), right_terms(right_e[:, c, :] * scale)
        res_e[0, c] = sum_e[c].astype(F32) - tn(lt, rt)
        own_e[c] = nn(own_rows(lt, place), rt)[:SHARD]
    lt, rt = left_terms(own_s[...]), right_terms(right_s[...] * scale)
    res_s[0] = sum_s[...].astype(F32) - tn(lt, rt)
    own_sh[...] = nn(own_rows(rt, place), lt)[:SHARD]


def feed_last(place, left_e, own_s, right_e, right_s, sum_e, sum_s):
    return pl.pallas_call(
        feed_last_kernel,
        grid=(CHUNKS,),
        in_specs=[
            SMEM,
            full((2, RANK, D)),
            pl.BlockSpec((RANK, CHUNK), lambda j: (0, j)),
            pl.BlockSpec((RANK, 2, CHUNK), lambda j: (0, 0, j)),
            full((RANK, D)),
            pl.BlockSpec((2, D, CHUNK), lambda j: (0, 0, j)),
            pl.BlockSpec((CHUNK, D), lambda j: (j, 0)),
        ],
        out_specs=[
            pl.BlockSpec((1, 2, D, CHUNK), lambda j: (0, 0, 0, j)),
            pl.BlockSpec((1, CHUNK, D), lambda j: (0, j, 0)),
            pl.BlockSpec((2, SHARD, CHUNK), lambda j: (0, 0, j)),
            pl.BlockSpec((SHARD, CHUNK), lambda j: (0, j)),
        ],
        out_shape=[
            like((1, 2, D, FF), F32),
            like((1, FF, D), F32),
            like((2, SHARD, FF), F32),
            like((SHARD, FF), F32),
        ],
        compiler_params=params(),
        cost_estimate=cost(10**8, 30 * 2**20),
    )(place, left_e, own_s, right_e, right_s, sum_e, sum_s)


def attn_left_kernel(place, mine, other, sum_i, sum_o, left_i, own_o, right_i, keep, send):
    t = place[3]
    a, b = mine[...], other[...]
    cut = lambda v, c: v[:, c * HALF : (c + 1) * HALF]
    found = orthonormal([joined(cut(a, c), cut(b, c), t) for c in range(4)])
    for c in range(3):
        left_i[c] = found[c]
        right_i[:, c * HALF : (c + 1) * HALF] = folded(nn(two_terms(found[c]), sum_i[c]))
    mine_o, _ = keep_and_send(found[3], t)
    own_o[...] = mine_o
    keep[...], send[...] = keep_and_send(folded(nn(two_terms(mine_o), sum_o[...])), t)


def attn_left(place, mine, other, sum_i, sum_o):
    return pl.pallas_call(
        attn_left_kernel,
        in_specs=[
            SMEM,
            full((RANK, 4 * HALF)),
            full((RANK, 4 * HALF)),
            full((3, D, HALF)),
            full((HALF, D)),
        ],
        out_specs=[
            full((3, RANK, D)),
            full((RANK, HALF)),
            full((RANK, 3 * HALF)),
            full((RANK, HALF)),
            full((RANK, HALF)),
        ],
        out_shape=[
            like((3, RANK, D), F32),
            like((RANK, HALF), F32),
            like((RANK, 3 * HALF), F32),
            like((RANK, HALF), F32),
            like((RANK, HALF), F32),
        ],
        compiler_params=params(),
        cost_estimate=cost(10**8, 3 * 2**20),
    )(place, mine, other, sum_i, sum_o)


def attn_last_kernel(place, left_i, own_o, right_i, right_o, sum_i, sum_o, res_i, res_o, own_i, own_ot):
    scale = 1.0 / 64
    for c in range(3):
        lt = left_terms(left_i[c])
        rt = right_terms(right_i[:, c * HALF : (c + 1) * HALF] * scale)
        res_i[0, c] = sum_i[c].astype(F32) - tn(lt, rt)
        own_i[c] = nn(own_rows(lt, place), rt)[:SHARD]
    lt, rt = left_terms(own_o[...]), right_terms(right_o[...] * scale)
    res_o[0] = sum_o[...].astype(F32) - tn(lt, rt)
    own_ot[...] = nn(own_rows(rt, place), lt)[:SHARD]


def attn_last(place, left_i, own_o, right_i, right_o, sum_i, sum_o):
    shapes = [(3, RANK, D), (RANK, HALF), (RANK, 3 * HALF), (RANK, D), (3, D, HALF), (HALF, D)]
    outs = [(1, 3, D, HALF), (1, HALF, D), (3, SHARD, HALF), (SHARD, HALF)]
    return pl.pallas_call(
        attn_last_kernel,
        in_specs=[SMEM] + [full(s) for s in shapes],
        out_specs=[full(s) for s in outs],
        out_shape=[like(s, F32) for s in outs],
        compiler_params=params(),
        cost_estimate=cost(10**8, 8 * 2**20),
    )(place, left_i, own_o, right_i, right_o, sum_i, sum_o)


def lane_tables(ids):
    zeros = jnp.sum((ids == 0).astype(jnp.int32))
    ones = jnp.sum((ids == 1).astype(jnp.int32))
    before = jnp.where(ids == 0, 0, jnp.where(ids == 1, zeros, zeros + ones))
    places = (jnp.arange(SEQ, dtype=jnp.int32) - before).astype(F32)
    lane = jnp.arange(128, dtype=jnp.int32)
    inverse = rope_base ** (-((lane % 32).astype(F32) * 2.0) / HEAD_DIM)
    angles = places[:, None] * inverse[None, :]
    first = (lane % 64 < 32)[None, :]
    sine = jnp.sin(angles)
    low, high = jnp.where(first, -sine, 0.0), jnp.where(first, 0.0, sine)
    kind = lane[None, :]
    same = ids[:, None] == kind
    fq = jnp.where((kind < 3) & same, 1.0, 0.0).astype(BF)
    fk = jnp.where(kind < 3, jnp.where(same, 0.0, MASKED), jnp.where(kind < 6, 1.0, 0.0))
    return (jnp.cos(angles), low, high), fq, fk.astype(BF)


def both_halves(own, t):
    other = swap(own)
    whole = jnp.zeros((SEQ, D), BF)
    whole = lax.dynamic_update_slice_in_dim(whole, own, t * 512, 0)
    return lax.dynamic_update_slice_in_dim(whole, other, (1 - t) * 512, 0)


def local(
    tokens,
    segment_ids,
    cotangent,
    norm_gains,
    gains_moment,
    inbound,
    outbound,
    expand,
    shrink,
    inbound_moment,
    outbound_moment,
    expand_moment,
    shrink_moment,
    inbound_error,
    outbound_error,
    expand_error,
    shrink_error,
    inbound_start,
    outbound_start,
    expand_start,
    shrink_start,
):
    y, x, z, t = (lax.axis_index(a) for a in DP_TENSOR)
    place = jnp.stack([y, x, z, t]).astype(jnp.int32)

    out_own = outbound.T.astype(BF)
    out_other = swap(out_own)
    parts = [inbound[c] for c in range(3)]
    gate, up, down = expand[0], expand[1], shrink.T
    first_half = [w[:, : FF // 2] for w in (gate, up, down)]
    second_half = [w[:, FF // 2 :] for w in (gate, up, down)]
    low = lambda ws: [w.astype(BF) for w in ws]
    shard = jnp.concatenate(
        low(parts) + low(first_half) + [out_own, out_other] + low(second_half), axis=1
    )
    column = rows_of_column(shard, z)
    side_a, side_b = column[:, :3456], column[:, 3456:]
    side_a = collect_first(side_a, X, 1792)
    side_b = collect_first(side_b, Y, 1536)
    in_own, feed_a = side_a[..., :1152], side_a[..., 1152:]
    outb_own, feed_b = side_b[..., :768], side_b[..., 768:]
    in_pieces = [in_own, *neighbours(in_own, Y), shift(in_own, Y, 2)]
    out_pieces = [outb_own, *neighbours(outb_own, X), shift(outb_own, X, 2)]
    near_a, near_b = neighbours(feed_a, Y), neighbours(feed_b, X)
    pieces_a = [feed_a, *near_a, *opposite(*near_a, Y, 1152)]
    pieces_b = [feed_b, *near_b, *opposite(*near_b, X, 1152)]

    x_all, cot_all = both_halves(tokens, t), both_halves(cotangent, t)
    tables, fq, fk = lane_tables(segment_ids)
    gain_one, gain_two = norm_gains[0:1], norm_gains[1:2]
    normed, q, k, v = project(place, x_all, gain_one, tables, in_pieces)
    att, fq_all = attend(q, k, v, fq, fk)
    middle, second = middle_rows(place, x_all, att, swap(att), gain_two, out_pieces)

    start_e, start_s = jnp.swapaxes(expand_start, 1, 2), shrink_start.T
    sum_e, sum_s, left_e, left_s, grad, own_out, send_out = feed(
        place, second, cot_all, middle, expand_error, shrink_error, start_e, start_s, pieces_a, pieces_b
    )
    layer_output = (own_out + swap(send_out).astype(F32)).astype(BF)
    grad_other = swap(grad)
    middle_grad, att_grad, gain_second, sum_o, left_o = branch_rows(
        place, cot_all, grad, grad_other, middle, gain_two, att, outbound_error, outbound_start.T, out_pieces
    )

    keep_e = jnp.where(t == 0, left_e[0], left_e[1])
    send_e = jnp.where(t == 0, left_e[1], left_e[0])
    mine = sum_over_dp(jnp.concatenate([keep_e + swap(send_e), left_s], axis=1))
    left_e, left_s, own_s = feed_left(place, mine, swap(mine))

    dproj = attend_back(q, k, v, att, att_grad, fq_all, fk, tables)
    sum_i, keep_i, send_i = inbound_sums(
        place, normed, dproj, inbound_error, jnp.swapaxes(inbound_start, 1, 2)
    )
    mine = sum_over_dp(jnp.concatenate([keep_i + swap(send_i), left_o], axis=1))

    right_e, keep_s, send_s = feed_right(place, left_e, own_s, sum_e, sum_s)
    feed_sums = sum_over_dp(
        jnp.concatenate([right_e.reshape(RANK, 2 * FF), keep_s + swap(send_s)], axis=1)
    )

    first_own, first_send = first_grad_rows(place, dproj, in_pieces)
    input_grad, keep_g, send_g = input_grad_rows(
        place, tokens, gain_one, middle_grad, first_own, swap(first_send), gain_second
    )

    left_i, own_o, right_i, keep_o, send_o = attn_left(place, mine, swap(mine), sum_i, sum_o)
    mine = sum_over_dp(
        jnp.concatenate(
            [right_i, keep_o + swap(send_o), keep_g + swap(send_g)], axis=1
        )
    )

    def whole(half, other):
        return jnp.where(
            t == 0,
            jnp.concatenate([half, other], axis=1),
            jnp.concatenate([other, half], axis=1),
        )

    tail = feed_sums[:, 2 * FF :]
    right_e = feed_sums[:, : 2 * FF].reshape(RANK, 2, FF)
    right_s = whole(tail, swap(tail))
    res_e, res_s, own_e, own_sh = feed_last(place, left_e, own_s, right_e, right_s, sum_e, sum_s)

    tail = mine[:, 3 * HALF :]
    other = swap(tail)
    right_i = mine[:, : 3 * HALF]
    right_o = whole(tail[:, :HALF], other[:, :HALF])
    gains = jnp.stack(
        [
            jnp.sum(whole(tail[:, (1 + g) * HALF : (2 + g) * HALF], other[:, (1 + g) * HALF : (2 + g) * HALF]), axis=0)
            for g in range(2)
        ]
    )
    res_i, res_o, own_i, own_ot = attn_last(place, left_i, own_o, right_i, right_o, sum_i, sum_o)

    inbound_momentum = momentum_decay * inbound_moment + own_i
    outbound_momentum = momentum_decay * outbound_moment + own_ot.T
    expand_momentum = momentum_decay * expand_moment + own_e
    shrink_momentum = momentum_decay * shrink_moment + own_sh.T
    gains_momentum = momentum_decay * gains_moment + gains
    return (
        layer_output,
        input_grad,
        gains_momentum,
        norm_gains - rate_gains * gains_momentum,
        inbound_momentum,
        outbound_momentum,
        expand_momentum,
        shrink_momentum,
        inbound - rate_inbound * inbound_momentum,
        outbound - rate_outbound * outbound_momentum,
        expand - rate_expand * expand_momentum,
        shrink - rate_shrink * shrink_momentum,
        res_i,
        res_o,
        res_e,
        res_s,
        jnp.swapaxes(left_i, 1, 2),
        jnp.swapaxes(right_i.reshape(RANK, 3, HALF), 0, 1).swapaxes(1, 2) / 64,
        own_o.T,
        right_o.T / 64,
        jnp.swapaxes(left_e, 1, 2),
        jnp.transpose(right_e, (1, 2, 0)) / 64,
        own_s.T,
        right_s.T / 64,
    )


def solution(mesh):
    torus = Mesh(mesh.devices.reshape(4, 4, 4, mesh.shape["tensor"]), DP_TENSOR)
    return jax.shard_map(
        local,
        mesh=torus,
        in_specs=(
            P(DP_TENSOR, None),
            P(DP),
            P(DP_TENSOR, None),
            P(),
            P(),
            P(None, DP, T),
            P(T, DP),
            P(None, DP, T),
            P(T, DP),
            P(None, DP, T),
            P(T, DP),
            P(None, DP, T),
            P(T, DP),
            P(DP, None, None, T),
            P(DP, T, None),
            P(DP, None, None, T),
            P(DP, T, None),
            P(None, T, None),
            P(),
            P(None, T, None),
            P(),
        ),
        out_specs=(
            P(DP_TENSOR, None),
            P(DP_TENSOR, None),
            P(),
            P(),
            P(None, DP, T),
            P(T, DP),
            P(None, DP, T),
            P(T, DP),
            P(None, DP, T),
            P(T, DP),
            P(None, DP, T),
            P(T, DP),
            P(DP, None, None, T),
            P(DP, T, None),
            P(DP, None, None, T),
            P(DP, T, None),
            P(),
            P(None, T, None),
            P(T, None),
            P(),
            P(),
            P(None, T, None),
            P(T, None),
            P(),
        ),
        check_vma=False,
    )
```

```python
import jax
import jax.numpy as jnp
from jax import lax
from jax.experimental import pallas as pl
from jax.experimental.pallas import tpu as pltpu
from jax.sharding import Mesh
from jax.sharding import PartitionSpec as P

Y, X, Z, T = "dp_0", "dp_1", "dp_2", "tensor"
DP = (Y, X, Z)
DP_TENSOR = (Y, X, Z, T)
F32, BF = jnp.float32, jnp.bfloat16

SEQ = 1024
D = 768
HEAD_DIM = 64
HALF = 384
FF = 1536
RANK = 8
BLOCK = 256
SHARD = 12
CHUNK = 256
CHUNKS = FF // CHUNK
WIDE = 512
WIDES = FF // WIDE
REL = (0, 3, 1, 2)
EPS = 1e-06
MASKED = -1e30

momentum_decay = 0.9
rate_inbound = 0.2
rate_outbound = 6.0
rate_expand = 0.3
rate_shrink = 0.25
rate_gains = 0.0005
rope_base = 10000.0

ANY = pl.BlockSpec(memory_space=pl.ANY)
SMEM = pl.BlockSpec(memory_space=pltpu.SMEM)


def nn(a, b):
    return jnp.dot(a, b, preferred_element_type=F32)


def nt(a, b):
    return lax.dot_general(a, b, (((1,), (1,)), ((), ())), preferred_element_type=F32)


def tn(a, b):
    return lax.dot_general(a, b, (((0,), (0,)), ((), ())), preferred_element_type=F32)


def params(mib=56):
    return pltpu.CompilerParams(vmem_limit_bytes=mib * 2**20)


def cost(flops, moved):
    return pl.CostEstimate(flops=flops // 64, bytes_accessed=moved // 64, transcendentals=0)


def full(shape):
    return pl.BlockSpec(shape, lambda *_: (0,) * len(shape))


def like(shape, dtype):
    return jax.ShapeDtypeStruct(shape, dtype)


def shift(v, axis, d):
    n = lax.axis_size(axis)
    return lax.ppermute(v, axis, [(i, (i + d) % n) for i in range(n)])


def swap(v):
    return lax.ppermute(v, T, [(0, 1), (1, 0)])


def rounded(v):
    return lax.reduce_precision(v, exponent_bits=8, mantissa_bits=7)


def ring_terms(v, axis):
    low = v.astype(BF)
    return v, shift(low, axis, 2), shift(low, axis, 1), shift(low, axis, 3)


def ring_sum(terms):
    own, two, one, back = (v.astype(F32) for v in terms)
    return (own + two) + (one + back)


def shard_kernel(inbound, outbound, expand, shrink, out):
    for c in range(3):
        out[:, c * HALF : (c + 1) * HALF] = inbound[c].astype(BF)
    out[:, 1152:1536] = outbound[...].astype(BF)
    for j in range(WIDES):
        for c in range(2):
            at = 1536 + (2 * j + c) * WIDE
            out[:, at : at + WIDE] = expand[:, c, j * WIDE : (j + 1) * WIDE].astype(BF)
    out[:, 4608:] = shrink[...].astype(BF)


def weight_shard(inbound, outbound, expand, shrink):
    return pl.pallas_call(
        shard_kernel,
        out_shape=like((SHARD, 6144), BF),
        compiler_params=params(),
        cost_estimate=cost(10**5, 2**19),
    )(inbound, outbound, expand, shrink)


def column_kernel(place, own, one, back, two, attn, feed, rows):
    z = place[2]
    pieces = [r[...].astype(F32) for r in (own, one, two, back)]
    for p in range(4):
        away = lax.rem(p + 4 - z, 4)
        piece = jnp.where(
            away == 0,
            pieces[0],
            jnp.where(away == 3, pieces[1], jnp.where(away == 2, pieces[2], pieces[3])),
        )
        rows[p * SHARD : (p + 1) * SHARD, :] = piece
    attn[...] = rows[:, :1536].astype(BF)
    feed[...] = rows[:, 1536:].astype(BF)


def rows_of_column(place, pieces):
    widths = (1536, 3 * FF)
    return pl.pallas_call(
        column_kernel,
        in_specs=[SMEM] + [full(pieces[0].shape)] * 4,
        out_specs=[full((48, w)) for w in widths],
        out_shape=[like((48, w), BF) for w in widths],
        scratch_shapes=[pltpu.VMEM((48, 6144), F32)],
        compiler_params=params(),
        cost_estimate=cost(10**6, 2**21),
    )(place, *pieces)


def pieces_of_ring(v, axis):
    return [v, shift(v, axis, 1), shift(v, axis, 3), shift(v, axis, 2)]


def place_pieces(pieces, target, sems, place):
    y0, x0 = place[0], place[1]
    copies = []
    for s, (piece, turn, at) in enumerate(zip(pieces, (0, 1, 2, 3, 3), (0, 0, 0, 0, D))):
        for i in range(4):
            row = lax.rem(y0 + REL[turn], 4) * 192 + lax.rem(x0 + REL[i], 4) * 48
            spot = target.at[pl.ds(pl.multiple_of(row, 16), 48), pl.ds(at, piece.shape[2])]
            copies.append(pltpu.make_async_copy(piece.at[i], spot, sems.at[s * 4 + i]))
    return copies


def turn_lanes(v, cos, low, high):
    return v * cos + pltpu.roll(v, 96, 1) * low + pltpu.roll(v, 32, 1) * high


def project_kernel(place, x, gain, cos, low, high, *refs):
    pieces, (normed, q, k, v, w_in, w_out, weights, sems) = refs[:5], refs[5:]
    i = pl.program_id(0)

    @pl.when(i == 0)
    def _():
        copies = place_pieces(pieces, weights, sems, place)
        for c in copies:
            c.start()
        for c in copies:
            c.wait()
        w_in[...] = weights[:, :1152]
        w_out[...] = weights[:, 1152:]

    xb = x[...].astype(F32)
    inverse = lax.rsqrt(jnp.mean(xb * xb, axis=1, keepdims=True) + EPS)
    n = (xb * inverse * gain[...]).astype(BF)
    normed[...] = n.T
    tables = cos[...], low[...], high[...]
    found = nn(n, weights[:, :1152])
    v[...] = found[:, 768:].astype(BF)
    for p in range(3):
        at = slice(p * 128, (p + 1) * 128)
        q[:, at] = (turn_lanes(found[:, at], *tables) * 0.125).astype(BF)
        k[:, at] = turn_lanes(found[:, HALF + p * 128 : HALF + (p + 1) * 128], *tables).astype(BF)


def project(place, x, gain, tables, pieces):
    rows = lambda w: pl.BlockSpec((512, w), lambda i: (i, 0))
    return pl.pallas_call(
        project_kernel,
        grid=(2,),
        in_specs=[SMEM, rows(D), full((1, D)), rows(128), rows(128), rows(128)] + [ANY] * 5,
        out_specs=[pl.BlockSpec((D, 512), lambda i: (0, i))]
        + [rows(HALF), rows(HALF), rows(HALF), full((D, 1152)), full((D, HALF))],
        out_shape=[like((D, SEQ), BF)]
        + [like((SEQ, HALF), BF)] * 3
        + [like((D, 1152), BF), like((D, HALF), BF)],
        scratch_shapes=[pltpu.VMEM((D, 1536), BF), pltpu.SemaphoreType.DMA((20,))],
        compiler_params=params(),
        cost_estimate=cost(2 * SEQ * D * 1152, 8 * 2**20),
    )(place, x, gain, *tables, *pieces)


def head_lanes(rows, h):
    lane = lax.broadcasted_iota(jnp.int32, (rows, 128), 1)
    return (lane < 64) if h == 0 else (lane >= 64)


def three_terms(v):
    one = v.astype(BF).astype(F32)
    two = (v - one).astype(BF).astype(F32)
    return one, two, v - one - two


def both_heads(v):
    zero = jnp.zeros((), BF)
    return [jnp.where(head_lanes(v.shape[0], h), v, zero) for h in range(2)]


def attend_kernel(q, k, v, fq, fk, out, fq_out):
    keys = jnp.concatenate([k[...], fk[...]], axis=1)
    vals = v[...]
    lane = lax.broadcasted_iota(jnp.int32, (256, 128), 1)
    first = head_lanes(256, 0)
    scores = []
    for b in range(4):
        rows = slice(b * 256, (b + 1) * 256)
        f = fq[rows, :]
        heads = [jnp.concatenate([m, f], axis=1) for m in both_heads(q[rows, :])]
        scores.append(nt(jnp.concatenate(heads, axis=0), keys[: (b + 1) * 256]))
    for b in range(4):
        rows = slice(b * 256, (b + 1) * 256)
        s = scores[b]
        largest = jnp.max(s, axis=1, keepdims=True)
        e = jnp.exp(s - largest)
        sums = jnp.sum(e, axis=1, keepdims=True)
        o = nn(e.astype(BF), vals[: (b + 1) * 256]) * (1.0 / sums)
        out[rows, :] = jnp.where(first, o[:256], o[256:]).astype(BF)
        one, two, three = three_terms(-(largest + jnp.log(sums)))
        for h in range(2):
            at = slice(h * 256, (h + 1) * 256)
            extra = jnp.where(lane == 3, one[at], jnp.where(lane == 4, two[at], three[at]))
            fq_out[h, rows, :] = jnp.where((lane >= 3) & (lane < 6), extra.astype(BF), fq[rows, :])


def attend(q, k, v, fq, fk):
    pair = pl.BlockSpec((SEQ, 128), lambda j: (0, j))
    return pl.pallas_call(
        attend_kernel,
        grid=(3,),
        in_specs=[pair, pair, pair, full((SEQ, 128)), full((SEQ, 128))],
        out_specs=[pair, pl.BlockSpec((2, SEQ, 128), lambda j: (j, 0, 0))],
        out_shape=[like((SEQ, HALF), BF), like((6, SEQ, 128), BF)],
        compiler_params=params(),
        cost_estimate=cost(8 * 10**9, 4 * 2**20),
    )(q, k, v, fq, fk)


def middle_kernel(x, att, att_other, gain, w, w_other, middle, second, turned):
    m = x[...].astype(F32) + nt(att[...], w[...]) + nt(att_other[...], w_other[...])
    middle[...] = m
    inverse = lax.rsqrt(jnp.mean(m * m, axis=1, keepdims=True) + EPS)
    low = (m * inverse * gain[...]).astype(BF)
    second[...] = low
    turned[...] = low.T


def middle_rows(x, att, att_other, gain, w, w_other):
    rows = lambda w: pl.BlockSpec((512, w), lambda i: (i, 0))
    return pl.pallas_call(
        middle_kernel,
        grid=(2,),
        in_specs=[rows(D), rows(HALF), rows(HALF), full((1, D)), full((D, HALF)), full((D, HALF))],
        out_specs=[rows(D), rows(D), pl.BlockSpec((D, 512), lambda i: (0, i))],
        out_shape=[like((SEQ, D), F32), like((SEQ, D), BF), like((D, SEQ), BF)],
        compiler_params=params(),
        cost_estimate=cost(2 * SEQ * D * D, 8 * 2**20),
    )(x, att, att_other, gain, w, w_other)


def two_terms(v):
    one = v.astype(BF).astype(F32)
    return jnp.concatenate([one, v - one], axis=0).astype(BF)


def folded(v):
    return v[0:8] + v[8:16]


def feed_kernel(place, second, turned, cot, err_e, err_s, start_e, start_s, both, down, *refs):
    (sum_e, sum_s, left_e, left_s, grad_out, own_out, send_out) = refs[:7]
    (hid, grads, grad_acc, out_acc) = refs[7:]
    j = pl.program_id(0)
    step = FEED_ROWS
    for b in range(SEQ // step):
        rows = slice(b * step, (b + 1) * step)
        n, c = second[rows, :], cot[rows, :]
        gu, hg = nn(n, both[...]), nn(c, down[...])
        g, u = gu[:, :WIDE], gu[:, WIDE:]
        sig = 0.5 * jnp.tanh(0.5 * g) + 0.5
        act = g * sig
        hid[rows, :] = (act * u).astype(BF)
        grads[rows, :WIDE] = (hg * u * (sig + act * (1.0 - sig))).astype(BF)
        grads[rows, WIDE:] = (hg * act).astype(BF)
    part = nt(hid[...], down[...])
    back = nt(grads[...], both[...])

    @pl.when(j == 0)
    def _():
        left_e[...] = jnp.zeros_like(left_e)
        out_acc[...] = part
        grad_acc[...] = back

    @pl.when(j > 0)
    def _():
        out_acc[...] += part
        grad_acc[...] += back

    low = (tn(hid[...], cot[...]) + err_s[0]).astype(BF)
    sum_s[...] = low
    left_s[...] = folded(nt(two_terms(start_s[...]), low))
    found = nn(turned[...], grads[...])
    for c in range(2):
        low = (found[:, c * WIDE : (c + 1) * WIDE] + err_e[0, c]).astype(BF)
        sum_e[c] = low
        left_e[:, c * D : (c + 1) * D] += folded(nt(two_terms(start_e[c]), low))

    @pl.when(j == WIDES - 1)
    def _():
        t = place[3]
        grad_out[...] = grad_acc[...].astype(BF)
        mine = pl.ds(pl.multiple_of(t * 512, 512), 512)
        other = pl.ds(pl.multiple_of((1 - t) * 512, 512), 512)
        own_out[...] = out_acc[mine, :]
        send_out[...] = out_acc[other, :].astype(BF)


FEED_ROWS = 512


def feed(place, second, turned, cot, err_e, err_s, start_e, start_s, weights):
    once = lambda shape: pl.BlockSpec(
        shape, lambda j: (0,) * len(shape), pipeline_mode=pl.Buffered(1)
    )
    return pl.pallas_call(
        feed_kernel,
        grid=(WIDES,),
        in_specs=[
            SMEM,
            once((SEQ, D)),
            once((D, SEQ)),
            once((SEQ, D)),
            pl.BlockSpec((1, 2, D, WIDE), lambda j: (0, 0, 0, j)),
            pl.BlockSpec((1, WIDE, D), lambda j: (0, j, 0)),
            pl.BlockSpec((2, RANK, WIDE), lambda j: (0, 0, j)),
            full((RANK, D)),
            pl.BlockSpec((D, 2 * WIDE), lambda j: (0, j)),
            pl.BlockSpec((D, WIDE), lambda j: (0, 2 * WIDES + j)),
        ],
        out_specs=[
            pl.BlockSpec((2, D, WIDE), lambda j: (0, 0, j)),
            pl.BlockSpec((WIDE, D), lambda j: (j, 0)),
            full((RANK, 2 * D)),
            pl.BlockSpec((RANK, WIDE), lambda j: (0, j)),
            once((SEQ, D)),
            once((512, D)),
            once((512, D)),
        ],
        out_shape=[
            like((2, D, FF), BF),
            like((FF, D), BF),
            like((RANK, 2 * D), F32),
            like((RANK, FF), F32),
            like((SEQ, D), BF),
            like((512, D), F32),
            like((512, D), BF),
        ],
        scratch_shapes=[
            pltpu.VMEM((SEQ, WIDE), BF),
            pltpu.VMEM((SEQ, 2 * WIDE), BF),
            pltpu.VMEM((SEQ, D), F32),
            pltpu.VMEM((SEQ, D), F32),
        ],
        compiler_params=params(60),
        cost_estimate=cost(18 * SEQ * D * FF, 40 * 2**20),
    )(place, second, turned, cot, err_e, err_s, start_e, start_s, weights, weights)


def by_eight(v):
    return jnp.sum(v.reshape(-1, 8, v.shape[1]), axis=0)


def branch_kernel(place, cot, grad, grad_other, middle, gain, att, err, start, w_out, *refs):
    middle_grad, att_grad, gain_sum, sums, left, acc = refs
    i = pl.program_id(0)

    @pl.when(i == 0)
    def _():
        acc[...] = jnp.zeros_like(acc)
        gain_sum[...] = jnp.zeros_like(gain_sum)

    m = middle[...]
    inverse = lax.rsqrt(jnp.mean(m * m, axis=1, keepdims=True) + EPS)
    unit = m * inverse
    w = grad[...].astype(F32) + grad_other[...].astype(F32)
    a = w * gain[...]
    mg = cot[...].astype(F32) + inverse * (a - unit * jnp.mean(a * unit, axis=1, keepdims=True))
    branch = mg.astype(BF)
    att_grad[...] = nn(branch, w_out[...]).astype(BF)
    acc[...] += tn(att[...], branch)

    @pl.when(i == place[3])
    def _():
        middle_grad[...] = mg
        gain_sum[...] += by_eight(w * unit)

    @pl.when(i == 1)
    def _():
        low = (acc[...] + err[0]).astype(BF)
        sums[...] = low
        left[...] = folded(nt(two_terms(start[...]), low))


def branch_rows(place, cot, grad, grad_other, middle, gain, att, err, start, w_out):
    rows = lambda w: pl.BlockSpec((512, w), lambda i, p: (i, 0))
    fixed = lambda shape: pl.BlockSpec(shape, lambda i, p: (0,) * len(shape))
    return pl.pallas_call(
        branch_kernel,
        grid_spec=pltpu.PrefetchScalarGridSpec(
            num_scalar_prefetch=1,
            grid=(2,),
            in_specs=[
                rows(D),
                rows(D),
                rows(D),
                rows(D),
                fixed((1, D)),
                rows(HALF),
                fixed((1, HALF, D)),
                fixed((RANK, D)),
                fixed((D, HALF)),
            ],
            out_specs=[
                fixed((512, D)),
                rows(HALF),
                fixed((8, D)),
                fixed((HALF, D)),
                fixed((RANK, HALF)),
            ],
            scratch_shapes=[pltpu.VMEM((HALF, D), F32)],
        ),
        out_shape=[
            like((512, D), F32),
            like((SEQ, HALF), BF),
            like((8, D), F32),
            like((HALF, D), BF),
            like((RANK, HALF), F32),
        ],
        compiler_params=params(),
        cost_estimate=cost(4 * SEQ * D * HALF, 14 * 2**20),
    )(place, cot, grad, grad_other, middle, gain, att, err, start, w_out)


def attend_back_kernel(q, k, v, att, grad, fq, fk, cos, low, high, out, dk_acc, dv_acc):
    lane = lax.broadcasted_iota(jnp.int32, (256, 128), 1)
    ones = jnp.where(lax.broadcasted_iota(jnp.int32, (SEQ, 128), 1) < 3, 1.0, 0.0).astype(BF)
    keys = jnp.concatenate([k[...], fk[...]], axis=1)
    vals = jnp.concatenate([v[...], ones], axis=1)
    kt = k[...].T
    dk_acc[...] = jnp.zeros_like(dk_acc)
    dv_acc[...] = jnp.zeros_like(dv_acc)
    for b in range(4):
        rows = slice(b * 256, (b + 1) * 256)
        count = (b + 1) * 256
        qs, gs = both_heads(q[rows, :]), both_heads(grad[rows, :])
        q_rows = [jnp.concatenate([qs[h], fq[h, rows, :]], axis=1) for h in range(2)]
        g_rows = []
        for h in range(2):
            centre = jnp.sum(gs[h].astype(F32) * att[rows, :].astype(F32), axis=1, keepdims=True)
            one, two, three = three_terms(-centre)
            extra = jnp.where(lane == 0, one, jnp.where(lane == 1, two, three))
            fg = jnp.where(lane < 3, extra, 0.0).astype(BF)
            g_rows.append(jnp.concatenate([gs[h], fg], axis=1))
        soft = jnp.exp(nt(keys[:count], jnp.concatenate(q_rows, axis=0)))
        ds = (soft * nt(vals[:count], jnp.concatenate(g_rows, axis=0))).astype(BF)
        dv_acc[:count, :] += nn(soft.astype(BF), jnp.concatenate(gs, axis=0))
        dk_acc[:count, :] += nn(ds, jnp.concatenate(qs, axis=0))
        part = nn(kt[:, :count], ds)
        dq = jnp.concatenate([part[:64, :256], part[64:, 256:]], axis=0).T * 0.125
        out[0, rows, :] = turn_lanes(dq, cos[rows, :], -low[rows, :], -high[rows, :]).astype(BF)
    out[1] = turn_lanes(dk_acc[...], cos[...], -low[...], -high[...]).astype(BF)
    out[2] = dv_acc[...].astype(BF)


def attend_back(q, k, v, att, grad, fq, fk, tables):
    pair = pl.BlockSpec((SEQ, 128), lambda j: (0, j))
    return pl.pallas_call(
        attend_back_kernel,
        grid=(3,),
        in_specs=[pair] * 5
        + [pl.BlockSpec((2, SEQ, 128), lambda j: (j, 0, 0))]
        + [full((SEQ, 128))] * 4,
        out_specs=pl.BlockSpec((3, SEQ, 128), lambda j: (0, 0, j)),
        out_shape=like((3, SEQ, HALF), BF),
        scratch_shapes=[
            pltpu.VMEM((SEQ, 128), F32),
            pltpu.VMEM((SEQ, 128), F32),
        ],
        compiler_params=params(),
        cost_estimate=cost(16 * 10**9, 8 * 2**20),
    )(q, k, v, att, grad, fq, fk, *tables)


def inbound_kernel(turned, dproj, err, start, left_o, left_e, left_s, sums, left):
    c = pl.program_id(0)

    @pl.when(c == 0)
    def _():
        left[:, LEFT_O] = left_o[...].astype(BF)
        left[:, LEFT_E] = left_e[...].astype(BF)
        left[:, LEFT_S] = left_s[...].astype(BF)

    low = (nn(turned[...], dproj[0]) + err[0, 0]).astype(BF)
    sums[0] = low
    found = folded(nt(two_terms(start[0]), low)).astype(BF)
    for n in range(3):

        @pl.when(c == n)
        def _():
            left[:, n * D : (n + 1) * D] = found


LEFT_O = slice(3 * D, 3 * D + HALF)
LEFT_E = slice(3 * D + HALF, 5 * D + HALF)
LEFT_S = slice(5 * D + HALF, 5 * D + HALF + FF)
LEFT = 5 * D + HALF + FF


def inbound_sums(turned, dproj, err, start, left_o, left_e, left_s):
    return pl.pallas_call(
        inbound_kernel,
        grid=(3,),
        in_specs=[
            full((D, SEQ)),
            pl.BlockSpec((1, SEQ, HALF), lambda c: (c, 0, 0)),
            pl.BlockSpec((1, 1, D, HALF), lambda c: (0, c, 0, 0)),
            pl.BlockSpec((1, RANK, HALF), lambda c: (c, 0, 0)),
            full((RANK, HALF)),
            full((RANK, 2 * D)),
            full((RANK, FF)),
        ],
        out_specs=[pl.BlockSpec((1, D, HALF), lambda c: (c, 0, 0)), full((RANK, LEFT))],
        out_shape=[like((3, D, HALF), BF), like((RANK, LEFT), BF)],
        compiler_params=params(),
        cost_estimate=cost(2 * SEQ * D * 1152, 12 * 2**20),
    )(turned, dproj, err, start, left_o, left_e, left_s)


def first_grad_kernel(place, dproj, weights, own, send, acc):
    c = pl.program_id(0)

    @pl.when(c == 0)
    def _():
        acc[...] = jnp.zeros_like(acc)

    acc[...] += nt(dproj[0], weights[...])

    @pl.when(c == 2)
    def _():
        t = place[3]
        own[...] = acc[pl.ds(pl.multiple_of(t * 512, 512), 512), :]
        send[...] = acc[pl.ds(pl.multiple_of((1 - t) * 512, 512), 512), :].astype(BF)


def first_grad_rows(place, dproj, w_in):
    return pl.pallas_call(
        first_grad_kernel,
        grid=(3,),
        in_specs=[
            SMEM,
            pl.BlockSpec((1, SEQ, HALF), lambda c: (c, 0, 0)),
            pl.BlockSpec((D, HALF), lambda c: (0, c)),
        ],
        out_specs=[full((512, D)), full((512, D))],
        out_shape=[like((512, D), F32), like((512, D), BF)],
        scratch_shapes=[pltpu.VMEM((SEQ, D), F32)],
        compiler_params=params(),
        cost_estimate=cost(2 * SEQ * D * 1152, 8 * 2**20),
    )(place, dproj, w_in)


def input_grad_kernel(x, gain, middle_grad, own, other, gain_second, out, gains):
    xb = x[...].astype(F32)
    inverse = lax.rsqrt(jnp.mean(xb * xb, axis=1, keepdims=True) + EPS)
    unit = xb * inverse
    w = own[...] + other[...].astype(F32)
    a = w * gain[...]
    back = inverse * (a - unit * jnp.mean(a * unit, axis=1, keepdims=True))
    out[...] = (middle_grad[...] + back).astype(BF)
    gains[:, :D] = by_eight(w * unit)
    gains[:, D:] = gain_second[...]


def input_grad_rows(x, gain, middle_grad, own, other, gain_second):
    shapes = [(512, D), (1, D), (512, D), (512, D), (512, D), (8, D)]
    return pl.pallas_call(
        input_grad_kernel,
        in_specs=[full(s) for s in shapes],
        out_specs=[full((512, D)), full((8, 2 * D))],
        out_shape=[like((512, D), BF), like((8, 2 * D), F32)],
        compiler_params=params(),
        cost_estimate=cost(10**7, 6 * 2**20),
    )(x, gain, middle_grad, own, other, gain_second)


def orthonormal(factors):
    done = [jnp.zeros_like(f) for f in factors]
    for k in range(RANK):
        for m, f in enumerate(factors):
            row = f[k : k + 1]
            if k > 0:
                coeffs = jnp.sum(done[m] * row, axis=1, keepdims=True)
                row = row - jnp.sum(coeffs * done[m], axis=0, keepdims=True)
            length = jnp.sum(row * row, axis=1, keepdims=True)
            row = row * lax.rsqrt(length + EPS)
            here = lax.broadcasted_iota(jnp.int32, f.shape, 0) == k
            done[m] = jnp.where(here, row, done[m])
    return done


def joined(mine, other, t):
    return jnp.concatenate(
        [jnp.where(t == 0, mine, other), jnp.where(t == 0, other, mine)], axis=1
    )


RIGHT_E = 3 * HALF
RIGHT_O = RIGHT_E + 2 * FF
RIGHT_S = RIGHT_O + D
RIGHT_G = RIGHT_S + D
RIGHT = RIGHT_G + 2 * D


def factor_kernel(place, mine, other, gains, h_i, h_o, h_e, h_s, *refs):
    left_i, left_o, left_e, left_s, right = refs[:5]
    sum_i, sum_o, sum_e, sum_s, sems = refs[5:]
    pairs = ((h_i, sum_i), (h_o, sum_o), (h_e, sum_e), (h_s, sum_s))
    copies = [pltpu.make_async_copy(h, v, sems.at[n]) for n, (h, v) in enumerate(pairs)]
    for c in copies:
        c.start()
    t = place[3]
    a, b = mine[...], other[...]
    both = a + b
    factors = [both[:, c * D : (c + 1) * D] for c in range(3)]
    factors.append(joined(a[:, LEFT_O], b[:, LEFT_O], t))
    at = LEFT_E.start
    factors += [both[:, at : at + D], both[:, at + D : at + 2 * D]]
    factors.append(joined(a[:, LEFT_S], b[:, LEFT_S], t))
    found = orthonormal(factors)
    own_o = jnp.where(t == 0, found[3][:, :HALF], found[3][:, HALF:])
    own_s = jnp.where(t == 0, found[6][:, :FF], found[6][:, FF:])
    left_o[...] = own_o
    left_s[...] = own_s
    for c in range(3):
        left_i[c] = found[c]
    for c in range(2):
        left_e[c] = found[4 + c]
    right[:, RIGHT_G:] = gains[...].astype(BF)
    for c in copies:
        c.wait()
    for c in range(3):
        right[:, c * HALF : (c + 1) * HALF] = folded(nn(two_terms(found[c]), sum_i[c])).astype(BF)
    for c in range(2):
        at = RIGHT_E + c * FF
        right[:, at : at + FF] = folded(nn(two_terms(found[4 + c]), sum_e[c])).astype(BF)
    right[:, RIGHT_O : RIGHT_O + D] = folded(nn(two_terms(own_o), sum_o[...])).astype(BF)
    right[:, RIGHT_S : RIGHT_S + D] = folded(nn(two_terms(own_s), sum_s[...])).astype(BF)


def factors_of(place, mine, other, gains, sum_i, sum_o, sum_e, sum_s):
    sums = (sum_i, sum_o, sum_e, sum_s)
    outs = [(3, RANK, D), (RANK, HALF), (2, RANK, D), (RANK, FF)]
    return pl.pallas_call(
        factor_kernel,
        in_specs=[SMEM, full((RANK, LEFT)), full((RANK, LEFT)), full((8, 2 * D))] + [ANY] * 4,
        out_specs=[full(s) for s in outs] + [full((RANK, RIGHT))],
        out_shape=[like(s, F32) for s in outs] + [like((RANK, RIGHT), BF)],
        scratch_shapes=[pltpu.VMEM(s.shape, BF) for s in sums] + [pltpu.SemaphoreType.DMA((4,))],
        compiler_params=params(),
        cost_estimate=cost(10**8, 10 * 2**20),
    )(place, mine, other, gains, *sums)


def left_terms(v):
    one = v.astype(BF).astype(F32)
    two = v - one
    return jnp.concatenate([one, one, two, two], axis=0).astype(BF)


def right_terms(v):
    one = v.astype(BF).astype(F32)
    two = v - one
    return jnp.concatenate([one, two, one, two], axis=0).astype(BF)


def own_rows(terms, place):
    dp = (place[0] * 4 + place[1]) * 4 + place[2]
    row = lax.broadcasted_iota(jnp.int32, (16, D), 0)
    col = lax.broadcasted_iota(jnp.int32, (16, D), 1)
    pick = jnp.where((row < SHARD) & (col == row + SHARD * dp), 1.0, 0.0).astype(BF)
    return nt(pick, terms).astype(BF)


def moved(old, weight, rate, own, momentum, updated):
    new = momentum_decay * old + own
    momentum[...] = new
    updated[...] = weight - rate * new


def feed_last_kernel(place, left_e, left_s, sums, tail, sum_e, sum_s, old_e, old_s, w_e, w_s, *refs):
    res_e, res_s, mom_e, mom_s, new_e, new_s, right_e, right_s = refs
    scale = 1.0 / 64
    for c in range(2):
        r = sums[c][...] * scale
        right_e[c] = r
        lt, rt = left_terms(left_e[c]), right_terms(r)
        res_e[0, c] = sum_e[c].astype(F32) - tn(lt, rt)
        own = nn(own_rows(lt, place), rt)[:SHARD]
        moved(old_e[:, c, :], w_e[:, c, :], rate_expand, own, mom_e.at[:, c, :], new_e.at[:, c, :])
    r = tail[...] * scale
    right_s[...] = r
    lt, rt = left_terms(left_s[...]), right_terms(r)
    res_s[0] = sum_s[...].astype(F32) - tn(lt, rt)
    own = nn(own_rows(rt, place), lt)[:SHARD]
    moved(old_s[...], w_s[...], rate_shrink, own, mom_s, new_s)


def feed_last(place, left_e, left_s, sums, right_s, sum_e, sum_s, old_e, old_s, w_e, w_s):
    lanes = lambda rows: pl.BlockSpec((rows, CHUNK), lambda j: (0, j))
    pair = pl.BlockSpec((SHARD, 2, CHUNK), lambda j: (0, 0, j))
    def kernel(place, left_e, left_s, s0, s1, *refs):
        feed_last_kernel(place, left_e, left_s, (s0, s1), *refs)

    return pl.pallas_call(
        kernel,
        grid=(CHUNKS,),
        in_specs=[
            SMEM,
            full((2, RANK, D)),
            lanes(RANK),
            pl.BlockSpec((RANK, CHUNK), lambda j: (0, j)),
            pl.BlockSpec((RANK, CHUNK), lambda j: (0, CHUNKS + j)),
            full((RANK, D)),
            pl.BlockSpec((2, D, CHUNK), lambda j: (0, 0, j)),
            pl.BlockSpec((CHUNK, D), lambda j: (j, 0)),
            pair,
            lanes(SHARD),
            pair,
            lanes(SHARD),
        ],
        out_specs=[
            pl.BlockSpec((1, 2, D, CHUNK), lambda j: (0, 0, 0, j)),
            pl.BlockSpec((1, CHUNK, D), lambda j: (0, j, 0)),
            pair,
            lanes(SHARD),
            pair,
            lanes(SHARD),
            pl.BlockSpec((2, RANK, CHUNK), lambda j: (0, 0, j)),
            full((RANK, D)),
        ],
        out_shape=[
            like((1, 2, D, FF), F32),
            like((1, FF, D), F32),
            like((SHARD, 2, FF), F32),
            like((SHARD, FF), F32),
            like((SHARD, 2, FF), F32),
            like((SHARD, FF), F32),
            like((2, RANK, FF), F32),
            like((RANK, D), F32),
        ],
        compiler_params=params(),
        cost_estimate=cost(10**8, 30 * 2**20),
    )(place, left_e, left_s, sums, sums, right_s, sum_e, sum_s, old_e, old_s, w_e, w_s)


def attn_last_kernel(place, left_i, left_o, sums, other, sum_i, sum_o, old_i, old_o, w_i, w_o, gains, old_g, *refs):
    res_i, res_o, mom_i, mom_o, new_i, new_o, right_i, right_o, mom_g, new_g, right_s = refs
    scale = 1.0 / 64
    for c in range(3):
        r = sums[:, c * HALF : (c + 1) * HALF] * scale
        right_i[c] = r
        lt, rt = left_terms(left_i[c]), right_terms(r)
        res_i[0, c] = sum_i[c].astype(F32) - tn(lt, rt)
        own = nn(own_rows(lt, place), rt)[:SHARD]
        moved(old_i[c], w_i[c], rate_inbound, own, mom_i.at[c], new_i.at[c])
    both = sums[:, RIGHT_O:] + other[...]
    r = both[:, :D] * scale
    right_o[...] = r
    lt, rt = left_terms(left_o[...]), right_terms(r)
    res_o[0] = sum_o[...].astype(F32) - tn(lt, rt)
    own = nn(own_rows(rt, place), lt)[:SHARD]
    moved(old_o[...], w_o[...], rate_outbound, own, mom_o, new_o)
    right_s[...] = both[:, D : 2 * D]
    for n in range(2):
        at = (2 + n) * D
        own = jnp.sum(both[:, at : at + D], axis=0, keepdims=True)
        row = slice(n, n + 1)
        moved(old_g[row], gains[row], rate_gains, own, mom_g.at[row], new_g.at[row])


def attn_last(place, left_i, left_o, sums, other, sum_i, sum_o, old_i, old_o, w_i, w_o, gains, old_g):
    args = (left_i, left_o, sums, other, sum_i, sum_o, old_i, old_o, w_i, w_o, gains, old_g)
    outs = [(1, 3, D, HALF), (1, HALF, D)]
    outs += [(3, SHARD, HALF), (SHARD, HALF)] * 2
    outs += [(3, RANK, HALF), (RANK, D), (2, D), (2, D), (RANK, D)]
    return pl.pallas_call(
        attn_last_kernel,
        in_specs=[SMEM] + [full(a.shape) for a in args],
        out_specs=[full(s) for s in outs],
        out_shape=[like(s, F32) for s in outs],
        compiler_params=params(),
        cost_estimate=cost(10**8, 8 * 2**20),
    )(place, *args)


def lane_tables(ids):
    zeros = jnp.sum((ids == 0).astype(jnp.int32))
    ones = jnp.sum((ids == 1).astype(jnp.int32))
    before = jnp.where(ids == 0, 0, jnp.where(ids == 1, zeros, zeros + ones))
    places = (jnp.arange(SEQ, dtype=jnp.int32) - before).astype(F32)
    lane = jnp.arange(128, dtype=jnp.int32)
    inverse = rope_base ** (-((lane % 32).astype(F32) * 2.0) / HEAD_DIM)
    angles = places[:, None] * inverse[None, :]
    first = (lane % 64 < 32)[None, :]
    sine = jnp.sin(angles)
    low, high = jnp.where(first, -sine, 0.0), jnp.where(first, 0.0, sine)
    kind = lane[None, :]
    same = ids[:, None] == kind
    fq = jnp.where((kind < 3) & same, 1.0, 0.0).astype(BF)
    fk = jnp.where(kind < 3, jnp.where(same, 0.0, MASKED), jnp.where(kind < 6, 1.0, 0.0))
    return (jnp.cos(angles), low, high), fq, fk.astype(BF)


def both_halves(own, t):
    other = swap(own)
    whole = jnp.zeros((SEQ, D), BF)
    whole = lax.dynamic_update_slice_in_dim(whole, own, t * 512, 0)
    return lax.dynamic_update_slice_in_dim(whole, other, (1 - t) * 512, 0)


def local(
    tokens,
    segment_ids,
    cotangent,
    norm_gains,
    gains_moment,
    inbound,
    outbound,
    expand,
    shrink,
    inbound_moment,
    outbound_moment,
    expand_moment,
    shrink_moment,
    inbound_error,
    outbound_error,
    expand_error,
    shrink_error,
    inbound_start,
    outbound_start,
    expand_start,
    shrink_start,
):
    y, x, z, t = (lax.axis_index(a) for a in DP_TENSOR)
    place = jnp.stack([y, x, z, t]).astype(jnp.int32)

    shard = weight_shard(inbound, outbound.T, jnp.swapaxes(expand, 0, 1), shrink.T)
    shard, segment_ids, tokens, cotangent = lax.optimization_barrier(
        (shard, segment_ids, tokens, cotangent)
    )
    column = [shard, shift(shard, Z, 1), shift(shard, Z, 3), shift(shard, Z, 2)]
    tables, fq, fk = lane_tables(segment_ids)
    column, tables, fq, fk = lax.optimization_barrier((column, tables, fq, fk))
    attn_rows, feed_rows = rows_of_column(place, column)
    feed_weights = lax.all_gather(feed_rows, (Y, X)).reshape(D, 3 * FF)
    x_all = both_halves(tokens, t)
    attn_ring = pieces_of_ring(attn_rows, X)
    attn_ring, x_all = lax.optimization_barrier((attn_ring, x_all))
    attn_ring = jnp.stack(attn_ring)
    cot_all = both_halves(cotangent, t)
    near = shift(attn_ring, Y, 1), shift(attn_ring, Y, 3)
    far = shift(near[0][..., :D], Y, 1), shift(near[1][..., D:], Y, 3)
    far, cot_all = lax.optimization_barrier((far, cot_all))
    in_pieces = [attn_ring, *near, *far]

    gain_one, gain_two = norm_gains[0:1], norm_gains[1:2]
    normed, q, k, v, w_in, w_out = project(place, x_all, gain_one, tables, in_pieces)
    w_other = swap(w_out)
    att, fq_all = attend(q, k, v, fq, fk)
    att, w_other = lax.optimization_barrier((att, w_other))
    middle, second, turned = middle_rows(x_all, att, swap(att), gain_two, w_out, w_other)

    start_e, start_s = jnp.swapaxes(expand_start, 1, 2), shrink_start.T
    sum_e, sum_s, left_e, left_s, grad, own_out, send_out = feed(
        place, second, turned, cot_all, expand_error, shrink_error, start_e, start_s, feed_weights
    )
    grad_other = swap(grad)
    middle_grad, att_grad, gain_second, sum_o, left_o = branch_rows(
        place, cot_all, grad, grad_other, middle, gain_two, att, outbound_error, outbound_start.T, w_out
    )

    dproj = attend_back(q, k, v, att, att_grad, fq_all, fk, tables)
    sum_i, left = inbound_sums(
        normed, dproj, inbound_error, jnp.swapaxes(inbound_start, 1, 2), left_o, left_e, left_s
    )

    left, dproj = lax.optimization_barrier((left, dproj))
    terms = ring_terms(left, Z)
    first_own, first_send = first_grad_rows(place, dproj, w_in)
    terms, first_own, first_send = lax.optimization_barrier((terms, first_own, first_send))
    terms = ring_terms(rounded(ring_sum(terms)), X)
    first_other = swap(first_send)
    terms, first_other = lax.optimization_barrier((terms, first_other))
    terms = ring_terms(rounded(ring_sum(terms)), Y)
    input_grad, gains = input_grad_rows(
        tokens, gain_one, middle_grad, first_own, first_other, gain_second
    )
    terms, gains = lax.optimization_barrier((terms, gains))
    mine = ring_sum(terms)
    left_i, left_o, left_e, left_s, right = factors_of(
        place, mine, swap(mine), gains, sum_i, sum_o, sum_e, sum_s
    )

    terms = ring_terms(right, Z)
    send_out = swap(send_out)
    terms, send_out = lax.optimization_barrier((terms, send_out))
    terms = ring_terms(rounded(ring_sum(terms)), X)
    own_middle = lax.dynamic_slice_in_dim(middle, t * 512, 512, 0)
    layer_output = (own_middle + (own_out + send_out.astype(F32))).astype(BF)
    terms, layer_output = lax.optimization_barrier((terms, layer_output))
    sums = ring_sum(ring_terms(rounded(ring_sum(terms)), Y))
    (
        res_i,
        res_o,
        inbound_momentum,
        outbound_momentum,
        inbound_updated,
        outbound_updated,
        right_i,
        right_o,
        gains_momentum,
        gains_updated,
        right_s,
    ) = attn_last(
        place,
        left_i,
        left_o,
        sums,
        swap(sums[:, RIGHT_O:]),
        sum_i,
        sum_o,
        inbound_moment,
        outbound_moment.T,
        inbound,
        outbound.T,
        norm_gains,
        gains_moment,
    )
    (
        res_e,
        res_s,
        expand_momentum,
        shrink_momentum,
        expand_updated,
        shrink_updated,
        right_e,
        right_s,
    ) = feed_last(
        place,
        left_e,
        left_s,
        sums[:, RIGHT_E:RIGHT_O],
        right_s,
        sum_e,
        sum_s,
        jnp.swapaxes(expand_moment, 0, 1),
        shrink_moment.T,
        jnp.swapaxes(expand, 0, 1),
        shrink.T,
    )
    return (
        layer_output,
        input_grad,
        gains_momentum,
        gains_updated,
        inbound_momentum,
        outbound_momentum.T,
        jnp.swapaxes(expand_momentum, 0, 1),
        shrink_momentum.T,
        inbound_updated,
        outbound_updated.T,
        jnp.swapaxes(expand_updated, 0, 1),
        shrink_updated.T,
        res_i,
        res_o,
        res_e,
        res_s,
        jnp.swapaxes(left_i, 1, 2),
        jnp.swapaxes(right_i, 1, 2),
        left_o.T,
        right_o.T,
        jnp.swapaxes(left_e, 1, 2),
        jnp.swapaxes(right_e, 1, 2),
        left_s.T,
        right_s.T,
    )


def solution(mesh):
    torus = Mesh(mesh.devices.reshape(4, 4, 4, mesh.shape["tensor"]), DP_TENSOR)
    return jax.shard_map(
        local,
        mesh=torus,
        in_specs=(
            P(DP_TENSOR, None),
            P(DP),
            P(DP_TENSOR, None),
            P(),
            P(),
            P(None, DP, T),
            P(T, DP),
            P(None, DP, T),
            P(T, DP),
            P(None, DP, T),
            P(T, DP),
            P(None, DP, T),
            P(T, DP),
            P(DP, None, None, T),
            P(DP, T, None),
            P(DP, None, None, T),
            P(DP, T, None),
            P(None, T, None),
            P(),
            P(None, T, None),
            P(),
        ),
        out_specs=(
            P(DP_TENSOR, None),
            P(DP_TENSOR, None),
            P(),
            P(),
            P(None, DP, T),
            P(T, DP),
            P(None, DP, T),
            P(T, DP),
            P(None, DP, T),
            P(T, DP),
            P(None, DP, T),
            P(T, DP),
            P(DP, None, None, T),
            P(DP, T, None),
            P(DP, None, None, T),
            P(DP, T, None),
            P(),
            P(None, T, None),
            P(T, None),
            P(),
            P(),
            P(None, T, None),
            P(T, None),
            P(),
        ),
        check_vma=False,
    )
```

```python
import jax
import jax.numpy as jnp
from jax import lax
from jax.experimental import pallas as pl
from jax.experimental.pallas import tpu as pltpu
from jax.sharding import Mesh
from jax.sharding import PartitionSpec as P

Y, X, Z, T = "dp_0", "dp_1", "dp_2", "tensor"
DP = (Y, X, Z)
DP_TENSOR = (Y, X, Z, T)
F32, BF = jnp.float32, jnp.bfloat16

SEQ = 1024
D = 768
HEAD_DIM = 64
HALF = 384
FF = 1536
RANK = 8
BLOCK = 256
SHARD = 12
CHUNK = 256
CHUNKS = FF // CHUNK
WIDE = 512
WIDES = FF // WIDE
REL = (0, 3, 1, 2)
EPS = 1e-06
MASKED = -1e30

momentum_decay = 0.9
rate_inbound = 0.2
rate_outbound = 6.0
rate_expand = 0.3
rate_shrink = 0.25
rate_gains = 0.0005
rope_base = 10000.0

HBM = pl.BlockSpec(memory_space=pltpu.HBM)
SMEM = pl.BlockSpec(memory_space=pltpu.SMEM)


def nn(a, b):
    return jnp.dot(a, b, preferred_element_type=F32)


def nt(a, b):
    return lax.dot_general(a, b, (((1,), (1,)), ((), ())), preferred_element_type=F32)


def tn(a, b):
    return lax.dot_general(a, b, (((0,), (0,)), ((), ())), preferred_element_type=F32)


def params(mib=56):
    return pltpu.CompilerParams(vmem_limit_bytes=mib * 2**20)


def cost(flops, moved):
    return pl.CostEstimate(flops=flops // 64, bytes_accessed=moved // 64, transcendentals=0)


def full(shape):
    return pl.BlockSpec(shape, lambda *_: (0,) * len(shape))


def like(shape, dtype):
    return jax.ShapeDtypeStruct(shape, dtype)


def shift(v, axis, d):
    n = lax.axis_size(axis)
    return lax.ppermute(v, axis, [(i, (i + d) % n) for i in range(n)])


def swap(v):
    return lax.ppermute(v, T, [(0, 1), (1, 0)])


def rounded(v):
    return lax.reduce_precision(v, exponent_bits=8, mantissa_bits=7)


def ring_terms(v, axis):
    low = v.astype(BF)
    return v, shift(low, axis, 2), shift(low, axis, 1), shift(low, axis, 3)


def ring_sum(terms):
    own, two, one, back = (v.astype(F32) for v in terms)
    return (own + two) + (one + back)


def shard_kernel(inbound, outbound, expand, shrink, out):
    for c in range(3):
        out[:, c * HALF : (c + 1) * HALF] = inbound[c].astype(BF)
    out[:, 1152:1536] = outbound[...].astype(BF)
    for j in range(WIDES):
        for c in range(2):
            at = 1536 + (2 * j + c) * WIDE
            out[:, at : at + WIDE] = expand[:, c, j * WIDE : (j + 1) * WIDE].astype(BF)
    out[:, 4608:] = shrink[...].astype(BF)


def weight_shard(inbound, outbound, expand, shrink):
    return pl.pallas_call(
        shard_kernel,
        out_shape=like((SHARD, 6144), BF),
        compiler_params=params(16),
        cost_estimate=cost(10**5, 2**19),
    )(inbound, outbound, expand, shrink)


def column_kernel(place, own, one, back, two, attn, feed, rows):
    z = place[2]
    pieces = [r[...].astype(F32) for r in (own, one, two, back)]
    for p in range(4):
        away = lax.rem(p + 4 - z, 4)
        piece = jnp.where(
            away == 0,
            pieces[0],
            jnp.where(away == 3, pieces[1], jnp.where(away == 2, pieces[2], pieces[3])),
        )
        rows[p * SHARD : (p + 1) * SHARD, :] = piece
    attn[...] = rows[:, :1536].astype(BF)
    feed[...] = rows[:, 1536:].astype(BF)


def rows_of_column(place, pieces):
    widths = (1536, 3 * FF)
    return pl.pallas_call(
        column_kernel,
        in_specs=[SMEM] + [full(pieces[0].shape)] * 4,
        out_specs=[full((48, w)) for w in widths],
        out_shape=[like((48, w), BF) for w in widths],
        scratch_shapes=[pltpu.VMEM((48, 6144), F32)],
        compiler_params=params(16),
        cost_estimate=cost(10**6, 2**21),
    )(place, *pieces)


def pieces_of_ring(v, axis):
    return [v, shift(v, axis, 1), shift(v, axis, 3), shift(v, axis, 2)]


def place_pieces(pieces, target, sems, place):
    y0, x0 = place[0], place[1]
    copies = []
    for s, (piece, turn, at) in enumerate(zip(pieces, (0, 1, 2, 3, 3), (0, 0, 0, 0, D))):
        for i in range(4):
            row = lax.rem(y0 + REL[turn], 4) * 192 + lax.rem(x0 + REL[i], 4) * 48
            spot = target.at[pl.ds(pl.multiple_of(row, 16), 48), pl.ds(at, piece.shape[2])]
            copies.append(pltpu.make_async_copy(piece.at[i], spot, sems.at[s * 4 + i]))
    return copies


def turn_lanes(v, cos, low, high):
    return v * cos + pltpu.roll(v, 96, 1) * low + pltpu.roll(v, 32, 1) * high


def head_lanes(rows, h):
    lane = lax.broadcasted_iota(jnp.int32, (rows, 128), 1)
    return (lane < 64) if h == 0 else (lane >= 64)


def three_terms(v):
    one = v.astype(BF).astype(F32)
    two = (v - one).astype(BF).astype(F32)
    return one, two, v - one - two


def both_heads(v):
    zero = jnp.zeros((), BF)
    return [jnp.where(head_lanes(v.shape[0], h), v, zero) for h in range(2)]


def pair_forward(q, k, v, fq, fk, out, fq_out):
    keys = jnp.concatenate([k[...], fk[...]], axis=1)
    vals = v[...]
    lane = lax.broadcasted_iota(jnp.int32, (256, 128), 1)
    first = head_lanes(256, 0)
    scores = []
    for b in range(4):
        rows = slice(b * 256, (b + 1) * 256)
        f = fq[rows, :]
        heads = [jnp.concatenate([m, f], axis=1) for m in both_heads(q[rows, :])]
        scores.append(nt(jnp.concatenate(heads, axis=0), keys[: (b + 1) * 256]))
    for b in range(4):
        rows = slice(b * 256, (b + 1) * 256)
        s = scores[b]
        largest = jnp.max(s, axis=1, keepdims=True)
        e = jnp.exp(s - largest)
        sums = jnp.sum(e, axis=1, keepdims=True)
        o = nn(e.astype(BF), vals[: (b + 1) * 256]) * (1.0 / sums)
        out[rows, :] = jnp.where(first, o[:256], o[256:]).astype(BF)
        one, two, three = three_terms(-(largest + jnp.log(sums)))
        for h in range(2):
            at = slice(h * 256, (h + 1) * 256)
            extra = jnp.where(lane == 3, one[at], jnp.where(lane == 4, two[at], three[at]))
            fq_out[h, rows, :] = jnp.where((lane >= 3) & (lane < 6), extra.astype(BF), fq[rows, :])


def attention_kernel(place, gain, *refs):
    hbm_in, pieces, hbm_out, refs = refs[:6], refs[6:11], refs[11:19], refs[19:]
    held, made, refs = refs[:6], refs[6:13], refs[13:]
    piece_sems, in_sems, out_sems = refs
    x, cos, low, high, fq, fk = held
    normed, weights, q, k, v, att, fq_all = made
    copy = pltpu.make_async_copy
    gets = [copy(hbm_in[0].at[pl.ds(i * 512, 512)], x.at[pl.ds(i * 512, 512)], in_sems.at[i]) for i in range(2)]
    gets += [copy(h, r, in_sems.at[n + 2]) for n, (h, r) in enumerate(zip(hbm_in[1:], held[1:]))]
    puts = [copy(r, h, out_sems.at[n]) for n, (r, h) in enumerate(zip(made, hbm_out))]
    put_out = copy(weights.at[:, pl.ds(3 * HALF, HALF)], hbm_out[7], out_sems.at[7])
    placed = place_pieces(pieces, weights, piece_sems, place)
    for c in gets[:2] + placed + gets[2:]:
        c.start()
    for i in range(2):
        rows = slice(i * 512, (i + 1) * 512)
        gets[i].wait()
        xb = x[rows, :].astype(F32)
        inverse = lax.rsqrt(jnp.mean(xb * xb, axis=1, keepdims=True) + EPS)
        n = (xb * inverse * gain[...]).astype(BF)
        x[rows, :] = n
        normed[:, rows] = n.T
    puts[0].start()
    for c in placed:
        c.wait()
    puts[1].start()
    put_out.start()
    for c in gets[2:]:
        c.wait()
    for i in range(2):
        rows = slice(i * 512, (i + 1) * 512)
        found = nn(x[rows, :], weights[:, :1152])
        tables = cos[rows, :], low[rows, :], high[rows, :]
        v[rows, :] = found[:, 768:].astype(BF)
        for p in range(3):
            at = slice(p * 128, (p + 1) * 128)
            q[rows, at] = (turn_lanes(found[:, at], *tables) * 0.125).astype(BF)
            k_lanes = found[:, HALF + p * 128 : HALF + (p + 1) * 128]
            k[rows, at] = turn_lanes(k_lanes, *tables).astype(BF)
    for c in puts[2:5]:
        c.start()

    def one_pair(p, carry):
        lanes = pl.ds(pl.multiple_of(p * 128, 128), 128)
        views = [r.at[:, lanes] for r in (q, k, v)]
        pair_forward(*views, fq, fk, att.at[:, lanes], fq_all.at[pl.ds(2 * p, 2)])
        return carry

    lax.fori_loop(0, 3, one_pair, 0)
    for c in puts[5:]:
        c.start()
    put_out.wait()
    for c in puts:
        c.wait()


def attention(place, gain, x, tables, fq, fk, pieces):
    arrays = (x, *tables, fq, fk)
    half = like((SEQ, HALF), BF)
    outs = [like((D, SEQ), BF), like((D, 2 * D), BF), half, half, half, half, like((6, SEQ, 128), BF)]
    return pl.pallas_call(
        attention_kernel,
        in_specs=[SMEM, full((1, D))] + [HBM] * 11,
        out_specs=[HBM] * 8,
        out_shape=[*outs, like((D, HALF), BF)],
        scratch_shapes=[pltpu.VMEM(a.shape, a.dtype) for a in arrays]
        + [pltpu.VMEM(o.shape, o.dtype) for o in outs]
        + [
            pltpu.SemaphoreType.DMA((20,)),
            pltpu.SemaphoreType.DMA((7,)),
            pltpu.SemaphoreType.DMA((8,)),
        ],
        compiler_params=params(),
        cost_estimate=cost(10**10, 12 * 2**20),
    )(place, gain, *arrays, *pieces)


def two_terms(v):
    one = v.astype(BF).astype(F32)
    return jnp.concatenate([one, v - one], axis=0).astype(BF)


def folded(v):
    return v[0:8] + v[8:16]


def feed_kernel(place, gain, *refs):
    h_x, h_att, h_other, h_w, h_w_other, h_cot, h_err_e, h_err_s, h_feed = refs[:9]
    start_e, start_s, sum_e, sum_s, left_e, left_s = refs[9:15]
    h_middle, h_grad, h_hid = refs[15:18]
    x, att, other, w_out, w_other, cot, both, down, err_e, err_s = refs[18:28]
    middle, second, turned, hid, grads, grad_low = refs[28:34]
    rows_sem, in_sem, both_sem, down_sem, err_sem, out_sem = refs[34:]
    j = pl.program_id(0)
    copy = pltpu.make_async_copy

    def lanes(n, width, start=0):
        return pl.ds(pl.multiple_of(start + n * width, width), width)

    def get_rows(i):
        rows = pl.ds(i * 512, 512)
        trio = ((h_x, x), (h_att, att), (h_other, other))
        return [copy(h.at[rows], r.at[rows], rows_sem.at[n, i]) for n, (h, r) in enumerate(trio)]

    def get_both(n):
        at = lanes(n, 2 * WIDE)
        return copy(h_feed.at[:, at], both.at[:, at], both_sem.at[n])

    def get_down(n):
        return copy(h_feed.at[:, lanes(n, WIDE, 2 * FF)], down.at[:, lanes(n, WIDE)], down_sem.at[n])

    def get_err(n):
        slot = lax.rem(n, 2)
        return (
            copy(h_err_e.at[0, :, :, lanes(n, WIDE)], err_e.at[slot], err_sem.at[0, slot]),
            copy(h_err_s.at[0, lanes(n, WIDE)], err_s.at[slot], err_sem.at[1, slot]),
        )

    get_w = copy(h_w, w_out, in_sem.at[0])
    get_w_other = copy(h_w_other, w_other, in_sem.at[1])
    get_cot = copy(h_cot, cot, in_sem.at[2])
    put_middle = copy(middle, h_middle, out_sem.at[0])
    put_grad = copy(grad_low, h_grad, out_sem.at[1])
    put_hid = copy(hid, h_hid, out_sem.at[2])

    @pl.when(j == 0)
    def _():
        order = [get_w, get_w_other, *get_rows(0), *get_rows(1), get_both(0), get_cot, get_down(0)]
        for c in order + [*get_err(0)]:
            c.start()
        for n in range(1, WIDES):
            get_both(n).start()
            get_down(n).start()
            if n == 1:
                for c in get_err(n):
                    c.start()
        left_e[...] = jnp.zeros_like(left_e)
        get_w.wait()
        get_w_other.wait()
        for i in range(2):
            rows = slice(i * 512, (i + 1) * 512)
            for c in get_rows(i):
                c.wait()
            m = x[rows, :].astype(F32) + nt(att[rows, :], w_out[...]) + nt(other[rows, :], w_other[...])
            middle[rows, :] = m
            inverse = lax.rsqrt(jnp.mean(m * m, axis=1, keepdims=True) + EPS)
            low = (m * inverse * gain[...]).astype(BF)
            second[rows, :] = low
            turned[:, rows] = low.T
        put_middle.start()

    get_both(j).wait()
    w_both = both.at[:, lanes(j, 2 * WIDE)]
    w_down = down.at[:, lanes(j, WIDE)]
    my_hid = hid.at[:, lanes(j, WIDE)]
    my_grads = grads.at[:, lanes(j, 2 * WIDE)]
    step = FEED_ROWS
    found = []
    for b in range(SEQ // step):
        found.append(nn(second[b * step : (b + 1) * step, :], w_both[...]))

    @pl.when(j == 0)
    def _():
        get_cot.wait()

    get_down(j).wait()
    for b in range(SEQ // step):
        rows = slice(b * step, (b + 1) * step)
        gu, hg = found[b], nn(cot[rows, :], w_down[...])
        g, u = gu[:, :WIDE], gu[:, WIDE:]
        sig = 0.5 * jnp.tanh(0.5 * g) + 0.5
        act = g * sig
        my_hid[rows, :] = (act * u).astype(BF)
        my_grads[rows, :WIDE] = (hg * u * (sig + act * (1.0 - sig))).astype(BF)
        my_grads[rows, WIDE:] = (hg * act).astype(BF)

    @pl.when(j == WIDES - 1)
    def _():
        put_hid.start()
        grad_low[...] = nt(grads[...], both[...]).astype(BF)
        put_grad.start()

    for c in get_err(j):
        c.wait()
    slot = lax.rem(j, 2)
    low = (tn(my_hid[...], cot[...]) + err_s[slot]).astype(BF)
    sum_s[...] = low
    left_s[...] = folded(nt(two_terms(start_s[...]), low))
    made = nn(turned[...], my_grads[...])
    for c in range(2):
        low = (made[:, c * WIDE : (c + 1) * WIDE] + err_e[slot, c]).astype(BF)
        sum_e[c] = low
        left_e[:, c * D : (c + 1) * D] += folded(nt(two_terms(start_e[c]), low))

    @pl.when(j + 2 < WIDES)
    def _():
        for c in get_err(j + 2):
            c.start()

    @pl.when(j == WIDES - 1)
    def _():
        put_middle.wait()
        put_hid.wait()
        put_grad.wait()


FEED_ROWS = 512


def feed(place, gain, x, att, other, weights, w_other, cot, err_e, err_s, feed_weights, start_e, start_s):
    arrays = (x, att, other, weights, w_other, cot, err_e, err_s, feed_weights)
    return pl.pallas_call(
        feed_kernel,
        grid=(WIDES,),
        in_specs=[SMEM, full((1, D))]
        + [HBM] * 9
        + [pl.BlockSpec((2, RANK, WIDE), lambda j: (0, 0, j)), full((RANK, D))],
        out_specs=[
            pl.BlockSpec((2, D, WIDE), lambda j: (0, 0, j)),
            pl.BlockSpec((WIDE, D), lambda j: (j, 0)),
            full((RANK, 2 * D)),
            pl.BlockSpec((RANK, WIDE), lambda j: (0, j)),
            HBM,
            HBM,
            HBM,
        ],
        out_shape=[
            like((2, D, FF), BF),
            like((FF, D), BF),
            like((RANK, 2 * D), F32),
            like((RANK, FF), F32),
            like((SEQ, D), F32),
            like((SEQ, D), BF),
            like((SEQ, FF), BF),
        ],
        scratch_shapes=[
            pltpu.VMEM((SEQ, D), BF),
            pltpu.VMEM((SEQ, HALF), BF),
            pltpu.VMEM((SEQ, HALF), BF),
            pltpu.VMEM((D, HALF), BF),
            pltpu.VMEM((D, HALF), BF),
            pltpu.VMEM((SEQ, D), BF),
            pltpu.VMEM((D, 2 * FF), BF),
            pltpu.VMEM((D, FF), BF),
            pltpu.VMEM((2, 2, D, WIDE), F32),
            pltpu.VMEM((2, WIDE, D), F32),
            pltpu.VMEM((SEQ, D), F32),
            pltpu.VMEM((SEQ, D), BF),
            pltpu.VMEM((D, SEQ), BF),
            pltpu.VMEM((SEQ, FF), BF),
            pltpu.VMEM((SEQ, 2 * FF), BF),
            pltpu.VMEM((SEQ, D), BF),
            pltpu.SemaphoreType.DMA((3, 2)),
            pltpu.SemaphoreType.DMA((3,)),
            pltpu.SemaphoreType.DMA((WIDES,)),
            pltpu.SemaphoreType.DMA((WIDES,)),
            pltpu.SemaphoreType.DMA((2, 2)),
            pltpu.SemaphoreType.DMA((3,)),
        ],
        compiler_params=params(60),
        cost_estimate=cost(18 * SEQ * D * FF, 40 * 2**20),
    )(place, gain, *arrays, start_e, start_s)


def down_kernel(place, hid, weights, own, send):
    t = place[3]
    for i in range(2):
        part = nt(hid[i * 512 : (i + 1) * 512, :], weights[...])

        @pl.when(t == i)
        def _():
            own[...] = part

        @pl.when(t != i)
        def _():
            send[...] = part.astype(BF)


def down_rows(place, hid, weights):
    return pl.pallas_call(
        down_kernel,
        grid=(1,),
        in_specs=[SMEM, full((SEQ, FF)), pl.BlockSpec((D, FF), lambda j: (0, 2))],
        out_specs=[full((512, D)), full((512, D))],
        out_shape=[like((512, D), F32), like((512, D), BF)],
        compiler_params=params(24),
        cost_estimate=cost(2 * SEQ * D * FF, 8 * 2**20),
    )(place, hid, weights)


def by_eight(v):
    return jnp.sum(v.reshape(-1, 8, v.shape[1]), axis=0)


LEFT_O = slice(3 * D, 3 * D + HALF)
LEFT_E = slice(3 * D + HALF, 5 * D + HALF)
LEFT_S = slice(5 * D + HALF, 5 * D + HALF + FF)
LEFT = 5 * D + HALF + FF


def pair_back(q, k, v, att, grad, fq, fk, cos, low, high, out, dk_acc, dv_acc):
    lane = lax.broadcasted_iota(jnp.int32, (256, 128), 1)
    ones = jnp.where(lax.broadcasted_iota(jnp.int32, (SEQ, 128), 1) < 3, 1.0, 0.0).astype(BF)
    keys = jnp.concatenate([k[...], fk[...]], axis=1)
    vals = jnp.concatenate([v[...], ones], axis=1)
    kt = k[...].T
    dk_acc[...] = jnp.zeros_like(dk_acc)
    dv_acc[...] = jnp.zeros_like(dv_acc)
    for b in range(4):
        rows = slice(b * 256, (b + 1) * 256)
        count = (b + 1) * 256
        qs, gs = both_heads(q[rows, :]), both_heads(grad[rows, :])
        q_rows = [jnp.concatenate([qs[h], fq[h, rows, :]], axis=1) for h in range(2)]
        g_rows = []
        for h in range(2):
            centre = jnp.sum(gs[h].astype(F32) * att[rows, :].astype(F32), axis=1, keepdims=True)
            one, two, three = three_terms(-centre)
            extra = jnp.where(lane == 0, one, jnp.where(lane == 1, two, three))
            fg = jnp.where(lane < 3, extra, 0.0).astype(BF)
            g_rows.append(jnp.concatenate([gs[h], fg], axis=1))
        soft = jnp.exp(nt(keys[:count], jnp.concatenate(q_rows, axis=0)))
        ds = (soft * nt(vals[:count], jnp.concatenate(g_rows, axis=0))).astype(BF)
        dv_acc[:count, :] += nn(soft.astype(BF), jnp.concatenate(gs, axis=0))
        dk_acc[:count, :] += nn(ds, jnp.concatenate(qs, axis=0))
        part = nn(kt[:, :count], ds)
        dq = jnp.concatenate([part[:64, :256], part[64:, 256:]], axis=0).T * 0.125
        out[0][rows, :] = turn_lanes(dq, cos[rows, :], -low[rows, :], -high[rows, :]).astype(BF)
    out[1][...] = turn_lanes(dk_acc[...], cos[...], -low[...], -high[...]).astype(BF)
    out[2][...] = dv_acc[...].astype(BF)


def backward_kernel(place, gain, start_o, start_i, left_e, left_s, *refs):
    hbm_in, hbm_out, refs = refs[:17], refs[17:21], refs[21:]
    gain_sum, left = refs[:2]
    held, made, refs = refs[2:19], refs[19:23], refs[23:]
    att_grad, acc, dk_acc, dv_acc, in_sems, out_sems = refs
    grad, grad_other, middle, cot, att, w_out, err_o, q, k, v, fq, fk, cos, low, high, turned, err_i = held
    middle_grad, sum_o, dproj, sum_i = made
    copy = pltpu.make_async_copy
    gets = []
    for n in range(4):
        for i in range(2):
            rows = pl.ds(i * 512, 512)
            gets.append(copy(hbm_in[n].at[rows], held[n].at[rows], in_sems.at[2 * n + i]))
    for n in range(4, 17):
        gets.append(copy(hbm_in[n], held[n], in_sems.at[n + 4]))
    puts = [copy(m, h, out_sems.at[n]) for n, (m, h) in enumerate(zip(made, hbm_out))]
    for c in gets[0:8:2] + gets[8:10] + gets[1:8:2] + gets[10:]:
        c.start()

    left[:, LEFT_E] = left_e[...].astype(BF)
    left[:, LEFT_S] = left_s[...].astype(BF)
    for i in range(2):
        for c in gets[i:8:2]:
            c.wait()
        if i == 0:
            for c in gets[8:10]:
                c.wait()
        rows = slice(i * 512, (i + 1) * 512)
        m = middle[rows, :]
        inverse = lax.rsqrt(jnp.mean(m * m, axis=1, keepdims=True) + EPS)
        unit = m * inverse
        w = grad[rows, :].astype(F32) + grad_other[rows, :].astype(F32)
        a = w * gain[...]
        back = inverse * (a - unit * jnp.mean(a * unit, axis=1, keepdims=True))
        mg = cot[rows, :].astype(F32) + back
        branch = mg.astype(BF)
        att_grad[rows, :] = nn(branch, w_out[...]).astype(BF)
        part = tn(att[rows, :], branch)
        if i == 0:
            acc[...] = part
        else:
            acc[...] += part

        @pl.when(place[3] == i)
        def _():
            middle_grad[...] = mg
            gain_sum[...] = by_eight(w * unit)

    puts[0].start()
    gets[10].wait()
    summed = (acc[...] + err_o[0]).astype(BF)
    sum_o[...] = summed
    puts[1].start()
    left[:, LEFT_O] = folded(nt(two_terms(start_o[...]), summed)).astype(BF)

    for c in gets[11:19]:
        c.wait()

    def one_pair(p, carry):
        lanes = pl.ds(pl.multiple_of(p * 128, 128), 128)
        pair_back(
            *(r.at[:, lanes] for r in (q, k, v, att, att_grad)),
            fq.at[pl.ds(2 * p, 2)],
            fk,
            cos,
            low,
            high,
            [dproj.at[:, pl.ds(pl.multiple_of(c * HALF + p * 128, 128), 128)] for c in range(3)],
            dk_acc,
            dv_acc,
        )
        return carry

    lax.fori_loop(0, 3, one_pair, 0)
    puts[2].start()

    for c in gets[19:]:
        c.wait()
    found = nn(turned[...], dproj[...])
    for c in range(3):
        summed = (found[:, c * HALF : (c + 1) * HALF] + err_i[0, c]).astype(BF)
        sum_i[c] = summed
        left[:, c * D : (c + 1) * D] = folded(nt(two_terms(start_i[c]), summed)).astype(BF)
    puts[3].start()
    for c in puts:
        c.wait()


def backward(place, gain, start_o, start_i, left_e, left_s, *arrays):
    small = (gain, start_o, start_i, left_e, left_s)
    outs = [like((512, D), F32), like((HALF, D), BF), like((SEQ, 3 * HALF), BF), like((3, D, HALF), BF)]
    return pl.pallas_call(
        backward_kernel,
        in_specs=[SMEM] + [full(a.shape) for a in small] + [HBM] * 17,
        out_specs=[HBM] * 4 + [full((8, D)), full((RANK, LEFT))],
        out_shape=outs + [like((8, D), F32), like((RANK, LEFT), BF)],
        scratch_shapes=[pltpu.VMEM(a.shape, a.dtype) for a in arrays]
        + [pltpu.VMEM(o.shape, o.dtype) for o in outs]
        + [
            pltpu.VMEM((SEQ, HALF), BF),
            pltpu.VMEM((HALF, D), F32),
            pltpu.VMEM((SEQ, 128), F32),
            pltpu.VMEM((SEQ, 128), F32),
            pltpu.SemaphoreType.DMA((21,)),
            pltpu.SemaphoreType.DMA((4,)),
        ],
        compiler_params=params(60),
        cost_estimate=cost(20 * 10**9, 30 * 2**20),
    )(place, *small, *arrays)


def first_grad_kernel(place, dproj, weights, own, send):
    for i in range(2):
        part = nt(dproj[i * 512 : (i + 1) * 512, :], weights[...])

        @pl.when(place[3] == i)
        def _():
            own[...] = part

        @pl.when(place[3] != i)
        def _():
            send[...] = part.astype(BF)


def first_grad_rows(place, dproj, weights):
    return pl.pallas_call(
        first_grad_kernel,
        grid=(1,),
        in_specs=[
            SMEM,
            full((SEQ, 3 * HALF)),
            pl.BlockSpec((D, 3 * HALF), lambda i: (0, 0)),
        ],
        out_specs=[full((512, D)), full((512, D))],
        out_shape=[like((512, D), F32), like((512, D), BF)],
        compiler_params=params(24),
        cost_estimate=cost(2 * SEQ * D * 1152, 8 * 2**20),
    )(place, dproj, weights)


def input_grad_kernel(x, gain, middle_grad, own, other, gain_second, out, gains):
    xb = x[...].astype(F32)
    inverse = lax.rsqrt(jnp.mean(xb * xb, axis=1, keepdims=True) + EPS)
    unit = xb * inverse
    w = own[...] + other[...].astype(F32)
    a = w * gain[...]
    back = inverse * (a - unit * jnp.mean(a * unit, axis=1, keepdims=True))
    out[...] = (middle_grad[...] + back).astype(BF)
    gains[:, :D] = by_eight(w * unit)
    gains[:, D:] = gain_second[...]


def input_grad_rows(x, gain, middle_grad, own, other, gain_second):
    shapes = [(512, D), (1, D), (512, D), (512, D), (512, D), (8, D)]
    return pl.pallas_call(
        input_grad_kernel,
        in_specs=[full(s) for s in shapes],
        out_specs=[full((512, D)), full((8, 2 * D))],
        out_shape=[like((512, D), BF), like((8, 2 * D), F32)],
        compiler_params=params(24),
        cost_estimate=cost(10**7, 6 * 2**20),
    )(x, gain, middle_grad, own, other, gain_second)


def orthonormal(factors):
    rest, done = list(factors), [jnp.zeros_like(f) for f in factors]
    for k in range(RANK):
        for m, f in enumerate(factors):
            row = rest[m][k : k + 1]
            row = row * lax.rsqrt(jnp.sum(row * row, axis=1, keepdims=True) + EPS)
            here = lax.broadcasted_iota(jnp.int32, f.shape, 0) == k
            done[m] = jnp.where(here, row, done[m])
            if k < RANK - 1:
                rest[m] = rest[m] - jnp.sum(f * row, axis=1, keepdims=True) * row
    return done


def joined(mine, other, t):
    return jnp.concatenate(
        [jnp.where(t == 0, mine, other), jnp.where(t == 0, other, mine)], axis=1
    )


RIGHT_E = 5 * CHUNK
RIGHT_O = RIGHT_E + 2 * FF
RIGHT_S = RIGHT_O + D
RIGHT_G = RIGHT_S + D
RIGHT = RIGHT_G + 2 * D


def factor_kernel(place, mine, other, gains, h_i, h_o, h_e, h_s, *refs):
    left_i, left_o, left_e, left_s, right = refs[:5]
    sum_i, sum_o, sum_e, sum_s, sems = refs[5:]
    pairs = ((h_i, sum_i), (h_o, sum_o), (h_e, sum_e), (h_s, sum_s))
    copies = [pltpu.make_async_copy(h, v, sems.at[n]) for n, (h, v) in enumerate(pairs)]
    for c in copies:
        c.start()
    t = place[3]
    a, b = mine[...], other[...]
    both = a + b
    factors = [both[:, c * D : (c + 1) * D] for c in range(3)]
    factors.append(joined(a[:, LEFT_O], b[:, LEFT_O], t))
    at = LEFT_E.start
    factors += [both[:, at : at + D], both[:, at + D : at + 2 * D]]
    factors.append(joined(a[:, LEFT_S], b[:, LEFT_S], t))
    found = orthonormal(factors)
    own_o = jnp.where(t == 0, found[3][:, :HALF], found[3][:, HALF:])
    own_s = jnp.where(t == 0, found[6][:, :FF], found[6][:, FF:])
    left_o[...] = own_o
    left_s[...] = own_s
    for c in range(3):
        left_i[c] = found[c]
    for c in range(2):
        left_e[c] = found[4 + c]
    right[:, RIGHT_G:] = gains[...].astype(BF)
    for c in copies:
        c.wait()
    for c in range(3):
        right[:, c * HALF : (c + 1) * HALF] = folded(nn(two_terms(found[c]), sum_i[c])).astype(BF)
    right[:, 3 * HALF : RIGHT_E] = jnp.zeros((RANK, RIGHT_E - 3 * HALF), BF)
    for c in range(2):
        at = RIGHT_E + c * FF
        right[:, at : at + FF] = folded(nn(two_terms(found[4 + c]), sum_e[c])).astype(BF)
    right[:, RIGHT_O : RIGHT_O + D] = folded(nn(two_terms(own_o), sum_o[...])).astype(BF)
    right[:, RIGHT_S : RIGHT_S + D] = folded(nn(two_terms(own_s), sum_s[...])).astype(BF)


def factors_of(place, mine, other, gains, sum_i, sum_o, sum_e, sum_s):
    sums = (sum_i, sum_o, sum_e, sum_s)
    outs = [(3, RANK, D), (RANK, HALF), (2, RANK, D), (RANK, FF)]
    return pl.pallas_call(
        factor_kernel,
        in_specs=[SMEM, full((RANK, LEFT)), full((RANK, LEFT)), full((8, 2 * D))] + [HBM] * 4,
        out_specs=[full(s) for s in outs] + [full((RANK, RIGHT))],
        out_shape=[like(s, F32) for s in outs] + [like((RANK, RIGHT), BF)],
        scratch_shapes=[pltpu.VMEM(s.shape, BF) for s in sums] + [pltpu.SemaphoreType.DMA((4,))],
        compiler_params=params(24),
        cost_estimate=cost(10**8, 10 * 2**20),
    )(place, mine, other, gains, *sums)


def left_terms(v):
    one = v.astype(BF).astype(F32)
    two = v - one
    return jnp.concatenate([one, one, two, two], axis=0).astype(BF)


def right_terms(v):
    one = v.astype(BF).astype(F32)
    two = v - one
    return jnp.concatenate([one, two, one, two], axis=0).astype(BF)


def own_rows(terms, place):
    dp = (place[0] * 4 + place[1]) * 4 + place[2]
    row = lax.broadcasted_iota(jnp.int32, (16, D), 0)
    col = lax.broadcasted_iota(jnp.int32, (16, D), 1)
    pick = jnp.where((row < SHARD) & (col == row + SHARD * dp), 1.0, 0.0).astype(BF)
    return nt(pick, terms).astype(BF)


def moved(old, weight, rate, own, momentum, updated):
    new = momentum_decay * old + own
    momentum[...] = new
    updated[...] = weight - rate * new


LAST = 3


def last_kernel(place, *refs):
    left_i, left_o, left_e, left_s, sums, other, sum_i, sum_o, sum_e, sum_s = refs[:10]
    old_i, old_o, old_e, old_s, w_i, w_o, w_e, w_s, gains, old_g = refs[10:20]
    res_i, res_o, res_e, res_s, mom_i, mom_o, mom_e, mom_s, new_i, new_o, new_e, new_s = refs[20:32]
    right_i, right_o, right_e, right_s, mom_g, new_g = refs[32:38]
    l_i, l_o, l_e, l_s, r_i, r_o, r_e, r_s = refs[38:]
    j = pl.program_id(0)
    scale = 1.0 / 64
    tail = lambda n: (sums[:, RIGHT_O + n * D : RIGHT_O + (n + 1) * D] + other[:, n * D : (n + 1) * D])
    e_rights = [sums[:, RIGHT_E + c * FF : RIGHT_E + (c + 1) * FF] for c in range(2)]
    i_rights = [sums[:, c * HALF : (c + 1) * HALF] for c in range(3)]

    @pl.when(j == 0)
    def _():
        for c in range(2):
            l_e[c * D : (c + 1) * D, :] = left_terms(left_e[c]).T
            r_e[c] = right_terms(e_rights[c] * scale)
        l_s[...] = left_terms(left_s[...]).T
        r_s[...] = right_terms(tail(1) * scale)
        for c in range(3):
            l_i[c * D : (c + 1) * D, :] = left_terms(left_i[c]).T
            r_i[c] = right_terms(i_rights[c] * scale)
        l_o[...] = left_terms(left_o[...]).T
        r_o[...] = right_terms(tail(0) * scale)

    at = lambda n: pl.ds(pl.multiple_of(j * n, n), n)
    for h in range(2):
        rows = pl.ds(pl.multiple_of(j * 512 + h * 256, 256), 256)
        which = (2 * j + h) // 3
        here = slice(h * 256, (h + 1) * 256)
        res_e[here, :] = sum_e[here, :].astype(F32) - nn(l_e[rows, :], r_e[which])
    res_s[0] = sum_s[...].astype(F32) - nn(l_s[at(512), :], r_s[...])
    res_i[0, 0] = sum_i[0].astype(F32) - nn(l_i[at(D), :], r_i[j])
    res_o[0] = sum_o[...].astype(F32) - nn(l_o[at(128), :], r_o[...])

    @pl.when(j == 1)
    def _():
        for c in range(2):
            right_e[c] = e_rights[c] * scale
            own = nn(own_rows(left_terms(left_e[c]), place), r_e[c])[:SHARD]
            moved(old_e[:, c, :], w_e[:, c, :], rate_expand, own, mom_e.at[:, c, :], new_e.at[:, c, :])
        right_s[...] = tail(1) * scale
        own = nn(own_rows(r_s[...], place), left_terms(left_s[...]))[:SHARD]
        moved(old_s[...], w_s[...], rate_shrink, own, mom_s, new_s)
        for c in range(3):
            right_i[c] = i_rights[c] * scale
            own = nn(own_rows(left_terms(left_i[c]), place), r_i[c])[:SHARD]
            moved(old_i[c], w_i[c], rate_inbound, own, mom_i.at[c], new_i.at[c])
        right_o[...] = tail(0) * scale
        own = nn(own_rows(r_o[...], place), left_terms(left_o[...]))[:SHARD]
        moved(old_o[...], w_o[...], rate_outbound, own, mom_o, new_o)
        for n in range(2):
            own = jnp.sum(tail(2 + n), axis=0, keepdims=True)
            row = slice(n, n + 1)
            moved(old_g[row], gains[row], rate_gains, own, mom_g.at[row], new_g.at[row])


def last(place, lefts, sums, other, made, old, w, gains, old_g):
    rows = lambda n, w: pl.BlockSpec((n, w), lambda j: (j, 0))
    sum_i, sum_o, sum_e, sum_s = made
    made = (sum_i, sum_o, sum_e.reshape(2 * D, FF), sum_s)
    small = [*lefts, sums, other]
    states = [*old, *w, gains, old_g]
    state_shapes = [(3, SHARD, HALF), (SHARD, HALF), (SHARD, 2, FF), (SHARD, FF)]
    rest_shapes = [(1, 3, D, HALF), (1, HALF, D), (2 * D, FF), (1, FF, D)]
    tails = [(3, RANK, HALF), (RANK, D), (2, RANK, FF), (RANK, D), (2, D), (2, D)]
    flat = state_shapes * 2 + tails
    outs = pl.pallas_call(
        last_kernel,
        grid=(LAST,),
        in_specs=[SMEM]
        + [full(a.shape) for a in small]
        + [pl.BlockSpec((1, D, HALF), lambda j: (j, 0, 0)), rows(128, D), rows(512, FF), rows(512, D)]
        + [full(a.shape) for a in states],
        out_specs=[
            pl.BlockSpec((1, 1, D, HALF), lambda j: (0, j, 0, 0)),
            pl.BlockSpec((1, 128, D), lambda j: (0, j, 0)),
            rows(512, FF),
            pl.BlockSpec((1, 512, D), lambda j: (0, j, 0)),
        ]
        + [full(s) for s in flat],
        out_shape=[like(s, F32) for s in rest_shapes + flat],
        scratch_shapes=[
            pltpu.VMEM((3 * D, 32), BF),
            pltpu.VMEM((HALF, 32), BF),
            pltpu.VMEM((2 * D, 32), BF),
            pltpu.VMEM((FF, 32), BF),
            pltpu.VMEM((3, 32, HALF), BF),
            pltpu.VMEM((32, D), BF),
            pltpu.VMEM((2, 32, FF), BF),
            pltpu.VMEM((32, D), BF),
        ],
        compiler_params=params(28),
        cost_estimate=cost(10**8, 30 * 2**20),
    )(place, *small, *made, *states)
    return (*outs[:2], outs[2].reshape(1, 2, D, FF), *outs[3:])


def lane_tables(ids):
    zeros = jnp.sum((ids == 0).astype(jnp.int32))
    ones = jnp.sum((ids == 1).astype(jnp.int32))
    before = jnp.where(ids == 0, 0, jnp.where(ids == 1, zeros, zeros + ones))
    places = (jnp.arange(SEQ, dtype=jnp.int32) - before).astype(F32)
    lane = jnp.arange(128, dtype=jnp.int32)
    inverse = rope_base ** (-((lane % 32).astype(F32) * 2.0) / HEAD_DIM)
    angles = places[:, None] * inverse[None, :]
    first = (lane % 64 < 32)[None, :]
    sine = jnp.sin(angles)
    low, high = jnp.where(first, -sine, 0.0), jnp.where(first, 0.0, sine)
    kind = lane[None, :]
    same = ids[:, None] == kind
    fq = jnp.where((kind < 3) & same, 1.0, 0.0).astype(BF)
    fk = jnp.where(kind < 3, jnp.where(same, 0.0, MASKED), jnp.where(kind < 6, 1.0, 0.0))
    return (jnp.cos(angles), low, high), fq, fk.astype(BF)


def both_halves(own, t):
    other = swap(own)
    whole = jnp.zeros((SEQ, D), BF)
    whole = lax.dynamic_update_slice_in_dim(whole, own, t * 512, 0)
    return lax.dynamic_update_slice_in_dim(whole, other, (1 - t) * 512, 0)


def local(
    tokens,
    segment_ids,
    cotangent,
    norm_gains,
    gains_moment,
    inbound,
    outbound,
    expand,
    shrink,
    inbound_moment,
    outbound_moment,
    expand_moment,
    shrink_moment,
    inbound_error,
    outbound_error,
    expand_error,
    shrink_error,
    inbound_start,
    outbound_start,
    expand_start,
    shrink_start,
):
    y, x, z, t = (lax.axis_index(a) for a in DP_TENSOR)
    place = jnp.stack([y, x, z, t]).astype(jnp.int32)

    shard = weight_shard(inbound, outbound.T, jnp.swapaxes(expand, 0, 1), shrink.T)
    shard, segment_ids, tokens, cotangent = lax.optimization_barrier(
        (shard, segment_ids, tokens, cotangent)
    )
    column = [shard, shift(shard, Z, 1), shift(shard, Z, 3), shift(shard, Z, 2)]
    tables, fq, fk = lane_tables(segment_ids)
    column, tables, fq, fk = lax.optimization_barrier((column, tables, fq, fk))
    attn_rows, feed_rows = rows_of_column(place, column)
    feed_weights = lax.all_gather(feed_rows, (Y, X)).reshape(D, 3 * FF)
    x_all = both_halves(tokens, t)
    attn_ring = pieces_of_ring(attn_rows, X)
    attn_ring, x_all = lax.optimization_barrier((attn_ring, x_all))
    attn_ring = jnp.stack(attn_ring)
    cot_all = both_halves(cotangent, t)
    near = shift(attn_ring, Y, 1), shift(attn_ring, Y, 3)
    far = shift(near[0][..., :D], Y, 1), shift(near[1][..., D:], Y, 3)
    far, cot_all = lax.optimization_barrier((far, cot_all))
    in_pieces = [attn_ring, *near, *far]

    gain_one, gain_two = norm_gains[0:1], norm_gains[1:2]
    normed, weights, q, k, v, att, fq_all, w_out = attention(
        place, gain_one, x_all, tables, fq, fk, in_pieces
    )
    w_other, att_other = swap(w_out), swap(att)

    start_e, start_s = jnp.swapaxes(expand_start, 1, 2), shrink_start.T
    sum_e, sum_s, left_e, left_s, middle, grad, hid = feed(
        place,
        gain_two,
        x_all,
        att,
        att_other,
        w_out,
        w_other,
        cot_all,
        expand_error,
        shrink_error,
        feed_weights,
        start_e,
        start_s,
    )
    grad_other = swap(grad)
    middle_grad, sum_o, dproj, sum_i, gain_second, left = backward(
        place,
        gain_two,
        outbound_start.T,
        jnp.swapaxes(inbound_start, 1, 2),
        left_e,
        left_s,
        grad,
        grad_other,
        middle,
        cot_all,
        att,
        w_out,
        outbound_error,
        q,
        k,
        v,
        fq_all,
        fk,
        *tables,
        normed,
        inbound_error,
    )

    left, dproj = lax.optimization_barrier((left, dproj))
    terms = ring_terms(left, Z)
    first_own, first_send = first_grad_rows(place, dproj, weights)
    terms, first_own, first_send = lax.optimization_barrier((terms, first_own, first_send))
    terms = ring_terms(rounded(ring_sum(terms)), X)
    first_other = swap(first_send)
    terms, first_other = lax.optimization_barrier((terms, first_other))
    terms = ring_terms(rounded(ring_sum(terms)), Y)
    input_grad, gains = input_grad_rows(
        tokens, gain_one, middle_grad, first_own, first_other, gain_second
    )
    terms, gains = lax.optimization_barrier((terms, gains))
    mine = ring_sum(terms)
    left_i, left_o, left_e, left_s, right = factors_of(
        place, mine, swap(mine), gains, sum_i, sum_o, sum_e, sum_s
    )

    right, hid = lax.optimization_barrier((right, hid))
    terms = ring_terms(right, Z)
    own_out, send_out = down_rows(place, hid, feed_weights)
    terms, own_out, send_out = lax.optimization_barrier((terms, own_out, send_out))
    terms = ring_terms(rounded(ring_sum(terms)), X)
    send_out = swap(send_out)
    terms, send_out = lax.optimization_barrier((terms, send_out))
    terms = ring_terms(rounded(ring_sum(terms)), Y)
    own_middle = lax.dynamic_slice_in_dim(middle, t * 512, 512, 0)
    layer_output = (own_middle + (own_out + send_out.astype(F32))).astype(BF)
    terms, layer_output = lax.optimization_barrier((terms, layer_output))
    sums = ring_sum(terms)
    (
        res_i,
        res_o,
        res_e,
        res_s,
        inbound_momentum,
        outbound_momentum,
        expand_momentum,
        shrink_momentum,
        inbound_updated,
        outbound_updated,
        expand_updated,
        shrink_updated,
        right_i,
        right_o,
        right_e,
        right_s,
        gains_momentum,
        gains_updated,
    ) = last(
        place,
        (left_i, left_o, left_e, left_s),
        sums,
        swap(sums[:, RIGHT_O:]),
        (sum_i, sum_o, sum_e, sum_s),
        (inbound_moment, outbound_moment.T, jnp.swapaxes(expand_moment, 0, 1), shrink_moment.T),
        (inbound, outbound.T, jnp.swapaxes(expand, 0, 1), shrink.T),
        norm_gains,
        gains_moment,
    )
    return (
        layer_output,
        input_grad,
        gains_momentum,
        gains_updated,
        inbound_momentum,
        outbound_momentum.T,
        jnp.swapaxes(expand_momentum, 0, 1),
        shrink_momentum.T,
        inbound_updated,
        outbound_updated.T,
        jnp.swapaxes(expand_updated, 0, 1),
        shrink_updated.T,
        res_i,
        res_o,
        res_e,
        res_s,
        jnp.swapaxes(left_i, 1, 2),
        jnp.swapaxes(right_i, 1, 2),
        left_o.T,
        right_o.T,
        jnp.swapaxes(left_e, 1, 2),
        jnp.swapaxes(right_e, 1, 2),
        left_s.T,
        right_s.T,
    )


def solution(mesh):
    torus = Mesh(mesh.devices.reshape(4, 4, 4, mesh.shape["tensor"]), DP_TENSOR)
    return jax.shard_map(
        local,
        mesh=torus,
        in_specs=(
            P(DP_TENSOR, None),
            P(DP),
            P(DP_TENSOR, None),
            P(),
            P(),
            P(None, DP, T),
            P(T, DP),
            P(None, DP, T),
            P(T, DP),
            P(None, DP, T),
            P(T, DP),
            P(None, DP, T),
            P(T, DP),
            P(DP, None, None, T),
            P(DP, T, None),
            P(DP, None, None, T),
            P(DP, T, None),
            P(None, T, None),
            P(),
            P(None, T, None),
            P(),
        ),
        out_specs=(
            P(DP_TENSOR, None),
            P(DP_TENSOR, None),
            P(),
            P(),
            P(None, DP, T),
            P(T, DP),
            P(None, DP, T),
            P(T, DP),
            P(None, DP, T),
            P(T, DP),
            P(None, DP, T),
            P(T, DP),
            P(DP, None, None, T),
            P(DP, T, None),
            P(DP, None, None, T),
            P(DP, T, None),
            P(),
            P(None, T, None),
            P(T, None),
            P(),
            P(),
            P(None, T, None),
            P(T, None),
            P(),
        ),
        check_vma=False,
    )
```

```python
import jax
import jax.numpy as jnp
from jax import lax
from jax.experimental import pallas as pl
from jax.experimental.pallas import tpu as pltpu
from jax.sharding import Mesh
from jax.sharding import PartitionSpec as P

Y, X, Z, T = "dp_0", "dp_1", "dp_2", "tensor"
DP = (Y, X, Z)
DP_TENSOR = (Y, X, Z, T)
F32, BF = jnp.float32, jnp.bfloat16

SEQ = 1024
D = 768
HEAD_DIM = 64
HALF = 384
FF = 1536
RANK = 8
BLOCK = 256
SHARD = 12
CHUNK = 256
CHUNKS = FF // CHUNK
WIDE = 512
WIDES = FF // WIDE
EPS = 1e-06
MASKED = -1e30

momentum_decay = 0.9
rate_inbound = 0.2
rate_outbound = 6.0
rate_expand = 0.3
rate_shrink = 0.25
rate_gains = 0.0005
rope_base = 10000.0

ANY = pl.BlockSpec(memory_space=pl.ANY)
HBM = pl.BlockSpec(memory_space=pltpu.HBM)
SMEM = pl.BlockSpec(memory_space=pltpu.SMEM)


def nn(a, b):
    return jnp.dot(a, b, preferred_element_type=F32)


def nt(a, b):
    return lax.dot_general(a, b, (((1,), (1,)), ((), ())), preferred_element_type=F32)


def tn(a, b):
    return lax.dot_general(a, b, (((0,), (0,)), ((), ())), preferred_element_type=F32)


def params(mib=56):
    return pltpu.CompilerParams(vmem_limit_bytes=mib * 2**20)


def cost(flops, moved):
    return pl.CostEstimate(flops=flops // 64, bytes_accessed=moved // 64, transcendentals=0)


def full(shape):
    return pl.BlockSpec(shape, lambda *_: (0,) * len(shape))


def like(shape, dtype):
    return jax.ShapeDtypeStruct(shape, dtype)


def shift(v, axis, d):
    n = lax.axis_size(axis)
    return lax.ppermute(v, axis, [(i, (i + d) % n) for i in range(n)])


def swap(v):
    return lax.ppermute(v, T, [(0, 1), (1, 0)])


def rounded(v):
    return lax.reduce_precision(v, exponent_bits=8, mantissa_bits=7)


def ring_terms(v, axis):
    low = v.astype(BF)
    return v, shift(low, axis, 2), shift(low, axis, 1), shift(low, axis, 3)


def ring_sum(terms):
    own, two, one, back = (v.astype(F32) for v in terms)
    return (own + two) + (one + back)


def shard_kernel(inbound, outbound, expand, shrink, out):
    for c in range(3):
        out[:, c * HALF : (c + 1) * HALF] = inbound[c].astype(BF)
    out[:, 1152:1536] = outbound[...].astype(BF)
    for j in range(WIDES):
        for c in range(2):
            at = 1536 + (2 * j + c) * WIDE
            out[:, at : at + WIDE] = expand[:, c, j * WIDE : (j + 1) * WIDE].astype(BF)
    out[:, 4608:] = shrink[...].astype(BF)


def weight_shard(inbound, outbound, expand, shrink):
    return pl.pallas_call(
        shard_kernel,
        out_shape=like((SHARD, 6144), BF),
        compiler_params=params(),
        cost_estimate=cost(10**5, 2**19),
    )(inbound, outbound, expand, shrink)


def column_kernel(place, own, one, back, two, quarter, feed, rows):
    z = place[2]
    pieces = [r[...].astype(F32) for r in (own, one, two, back)]
    for p in range(4):
        away = lax.rem(p + 4 - z, 4)
        piece = jnp.where(
            away == 0,
            pieces[0],
            jnp.where(away == 3, pieces[1], jnp.where(away == 2, pieces[2], pieces[3])),
        )
        rows[p * SHARD : (p + 1) * SHARD, :] = piece
    quarter[...] = rows[:, pl.ds(pl.multiple_of(z * HALF, 128), HALF)].astype(BF)
    feed[...] = rows[:, 1536:].astype(BF)


def rows_of_column(place, pieces):
    widths = (HALF, 3 * FF)
    return pl.pallas_call(
        column_kernel,
        in_specs=[SMEM] + [full(pieces[0].shape)] * 4,
        out_specs=[full((48, w)) for w in widths],
        out_shape=[like((48, w), BF) for w in widths],
        scratch_shapes=[pltpu.VMEM((48, 6144), F32)],
        compiler_params=params(),
        cost_estimate=cost(10**6, 2**21),
    )(place, *pieces)


def rows_of_plane(v):
    everyone = jnp.broadcast_to(v[None], (16, *v.shape))
    rows = lax.all_to_all(everyone, (Y, X), 0, 0, tiled=True)
    return rows.reshape(16 * v.shape[0], v.shape[1])


def place_pieces(pieces, target, sems, place):
    copies = []
    spots = ((0, 0), (3, 0), (1, 0), (2, 0), (2, HALF))
    for n, (piece, (away, row)) in enumerate(zip(pieces, spots)):
        at = pl.multiple_of(lax.rem(place[2] + away, 4) * HALF, 128)
        spot = target.at[pl.ds(row, piece.shape[0]), pl.ds(at, HALF)]
        copies.append(pltpu.make_async_copy(piece, spot, sems.at[n]))
    return copies


def turn_lanes(v, cos, low, high):
    return v * cos + pltpu.roll(v, 96, 1) * low + pltpu.roll(v, 32, 1) * high


def head_lanes(rows, h):
    lane = lax.broadcasted_iota(jnp.int32, (rows, 128), 1)
    return (lane < 64) if h == 0 else (lane >= 64)


def three_terms(v):
    one = v.astype(BF).astype(F32)
    two = (v - one).astype(BF).astype(F32)
    return one, two, v - one - two


def both_heads(v):
    zero = jnp.zeros((), BF)
    return [jnp.where(head_lanes(v.shape[0], h), v, zero) for h in range(2)]


def pair_forward(q, k, v, fq, fk, out, fq_out):
    keys = jnp.concatenate([k[...], fk[...]], axis=1)
    vals = v[...]
    lane = lax.broadcasted_iota(jnp.int32, (256, 128), 1)
    first = head_lanes(256, 0)
    scores = []
    for b in range(4):
        rows = slice(b * 256, (b + 1) * 256)
        f = fq[rows, :]
        heads = [jnp.concatenate([m, f], axis=1) for m in both_heads(q[rows, :])]
        scores.append(nt(jnp.concatenate(heads, axis=0), keys[: (b + 1) * 256]))
    for b in range(4):
        rows = slice(b * 256, (b + 1) * 256)
        s = scores[b]
        largest = jnp.max(s, axis=1, keepdims=True)
        e = jnp.exp(s - largest)
        sums = jnp.sum(e, axis=1, keepdims=True)
        o = nn(e.astype(BF), vals[: (b + 1) * 256]) * (1.0 / sums)
        out[rows, :] = jnp.where(first, o[:256], o[256:]).astype(BF)
        one, two, three = three_terms(-(largest + jnp.log(sums)))
        for h in range(2):
            at = slice(h * 256, (h + 1) * 256)
            extra = jnp.where(lane == 3, one[at], jnp.where(lane == 4, two[at], three[at]))
            fq_out[h, rows, :] = jnp.where((lane >= 3) & (lane < 6), extra.astype(BF), fq[rows, :])


def attention_kernel(place, gain, *refs):
    hbm_in, pieces, hbm_out, refs = refs[:6], refs[6:11], refs[11:19], refs[19:]
    held, made, refs = refs[:6], refs[6:13], refs[13:]
    piece_sems, in_sems, out_sems, pair_sems = refs
    x, cos, low, high, fq, fk = held
    normed, weights, q, k, v, att, fq_all = made
    copy = pltpu.make_async_copy
    gets = [copy(hbm_in[0].at[pl.ds(i * 512, 512)], x.at[pl.ds(i * 512, 512)], in_sems.at[i]) for i in range(2)]
    gets += [copy(h, r, in_sems.at[n + 2]) for n, (h, r) in enumerate(zip(hbm_in[1:], held[1:]))]
    puts = [copy(r, h, out_sems.at[n]) for n, (r, h) in enumerate(zip(made[:5], hbm_out))]
    put_out = copy(weights.at[:, pl.ds(3 * HALF, HALF)], hbm_out[7], out_sems.at[7])

    def put_pair(p):
        lanes = pl.ds(pl.multiple_of(p * 128, 128), 128)
        heads = pl.ds(2 * p, 2)
        return (
            copy(att.at[:, lanes], hbm_out[5].at[:, lanes], pair_sems.at[0, p]),
            copy(fq_all.at[heads], hbm_out[6].at[heads], pair_sems.at[1, p]),
        )

    placed = place_pieces(pieces, weights, piece_sems, place)
    for c in gets[:2] + placed + gets[2:]:
        c.start()
    for i in range(2):
        rows = slice(i * 512, (i + 1) * 512)
        gets[i].wait()
        xb = x[rows, :].astype(F32)
        inverse = lax.rsqrt(jnp.mean(xb * xb, axis=1, keepdims=True) + EPS)
        n = (xb * inverse * gain[...]).astype(BF)
        x[rows, :] = n
        normed[:, rows] = n.T
    puts[0].start()
    for c in placed:
        c.wait()
    puts[1].start()
    put_out.start()
    for c in gets[2:]:
        c.wait()
    for i in range(2):
        rows = slice(i * 512, (i + 1) * 512)
        found = nn(x[rows, :], weights[:, :1152])
        tables = cos[rows, :], low[rows, :], high[rows, :]
        v[rows, :] = found[:, 768:].astype(BF)
        for p in range(3):
            at = slice(p * 128, (p + 1) * 128)
            q[rows, at] = (turn_lanes(found[:, at], *tables) * 0.125).astype(BF)
            k_lanes = found[:, HALF + p * 128 : HALF + (p + 1) * 128]
            k[rows, at] = turn_lanes(k_lanes, *tables).astype(BF)
    for c in puts[2:5]:
        c.start()

    def one_pair(p, carry):
        lanes = pl.ds(pl.multiple_of(p * 128, 128), 128)
        views = [r.at[:, lanes] for r in (q, k, v)]
        pair_forward(*views, fq, fk, att.at[:, lanes], fq_all.at[pl.ds(2 * p, 2)])
        for c in put_pair(p):
            c.start()
        return carry

    lax.fori_loop(0, 3, one_pair, 0)
    put_out.wait()
    for c in puts[:5]:
        c.wait()
    for p in range(3):
        for c in put_pair(p):
            c.wait()


def attention(place, gain, x, tables, fq, fk, pieces):
    arrays = (x, *tables, fq, fk)
    half = like((SEQ, HALF), BF)
    outs = [like((D, SEQ), BF), like((D, 2 * D), BF), half, half, half, half, like((6, SEQ, 128), BF)]
    return pl.pallas_call(
        attention_kernel,
        in_specs=[SMEM, full((1, D))] + [HBM] * 11,
        out_specs=[HBM] * 8,
        out_shape=[*outs, like((D, HALF), BF)],
        scratch_shapes=[pltpu.VMEM(a.shape, a.dtype) for a in arrays]
        + [pltpu.VMEM(o.shape, o.dtype) for o in outs]
        + [
            pltpu.SemaphoreType.DMA((5,)),
            pltpu.SemaphoreType.DMA((7,)),
            pltpu.SemaphoreType.DMA((8,)),
            pltpu.SemaphoreType.DMA((2, 3)),
        ],
        compiler_params=params(),
        cost_estimate=cost(10**10, 12 * 2**20),
    )(place, gain, *arrays, *pieces)


def two_terms(v):
    one = v.astype(BF).astype(F32)
    return jnp.concatenate([one, v - one], axis=0).astype(BF)


def folded(v):
    return v[0:8] + v[8:16]


def feed_kernel(place, gain, *refs):
    h_x, h_att, h_other, h_w, h_w_other, h_cot, h_err_e, h_err_s, h_feed = refs[:9]
    start_e, start_s, sum_e, sum_s, left_e, left_s = refs[9:15]
    h_middle, h_grad, h_hid = refs[15:18]
    x, att, other, w_out, w_other, cot, both, down, err_e, err_s = refs[18:28]
    middle, second, turned, hid, grads, grad_low = refs[28:34]
    rows_sem, in_sem, both_sem, down_sem, err_sem, out_sem = refs[34:]
    j = pl.program_id(0)
    copy = pltpu.make_async_copy

    def lanes(n, width, start=0):
        return pl.ds(pl.multiple_of(start + n * width, width), width)

    def get_rows(i):
        rows = pl.ds(i * 512, 512)
        trio = ((h_x, x), (h_att, att), (h_other, other))
        return [copy(h.at[rows], r.at[rows], rows_sem.at[n, i]) for n, (h, r) in enumerate(trio)]

    def get_both(n):
        at = lanes(n, 2 * WIDE)
        return copy(h_feed.at[:, at], both.at[:, at], both_sem.at[n])

    def get_down(n):
        return copy(h_feed.at[:, lanes(n, WIDE, 2 * FF)], down.at[:, lanes(n, WIDE)], down_sem.at[n])

    def get_err(n):
        slot = lax.rem(n, 2)
        return (
            copy(h_err_e.at[0, :, :, lanes(n, WIDE)], err_e.at[slot], err_sem.at[0, slot]),
            copy(h_err_s.at[0, lanes(n, WIDE)], err_s.at[slot], err_sem.at[1, slot]),
        )

    get_w = copy(h_w, w_out, in_sem.at[0])
    get_w_other = copy(h_w_other, w_other, in_sem.at[1])
    get_cot = copy(h_cot, cot, in_sem.at[2])
    put_middle = copy(middle, h_middle, out_sem.at[0])
    put_grad = copy(grad_low, h_grad, out_sem.at[1])
    put_hid = copy(hid, h_hid, out_sem.at[2])

    @pl.when(j == 0)
    def _():
        order = [get_w, get_w_other, *get_rows(0), *get_rows(1), get_both(0), get_cot, get_down(0)]
        for c in order + [*get_err(0)]:
            c.start()
        for n in range(1, WIDES):
            get_both(n).start()
            get_down(n).start()
            if n == 1:
                for c in get_err(n):
                    c.start()
        left_e[...] = jnp.zeros_like(left_e)
        get_w.wait()
        get_w_other.wait()
        for i in range(2):
            rows = slice(i * 512, (i + 1) * 512)
            for c in get_rows(i):
                c.wait()
            m = x[rows, :].astype(F32) + nt(att[rows, :], w_out[...]) + nt(other[rows, :], w_other[...])
            middle[rows, :] = m
            inverse = lax.rsqrt(jnp.mean(m * m, axis=1, keepdims=True) + EPS)
            low = (m * inverse * gain[...]).astype(BF)
            second[rows, :] = low
            turned[:, rows] = low.T
        put_middle.start()

    get_both(j).wait()
    w_both = both.at[:, lanes(j, 2 * WIDE)]
    w_down = down.at[:, lanes(j, WIDE)]
    my_hid = hid.at[:, lanes(j, WIDE)]
    my_grads = grads.at[:, lanes(j, 2 * WIDE)]
    step = FEED_ROWS
    found = []
    for b in range(SEQ // step):
        found.append(nn(second[b * step : (b + 1) * step, :], w_both[...]))

    @pl.when(j == 0)
    def _():
        get_cot.wait()

    get_down(j).wait()
    for b in range(SEQ // step):
        rows = slice(b * step, (b + 1) * step)
        gu, hg = found[b], nn(cot[rows, :], w_down[...])
        g, u = gu[:, :WIDE], gu[:, WIDE:]
        sig = 0.5 * jnp.tanh(0.5 * g) + 0.5
        act = g * sig
        my_hid[rows, :] = (act * u).astype(BF)
        my_grads[rows, :WIDE] = (hg * u * (sig + act * (1.0 - sig))).astype(BF)
        my_grads[rows, WIDE:] = (hg * act).astype(BF)

    @pl.when(j == WIDES - 1)
    def _():
        put_hid.start()
        grad_low[...] = nt(grads[...], both[...]).astype(BF)
        put_grad.start()

    for c in get_err(j):
        c.wait()
    slot = lax.rem(j, 2)
    low = (tn(my_hid[...], cot[...]) + err_s[slot]).astype(BF)
    sum_s[...] = low
    left_s[...] = folded(nt(two_terms(start_s[...]), low))
    made = nn(turned[...], my_grads[...])
    for c in range(2):
        low = (made[:, c * WIDE : (c + 1) * WIDE] + err_e[slot, c]).astype(BF)
        sum_e[c] = low
        left_e[:, c * D : (c + 1) * D] += folded(nt(two_terms(start_e[c]), low))

    @pl.when(j + 2 < WIDES)
    def _():
        for c in get_err(j + 2):
            c.start()

    @pl.when(j == WIDES - 1)
    def _():
        put_middle.wait()
        put_hid.wait()
        put_grad.wait()


FEED_ROWS = 256
FEED_MIB = 56


def feed(place, gain, x, att, other, weights, w_other, cot, err_e, err_s, feed_weights, start_e, start_s):
    arrays = (x, att, other, weights, w_other, cot, err_e, err_s, feed_weights)
    return pl.pallas_call(
        feed_kernel,
        grid=(WIDES,),
        in_specs=[SMEM, full((1, D)), HBM, HBM, ANY, HBM, ANY]
        + [HBM] * 4
        + [pl.BlockSpec((2, RANK, WIDE), lambda j: (0, 0, j)), full((RANK, D))],
        out_specs=[
            pl.BlockSpec((2, D, WIDE), lambda j: (0, 0, j)),
            pl.BlockSpec((WIDE, D), lambda j: (j, 0)),
            full((RANK, 2 * D)),
            pl.BlockSpec((RANK, WIDE), lambda j: (0, j)),
            HBM,
            HBM,
            HBM,
        ],
        out_shape=[
            like((2, D, FF), BF),
            like((FF, D), BF),
            like((RANK, 2 * D), F32),
            like((RANK, FF), F32),
            like((SEQ, D), F32),
            like((SEQ, D), BF),
            like((SEQ, FF), BF),
        ],
        scratch_shapes=[
            pltpu.VMEM((SEQ, D), BF),
            pltpu.VMEM((SEQ, HALF), BF),
            pltpu.VMEM((SEQ, HALF), BF),
            pltpu.VMEM((D, HALF), BF),
            pltpu.VMEM((D, HALF), BF),
            pltpu.VMEM((SEQ, D), BF),
            pltpu.VMEM((D, 2 * FF), BF),
            pltpu.VMEM((D, FF), BF),
            pltpu.VMEM((2, 2, D, WIDE), F32),
            pltpu.VMEM((2, WIDE, D), F32),
            pltpu.VMEM((SEQ, D), F32),
            pltpu.VMEM((SEQ, D), BF),
            pltpu.VMEM((D, SEQ), BF),
            pltpu.VMEM((SEQ, FF), BF),
            pltpu.VMEM((SEQ, 2 * FF), BF),
            pltpu.VMEM((SEQ, D), BF),
            pltpu.SemaphoreType.DMA((3, 2)),
            pltpu.SemaphoreType.DMA((3,)),
            pltpu.SemaphoreType.DMA((WIDES,)),
            pltpu.SemaphoreType.DMA((WIDES,)),
            pltpu.SemaphoreType.DMA((2, 2)),
            pltpu.SemaphoreType.DMA((3,)),
        ],
        compiler_params=params(FEED_MIB),
        cost_estimate=cost(18 * SEQ * D * FF, 40 * 2**20),
    )(place, gain, *arrays, start_e, start_s)


def down_kernel(place, hid, weights, own, send):
    t = place[3]
    for i in range(2):
        part = nt(hid[i * 512 : (i + 1) * 512, :], weights[...])

        @pl.when(t == i)
        def _():
            own[...] = part

        @pl.when(t != i)
        def _():
            send[...] = part.astype(BF)


def down_rows(place, hid, weights):
    return pl.pallas_call(
        down_kernel,
        grid=(1,),
        in_specs=[SMEM, full((SEQ, FF)), pl.BlockSpec((D, FF), lambda j: (0, 2))],
        out_specs=[full((512, D)), full((512, D))],
        out_shape=[like((512, D), F32), like((512, D), BF)],
        compiler_params=params(24),
        cost_estimate=cost(2 * SEQ * D * FF, 8 * 2**20),
    )(place, hid, weights)


def by_eight(v):
    return jnp.sum(v.reshape(-1, 8, v.shape[1]), axis=0)


LEFT_O = slice(3 * D, 3 * D + HALF)
LEFT_E = slice(3 * D + HALF, 5 * D + HALF)
LEFT_S = slice(5 * D + HALF, 5 * D + HALF + FF)
LEFT = 5 * D + HALF + FF


def pair_back(q, k, v, att, grad, fq, fk, cos, low, high, out, dk_acc, dv_acc):
    lane = lax.broadcasted_iota(jnp.int32, (256, 128), 1)
    ones = jnp.where(lax.broadcasted_iota(jnp.int32, (SEQ, 128), 1) < 3, 1.0, 0.0).astype(BF)
    keys = jnp.concatenate([k[...], fk[...]], axis=1)
    vals = jnp.concatenate([v[...], ones], axis=1)
    kt = k[...].T
    dk_acc[...] = jnp.zeros_like(dk_acc)
    dv_acc[...] = jnp.zeros_like(dv_acc)
    for b in range(4):
        rows = slice(b * 256, (b + 1) * 256)
        count = (b + 1) * 256
        qs, gs = both_heads(q[rows, :]), both_heads(grad[rows, :])
        q_rows = [jnp.concatenate([qs[h], fq[h, rows, :]], axis=1) for h in range(2)]
        g_rows = []
        for h in range(2):
            centre = jnp.sum(gs[h].astype(F32) * att[rows, :].astype(F32), axis=1, keepdims=True)
            one, two, three = three_terms(-centre)
            extra = jnp.where(lane == 0, one, jnp.where(lane == 1, two, three))
            fg = jnp.where(lane < 3, extra, 0.0).astype(BF)
            g_rows.append(jnp.concatenate([gs[h], fg], axis=1))
        soft = jnp.exp(nt(keys[:count], jnp.concatenate(q_rows, axis=0)))
        ds = (soft * nt(vals[:count], jnp.concatenate(g_rows, axis=0))).astype(BF)
        dv_acc[:count, :] += nn(soft.astype(BF), jnp.concatenate(gs, axis=0))
        dk_acc[:count, :] += nn(ds, jnp.concatenate(qs, axis=0))
        part = nn(kt[:, :count], ds)
        dq = jnp.concatenate([part[:64, :256], part[64:, 256:]], axis=0).T * 0.125
        out[0][rows, :] = turn_lanes(dq, cos[rows, :], -low[rows, :], -high[rows, :]).astype(BF)
    out[1][...] = turn_lanes(dk_acc[...], cos[...], -low[...], -high[...]).astype(BF)
    out[2][...] = dv_acc[...].astype(BF)


def backward_kernel(place, gain, start_o, start_i, grad_other, *refs):
    hbm_in, hbm_out, refs = refs[:18], refs[18:22], refs[22:]
    gain_sum, left = refs[:2]
    held, made, refs = refs[2:20], refs[20:24], refs[24:]
    att_grad, acc, dk_acc, dv_acc, in_sems, out_sems = refs
    grad, middle, cot, att, w_out, err_o, q, k, v, fq, fk, cos, low, high, turned, err_i, left_e, left_s = held
    middle_grad, sum_o, dproj, sum_i = made
    copy = pltpu.make_async_copy
    gets = []
    for n in range(3):
        for i in range(2):
            rows = pl.ds(i * 512, 512)
            gets.append(copy(hbm_in[n].at[rows], held[n].at[rows], in_sems.at[2 * n + i]))
    for n in range(3, 18):
        gets.append(copy(hbm_in[n], held[n], in_sems.at[n + 3]))
    puts = [copy(m, h, out_sems.at[n]) for n, (m, h) in enumerate(zip(made, hbm_out))]
    for c in gets[0:6:2] + gets[6:8] + gets[1:6:2] + gets[8:]:
        c.start()

    for i in range(2):
        for c in gets[i:6:2]:
            c.wait()
        if i == 0:
            for c in gets[6:8]:
                c.wait()
        rows = slice(i * 512, (i + 1) * 512)
        m = middle[rows, :]
        inverse = lax.rsqrt(jnp.mean(m * m, axis=1, keepdims=True) + EPS)
        unit = m * inverse
        w = grad[rows, :].astype(F32) + grad_other[rows, :].astype(F32)
        a = w * gain[...]
        back = inverse * (a - unit * jnp.mean(a * unit, axis=1, keepdims=True))
        mg = cot[rows, :].astype(F32) + back
        branch = mg.astype(BF)
        att_grad[rows, :] = nn(branch, w_out[...]).astype(BF)
        part = tn(att[rows, :], branch)
        if i == 0:
            acc[...] = part
        else:
            acc[...] += part

        @pl.when(place[3] == i)
        def _():
            middle_grad[...] = mg
            gain_sum[...] = by_eight(w * unit)

    puts[0].start()
    gets[8].wait()
    summed = (acc[...] + err_o[0]).astype(BF)
    sum_o[...] = summed
    puts[1].start()
    left[:, LEFT_O] = folded(nt(two_terms(start_o[...]), summed)).astype(BF)

    for c in gets[9:17]:
        c.wait()

    def one_pair(p, carry):
        lanes = pl.ds(pl.multiple_of(p * 128, 128), 128)
        pair_back(
            *(r.at[:, lanes] for r in (q, k, v, att, att_grad)),
            fq.at[pl.ds(2 * p, 2)],
            fk,
            cos,
            low,
            high,
            [dproj.at[:, pl.ds(pl.multiple_of(c * HALF + p * 128, 128), 128)] for c in range(3)],
            dk_acc,
            dv_acc,
        )
        return carry

    lax.fori_loop(0, 3, one_pair, 0)
    puts[2].start()

    for c in gets[17:]:
        c.wait()
    left[:, LEFT_E] = left_e[...].astype(BF)
    left[:, LEFT_S] = left_s[...].astype(BF)
    found = nn(turned[...], dproj[...])
    for c in range(3):
        summed = (found[:, c * HALF : (c + 1) * HALF] + err_i[0, c]).astype(BF)
        sum_i[c] = summed
        left[:, c * D : (c + 1) * D] = folded(nt(two_terms(start_i[c]), summed)).astype(BF)
    puts[3].start()
    for c in puts:
        c.wait()


BACK_MIB = 60


def backward(place, gain, start_o, start_i, grad_other, *arrays):
    small = (gain, start_o, start_i, grad_other)
    outs = [like((512, D), F32), like((HALF, D), BF), like((SEQ, 3 * HALF), BF), like((3, D, HALF), BF)]
    return pl.pallas_call(
        backward_kernel,
        in_specs=[SMEM] + [full(a.shape) for a in small] + [HBM] * 18,
        out_specs=[HBM] * 4 + [full((8, D)), full((RANK, LEFT))],
        out_shape=outs + [like((8, D), F32), like((RANK, LEFT), BF)],
        scratch_shapes=[pltpu.VMEM(a.shape, a.dtype) for a in arrays]
        + [pltpu.VMEM(o.shape, o.dtype) for o in outs]
        + [
            pltpu.VMEM((SEQ, HALF), BF),
            pltpu.VMEM((HALF, D), F32),
            pltpu.VMEM((SEQ, 128), F32),
            pltpu.VMEM((SEQ, 128), F32),
            pltpu.SemaphoreType.DMA((21,)),
            pltpu.SemaphoreType.DMA((4,)),
        ],
        compiler_params=params(BACK_MIB),
        cost_estimate=cost(20 * 10**9, 30 * 2**20),
    )(place, *small, *arrays)


def first_grad_kernel(place, dproj, weights, own, send):
    for i in range(2):
        part = nt(dproj[i * 512 : (i + 1) * 512, :], weights[...])

        @pl.when(place[3] == i)
        def _():
            own[...] = part

        @pl.when(place[3] != i)
        def _():
            send[...] = part.astype(BF)


def first_grad_rows(place, dproj, weights):
    return pl.pallas_call(
        first_grad_kernel,
        grid=(1,),
        in_specs=[
            SMEM,
            full((SEQ, 3 * HALF)),
            pl.BlockSpec((D, 3 * HALF), lambda i: (0, 0)),
        ],
        out_specs=[full((512, D)), full((512, D))],
        out_shape=[like((512, D), F32), like((512, D), BF)],
        compiler_params=params(24),
        cost_estimate=cost(2 * SEQ * D * 1152, 8 * 2**20),
    )(place, dproj, weights)


def input_grad_kernel(x, gain, middle_grad, own, other, gain_second, out, gains):
    xb = x[...].astype(F32)
    inverse = lax.rsqrt(jnp.mean(xb * xb, axis=1, keepdims=True) + EPS)
    unit = xb * inverse
    w = own[...] + other[...].astype(F32)
    a = w * gain[...]
    back = inverse * (a - unit * jnp.mean(a * unit, axis=1, keepdims=True))
    out[...] = (middle_grad[...] + back).astype(BF)
    gains[:, :D] = by_eight(w * unit)
    gains[:, D:] = gain_second[...]


def input_grad_rows(x, gain, middle_grad, own, other, gain_second):
    shapes = [(512, D), (1, D), (512, D), (512, D), (512, D), (8, D)]
    return pl.pallas_call(
        input_grad_kernel,
        in_specs=[full(s) for s in shapes],
        out_specs=[full((512, D)), full((8, 2 * D))],
        out_shape=[like((512, D), BF), like((8, 2 * D), F32)],
        compiler_params=params(24),
        cost_estimate=cost(10**7, 6 * 2**20),
    )(x, gain, middle_grad, own, other, gain_second)


def orthonormal(factors):
    rest, done = list(factors), [jnp.zeros_like(f) for f in factors]
    for k in range(RANK):
        for m, f in enumerate(factors):
            row = rest[m][k : k + 1]
            row = row * lax.rsqrt(jnp.sum(row * row, axis=1, keepdims=True) + EPS)
            here = lax.broadcasted_iota(jnp.int32, f.shape, 0) == k
            done[m] = jnp.where(here, row, done[m])
            if k < RANK - 1:
                rest[m] = rest[m] - jnp.sum(f * row, axis=1, keepdims=True) * row
    return done


def joined(mine, other, t):
    return jnp.concatenate(
        [jnp.where(t == 0, mine, other), jnp.where(t == 0, other, mine)], axis=1
    )


RIGHT_E = 5 * CHUNK
RIGHT_O = RIGHT_E + 2 * FF
RIGHT_S = RIGHT_O + D
RIGHT_G = RIGHT_S + D
RIGHT = RIGHT_G + 2 * D


def factor_kernel(place, mine, other, gains, h_i, h_o, h_e, h_s, *refs):
    left_i, left_o, left_e, left_s, right = refs[:5]
    sum_i, sum_o, sum_e, sum_s, sems = refs[5:]
    pairs = ((h_i, sum_i), (h_o, sum_o), (h_e, sum_e), (h_s, sum_s))
    copies = [pltpu.make_async_copy(h, v, sems.at[n]) for n, (h, v) in enumerate(pairs)]
    for c in copies:
        c.start()
    t = place[3]
    a, b = mine[...], other[...]
    both = a + b
    factors = [both[:, c * D : (c + 1) * D] for c in range(3)]
    factors.append(joined(a[:, LEFT_O], b[:, LEFT_O], t))
    at = LEFT_E.start
    factors += [both[:, at : at + D], both[:, at + D : at + 2 * D]]
    factors.append(joined(a[:, LEFT_S], b[:, LEFT_S], t))
    found = orthonormal(factors)
    own_o = jnp.where(t == 0, found[3][:, :HALF], found[3][:, HALF:])
    own_s = jnp.where(t == 0, found[6][:, :FF], found[6][:, FF:])
    left_o[...] = own_o
    left_s[...] = own_s
    for c in range(3):
        left_i[c] = found[c]
    for c in range(2):
        left_e[c] = found[4 + c]
    right[:, RIGHT_G:] = gains[...].astype(BF)
    for c in copies:
        c.wait()
    for c in range(3):
        right[:, c * HALF : (c + 1) * HALF] = folded(nn(two_terms(found[c]), sum_i[c])).astype(BF)
    right[:, 3 * HALF : RIGHT_E] = jnp.zeros((RANK, RIGHT_E - 3 * HALF), BF)
    for c in range(2):
        at = RIGHT_E + c * FF
        right[:, at : at + FF] = folded(nn(two_terms(found[4 + c]), sum_e[c])).astype(BF)
    right[:, RIGHT_O : RIGHT_O + D] = folded(nn(two_terms(own_o), sum_o[...])).astype(BF)
    right[:, RIGHT_S : RIGHT_S + D] = folded(nn(two_terms(own_s), sum_s[...])).astype(BF)


def factors_of(place, mine, other, gains, sum_i, sum_o, sum_e, sum_s):
    sums = (sum_i, sum_o, sum_e, sum_s)
    outs = [(3, RANK, D), (RANK, HALF), (2, RANK, D), (RANK, FF)]
    return pl.pallas_call(
        factor_kernel,
        in_specs=[SMEM, full((RANK, LEFT)), full((RANK, LEFT)), full((8, 2 * D))] + [HBM] * 4,
        out_specs=[full(s) for s in outs] + [full((RANK, RIGHT))],
        out_shape=[like(s, F32) for s in outs] + [like((RANK, RIGHT), BF)],
        scratch_shapes=[pltpu.VMEM(s.shape, BF) for s in sums] + [pltpu.SemaphoreType.DMA((4,))],
        compiler_params=params(24),
        cost_estimate=cost(10**8, 10 * 2**20),
    )(place, mine, other, gains, *sums)


def left_terms(v):
    one = v.astype(BF).astype(F32)
    two = v - one
    return jnp.concatenate([one, one, two, two], axis=0).astype(BF)


def right_terms(v):
    one = v.astype(BF).astype(F32)
    two = v - one
    return jnp.concatenate([one, two, one, two], axis=0).astype(BF)


def own_rows(terms, place):
    dp = (place[0] * 4 + place[1]) * 4 + place[2]
    row = lax.broadcasted_iota(jnp.int32, (16, D), 0)
    col = lax.broadcasted_iota(jnp.int32, (16, D), 1)
    pick = jnp.where((row < SHARD) & (col == row + SHARD * dp), 1.0, 0.0).astype(BF)
    return nt(pick, terms).astype(BF)


def moved(old, weight, rate, own, momentum, updated):
    new = momentum_decay * old + own
    momentum[...] = new
    updated[...] = weight - rate * new


LAST = 3


def last_kernel(place, *refs):
    left_i, left_o, left_e, left_s, sums, other, sum_i, sum_o, sum_e, sum_s = refs[:10]
    old_i, old_o, old_e, old_s, w_i, w_o, w_e, w_s, gains, old_g = refs[10:20]
    res_i, res_o, res_e, res_s, mom_i, mom_o, mom_e, mom_s, new_i, new_o, new_e, new_s = refs[20:32]
    right_i, right_o, right_e, right_s, mom_g, new_g = refs[32:38]
    l_i, l_o, l_e, l_s, r_i, r_o, r_e, r_s = refs[38:]
    j = pl.program_id(0)
    scale = 1.0 / 64
    tail = lambda n: (sums[:, RIGHT_O + n * D : RIGHT_O + (n + 1) * D] + other[:, n * D : (n + 1) * D])
    e_rights = [sums[:, RIGHT_E + c * FF : RIGHT_E + (c + 1) * FF] for c in range(2)]
    i_rights = [sums[:, c * HALF : (c + 1) * HALF] for c in range(3)]

    @pl.when(j == 0)
    def _():
        for c in range(2):
            l_e[c * D : (c + 1) * D, :] = left_terms(left_e[c]).T
            r_e[c] = right_terms(e_rights[c] * scale)
        l_s[...] = left_terms(left_s[...]).T
        r_s[...] = right_terms(tail(1) * scale)
        for c in range(3):
            l_i[c * D : (c + 1) * D, :] = left_terms(left_i[c]).T
            r_i[c] = right_terms(i_rights[c] * scale)
        l_o[...] = left_terms(left_o[...]).T
        r_o[...] = right_terms(tail(0) * scale)

    at = lambda n: pl.ds(pl.multiple_of(j * n, n), n)
    for h in range(2):
        rows = pl.ds(pl.multiple_of(j * 512 + h * 256, 256), 256)
        which = (2 * j + h) // 3
        here = slice(h * 256, (h + 1) * 256)
        res_e[here, :] = sum_e[here, :].astype(F32) - nn(l_e[rows, :], r_e[which])
    res_s[0] = sum_s[...].astype(F32) - nn(l_s[at(512), :], r_s[...])
    res_i[0, 0] = sum_i[0].astype(F32) - nn(l_i[at(D), :], r_i[j])
    res_o[0] = sum_o[...].astype(F32) - nn(l_o[at(128), :], r_o[...])

    @pl.when(j == 1)
    def _():
        for c in range(2):
            right_e[c] = e_rights[c] * scale
            own = nn(own_rows(left_terms(left_e[c]), place), r_e[c])[:SHARD]
            moved(old_e[:, c, :], w_e[:, c, :], rate_expand, own, mom_e.at[:, c, :], new_e.at[:, c, :])
        right_s[...] = tail(1) * scale
        own = nn(own_rows(r_s[...], place), left_terms(left_s[...]))[:SHARD]
        moved(old_s[...], w_s[...], rate_shrink, own, mom_s, new_s)
        for c in range(3):
            right_i[c] = i_rights[c] * scale
            own = nn(own_rows(left_terms(left_i[c]), place), r_i[c])[:SHARD]
            moved(old_i[c], w_i[c], rate_inbound, own, mom_i.at[c], new_i.at[c])
        right_o[...] = tail(0) * scale
        own = nn(own_rows(r_o[...], place), left_terms(left_o[...]))[:SHARD]
        moved(old_o[...], w_o[...], rate_outbound, own, mom_o, new_o)
        for n in range(2):
            own = jnp.sum(tail(2 + n), axis=0, keepdims=True)
            row = slice(n, n + 1)
            moved(old_g[row], gains[row], rate_gains, own, mom_g.at[row], new_g.at[row])


def last(place, lefts, sums, other, made, old, w, gains, old_g):
    rows = lambda n, w: pl.BlockSpec((n, w), lambda j: (j, 0))
    sum_i, sum_o, sum_e, sum_s = made
    made = (sum_i, sum_o, sum_e.reshape(2 * D, FF), sum_s)
    small = [*lefts, sums, other]
    states = [*old, *w, gains, old_g]
    state_shapes = [(3, SHARD, HALF), (SHARD, HALF), (SHARD, 2, FF), (SHARD, FF)]
    rest_shapes = [(1, 3, D, HALF), (1, HALF, D), (2 * D, FF), (1, FF, D)]
    tails = [(3, RANK, HALF), (RANK, D), (2, RANK, FF), (RANK, D), (2, D), (2, D)]
    flat = state_shapes * 2 + tails
    outs = pl.pallas_call(
        last_kernel,
        grid=(LAST,),
        in_specs=[SMEM]
        + [full(a.shape) for a in small]
        + [pl.BlockSpec((1, D, HALF), lambda j: (j, 0, 0)), rows(128, D), rows(512, FF), rows(512, D)]
        + [full(a.shape) for a in states],
        out_specs=[
            pl.BlockSpec((1, 1, D, HALF), lambda j: (0, j, 0, 0)),
            pl.BlockSpec((1, 128, D), lambda j: (0, j, 0)),
            rows(512, FF),
            pl.BlockSpec((1, 512, D), lambda j: (0, j, 0)),
        ]
        + [full(s) for s in flat],
        out_shape=[like(s, F32) for s in rest_shapes + flat],
        scratch_shapes=[
            pltpu.VMEM((3 * D, 32), BF),
            pltpu.VMEM((HALF, 32), BF),
            pltpu.VMEM((2 * D, 32), BF),
            pltpu.VMEM((FF, 32), BF),
            pltpu.VMEM((3, 32, HALF), BF),
            pltpu.VMEM((32, D), BF),
            pltpu.VMEM((2, 32, FF), BF),
            pltpu.VMEM((32, D), BF),
        ],
        compiler_params=params(28),
        cost_estimate=cost(10**8, 30 * 2**20),
    )(place, *small, *made, *states)
    return (*outs[:2], outs[2].reshape(1, 2, D, FF), *outs[3:])


def lane_tables(ids):
    zeros = jnp.sum((ids == 0).astype(jnp.int32))
    ones = jnp.sum((ids == 1).astype(jnp.int32))
    before = jnp.where(ids == 0, 0, jnp.where(ids == 1, zeros, zeros + ones))
    places = (jnp.arange(SEQ, dtype=jnp.int32) - before).astype(F32)
    lane = jnp.arange(128, dtype=jnp.int32)
    inverse = rope_base ** (-((lane % 32).astype(F32) * 2.0) / HEAD_DIM)
    angles = places[:, None] * inverse[None, :]
    first = (lane % 64 < 32)[None, :]
    sine = jnp.sin(angles)
    low, high = jnp.where(first, -sine, 0.0), jnp.where(first, 0.0, sine)
    kind = lane[None, :]
    same = ids[:, None] == kind
    fq = jnp.where((kind < 3) & same, 1.0, 0.0).astype(BF)
    fk = jnp.where(kind < 3, jnp.where(same, 0.0, MASKED), jnp.where(kind < 6, 1.0, 0.0))
    return (jnp.cos(angles), low, high), fq, fk.astype(BF)


def both_halves(own, t):
    other = swap(own)
    whole = jnp.zeros((SEQ, D), BF)
    whole = lax.dynamic_update_slice_in_dim(whole, own, t * 512, 0)
    return lax.dynamic_update_slice_in_dim(whole, other, (1 - t) * 512, 0)


def local(
    tokens,
    segment_ids,
    cotangent,
    norm_gains,
    gains_moment,
    inbound,
    outbound,
    expand,
    shrink,
    inbound_moment,
    outbound_moment,
    expand_moment,
    shrink_moment,
    inbound_error,
    outbound_error,
    expand_error,
    shrink_error,
    inbound_start,
    outbound_start,
    expand_start,
    shrink_start,
):
    y, x, z, t = (lax.axis_index(a) for a in DP_TENSOR)
    place = jnp.stack([y, x, z, t]).astype(jnp.int32)

    shard = weight_shard(inbound, outbound.T, jnp.swapaxes(expand, 0, 1), shrink.T)
    shard, segment_ids, tokens, cotangent = lax.optimization_barrier(
        (shard, segment_ids, tokens, cotangent)
    )
    column = [shard, shift(shard, Z, 1), shift(shard, Z, 3), shift(shard, Z, 2)]
    tables, fq, fk = lane_tables(segment_ids)
    column, fq, fk = lax.optimization_barrier((column, fq, fk))
    quarter, feed_rows = rows_of_column(place, column)
    feed_weights = lax.all_gather(feed_rows, (Y, X)).reshape(D, 3 * FF)
    x_all = both_halves(tokens, t)
    quarter = rows_of_plane(quarter)
    cot_all = both_halves(cotangent, t)
    near = shift(quarter, Z, 1), shift(quarter, Z, 3)
    near, x_all, cot_all, tables = lax.optimization_barrier((near, x_all, cot_all, tables))
    far = shift(near[0][:HALF], Z, 1), shift(near[1][HALF:], Z, 3)
    in_pieces = [quarter, *near, *far]

    gain_one, gain_two = norm_gains[0:1], norm_gains[1:2]
    normed, weights, q, k, v, att, fq_all, w_out = attention(
        place, gain_one, x_all, tables, fq, fk, in_pieces
    )
    w_other, att_other = swap(w_out), swap(att)

    start_e, start_s = jnp.swapaxes(expand_start, 1, 2), shrink_start.T
    sum_e, sum_s, left_e, left_s, middle, grad, hid = feed(
        place,
        gain_two,
        x_all,
        att,
        att_other,
        w_out,
        w_other,
        cot_all,
        expand_error,
        shrink_error,
        feed_weights,
        start_e,
        start_s,
    )
    grad_other = swap(grad)
    middle_grad, sum_o, dproj, sum_i, gain_second, left = backward(
        place,
        gain_two,
        outbound_start.T,
        jnp.swapaxes(inbound_start, 1, 2),
        grad_other,
        grad,
        middle,
        cot_all,
        att,
        w_out,
        outbound_error,
        q,
        k,
        v,
        fq_all,
        fk,
        *tables,
        normed,
        inbound_error,
        left_e,
        left_s,
    )

    left, dproj = lax.optimization_barrier((left, dproj))
    terms = ring_terms(left, Z)
    first_own, first_send = first_grad_rows(place, dproj, weights)
    terms, first_own, first_send = lax.optimization_barrier((terms, first_own, first_send))
    terms = ring_terms(rounded(ring_sum(terms)), X)
    first_other = swap(first_send)
    terms, first_other = lax.optimization_barrier((terms, first_other))
    terms = ring_terms(rounded(ring_sum(terms)), Y)
    input_grad, gains = input_grad_rows(
        tokens, gain_one, middle_grad, first_own, first_other, gain_second
    )
    terms, gains = lax.optimization_barrier((terms, gains))
    mine = ring_sum(terms)
    left_i, left_o, left_e, left_s, right = factors_of(
        place, mine, swap(mine), gains, sum_i, sum_o, sum_e, sum_s
    )

    right, hid = lax.optimization_barrier((right, hid))
    terms = ring_terms(right, Z)
    own_out, send_out = down_rows(place, hid, feed_weights)
    terms, own_out, send_out = lax.optimization_barrier((terms, own_out, send_out))
    terms = ring_terms(rounded(ring_sum(terms)), X)
    send_out = swap(send_out)
    terms, send_out = lax.optimization_barrier((terms, send_out))
    terms = ring_terms(rounded(ring_sum(terms)), Y)
    own_middle = lax.dynamic_slice_in_dim(middle, t * 512, 512, 0)
    layer_output = (own_middle + (own_out + send_out.astype(F32))).astype(BF)
    terms, layer_output = lax.optimization_barrier((terms, layer_output))
    sums = ring_sum(terms)
    (
        res_i,
        res_o,
        res_e,
        res_s,
        inbound_momentum,
        outbound_momentum,
        expand_momentum,
        shrink_momentum,
        inbound_updated,
        outbound_updated,
        expand_updated,
        shrink_updated,
        right_i,
        right_o,
        right_e,
        right_s,
        gains_momentum,
        gains_updated,
    ) = last(
        place,
        (left_i, left_o, left_e, left_s),
        sums,
        swap(sums[:, RIGHT_O:]),
        (sum_i, sum_o, sum_e, sum_s),
        (inbound_moment, outbound_moment.T, jnp.swapaxes(expand_moment, 0, 1), shrink_moment.T),
        (inbound, outbound.T, jnp.swapaxes(expand, 0, 1), shrink.T),
        norm_gains,
        gains_moment,
    )
    return (
        layer_output,
        input_grad,
        gains_momentum,
        gains_updated,
        inbound_momentum,
        outbound_momentum.T,
        jnp.swapaxes(expand_momentum, 0, 1),
        shrink_momentum.T,
        inbound_updated,
        outbound_updated.T,
        jnp.swapaxes(expand_updated, 0, 1),
        shrink_updated.T,
        res_i,
        res_o,
        res_e,
        res_s,
        jnp.swapaxes(left_i, 1, 2),
        jnp.swapaxes(right_i, 1, 2),
        left_o.T,
        right_o.T,
        jnp.swapaxes(left_e, 1, 2),
        jnp.swapaxes(right_e, 1, 2),
        left_s.T,
        right_s.T,
    )


def solution(mesh):
    torus = Mesh(mesh.devices.reshape(4, 4, 4, mesh.shape["tensor"]), DP_TENSOR)
    return jax.shard_map(
        local,
        mesh=torus,
        in_specs=(
            P(DP_TENSOR, None),
            P(DP),
            P(DP_TENSOR, None),
            P(),
            P(),
            P(None, DP, T),
            P(T, DP),
            P(None, DP, T),
            P(T, DP),
            P(None, DP, T),
            P(T, DP),
            P(None, DP, T),
            P(T, DP),
            P(DP, None, None, T),
            P(DP, T, None),
            P(DP, None, None, T),
            P(DP, T, None),
            P(None, T, None),
            P(),
            P(None, T, None),
            P(),
        ),
        out_specs=(
            P(DP_TENSOR, None),
            P(DP_TENSOR, None),
            P(),
            P(),
            P(None, DP, T),
            P(T, DP),
            P(None, DP, T),
            P(T, DP),
            P(None, DP, T),
            P(T, DP),
            P(None, DP, T),
            P(T, DP),
            P(DP, None, None, T),
            P(DP, T, None),
            P(DP, None, None, T),
            P(DP, T, None),
            P(),
            P(None, T, None),
            P(T, None),
            P(),
            P(),
            P(None, T, None),
            P(T, None),
            P(),
        ),
        check_vma=False,
    )
```

```python
import jax
import jax.numpy as jnp
from jax import lax
from jax.experimental import pallas as pl
from jax.experimental.pallas import tpu as pltpu
from jax.sharding import Mesh
from jax.sharding import PartitionSpec as P

Y, X, Z, T = "dp_0", "dp_1", "dp_2", "tensor"
DP = (Y, X, Z)
DP_TENSOR = (Y, X, Z, T)
F32, BF = jnp.float32, jnp.bfloat16

SEQ = 1024
D = 768
HEAD_DIM = 64
HALF = 384
FF = 1536
RANK = 8
BLOCK = 256
SHARD = 12
CHUNK = 256
CHUNKS = FF // CHUNK
WIDE = 512
WIDES = FF // WIDE
EPS = 1e-06
MASKED = -1e30

momentum_decay = 0.9
rate_inbound = 0.2
rate_outbound = 6.0
rate_expand = 0.3
rate_shrink = 0.25
rate_gains = 0.0005
rope_base = 10000.0

ANY = pl.BlockSpec(memory_space=pl.ANY)
HBM = pl.BlockSpec(memory_space=pltpu.HBM)
SMEM = pl.BlockSpec(memory_space=pltpu.SMEM)


def nn(a, b):
    return jnp.dot(a, b, preferred_element_type=F32)


def nt(a, b):
    return lax.dot_general(a, b, (((1,), (1,)), ((), ())), preferred_element_type=F32)


def tn(a, b):
    return lax.dot_general(a, b, (((0,), (0,)), ((), ())), preferred_element_type=F32)


def params(mib=56):
    return pltpu.CompilerParams(vmem_limit_bytes=mib * 2**20)


def cost(flops, moved):
    return pl.CostEstimate(flops=flops // 64, bytes_accessed=moved // 64, transcendentals=0)


def full(shape):
    return pl.BlockSpec(shape, lambda *_: (0,) * len(shape))


def like(shape, dtype):
    return jax.ShapeDtypeStruct(shape, dtype)


def shift(v, axis, d):
    n = lax.axis_size(axis)
    return lax.ppermute(v, axis, [(i, (i + d) % n) for i in range(n)])


def swap(v):
    return lax.ppermute(v, T, [(0, 1), (1, 0)])


def rounded(v):
    return lax.reduce_precision(v, exponent_bits=8, mantissa_bits=7)


def ring_terms(v, axis):
    low = v.astype(BF)
    return v, shift(low, axis, 2), shift(low, axis, 1), shift(low, axis, 3)


def ring_sum(terms):
    own, two, one, back = (v.astype(F32) for v in terms)
    return (own + two) + (one + back)


def shard_kernel(inbound, outbound, expand, shrink, out):
    for c in range(3):
        out[:, c * HALF : (c + 1) * HALF] = inbound[c].astype(BF)
    out[:, 1152:1536] = outbound[...].astype(BF)
    for j in range(WIDES):
        for c in range(2):
            at = 1536 + (2 * j + c) * WIDE
            out[:, at : at + WIDE] = expand[:, c, j * WIDE : (j + 1) * WIDE].astype(BF)
    out[:, 4608:] = shrink[...].astype(BF)


def weight_shard(inbound, outbound, expand, shrink):
    return pl.pallas_call(
        shard_kernel,
        out_shape=like((SHARD, 6144), BF),
        compiler_params=params(),
        cost_estimate=cost(10**5, 2**19),
    )(inbound, outbound, expand, shrink)


def column_kernel(place, own, one, back, two, quarter, feed, rows):
    z = place[2]
    pieces = [r[...].astype(F32) for r in (own, one, two, back)]
    for p in range(4):
        away = lax.rem(p + 4 - z, 4)
        piece = jnp.where(
            away == 0,
            pieces[0],
            jnp.where(away == 3, pieces[1], jnp.where(away == 2, pieces[2], pieces[3])),
        )
        rows[p * SHARD : (p + 1) * SHARD, :] = piece
    quarter[...] = rows[:, pl.ds(pl.multiple_of(z * HALF, 128), HALF)].astype(BF)
    feed[...] = rows[:, 1536:].astype(BF)


def rows_of_column(place, pieces):
    widths = (HALF, 3 * FF)
    return pl.pallas_call(
        column_kernel,
        in_specs=[SMEM] + [full(pieces[0].shape)] * 4,
        out_specs=[full((48, w)) for w in widths],
        out_shape=[like((48, w), BF) for w in widths],
        scratch_shapes=[pltpu.VMEM((48, 6144), F32)],
        compiler_params=params(16),
        cost_estimate=cost(10**6, 2**21),
    )(place, *pieces)


def rows_of_plane(v):
    everyone = jnp.broadcast_to(v[None], (16, *v.shape))
    rows = lax.all_to_all(everyone, (Y, X), 0, 0, tiled=True)
    return rows.reshape(16 * v.shape[0], v.shape[1])


def place_pieces(pieces, target, sems, place):
    copies = []
    spots = ((0, 0), (3, 0), (1, 0), (2, 0), (2, HALF))
    for n, (piece, (away, row)) in enumerate(zip(pieces, spots)):
        at = pl.multiple_of(lax.rem(place[2] + away, 4) * HALF, 128)
        spot = target.at[pl.ds(row, piece.shape[0]), pl.ds(at, HALF)]
        copies.append(pltpu.make_async_copy(piece, spot, sems.at[n]))
    return copies


def turn_lanes(v, cos, low, high):
    return v * cos + pltpu.roll(v, 96, 1) * low + pltpu.roll(v, 32, 1) * high


def head_lanes(rows, h):
    lane = lax.broadcasted_iota(jnp.int32, (rows, 128), 1)
    return (lane < 64) if h == 0 else (lane >= 64)


def three_terms(v):
    one = v.astype(BF).astype(F32)
    two = (v - one).astype(BF).astype(F32)
    return one, two, v - one - two


def both_heads(v):
    zero = jnp.zeros((), BF)
    return [jnp.where(head_lanes(v.shape[0], h), v, zero) for h in range(2)]


def pair_forward(q, k, v, fq, fk, out, fq_out):
    keys = jnp.concatenate([k[...], fk[...]], axis=1)
    vals = v[...]
    lane = lax.broadcasted_iota(jnp.int32, (256, 128), 1)
    first = head_lanes(256, 0)
    scores = []
    for b in range(4):
        rows = slice(b * 256, (b + 1) * 256)
        f = fq[rows, :]
        heads = [jnp.concatenate([m, f], axis=1) for m in both_heads(q[rows, :])]
        scores.append(nt(jnp.concatenate(heads, axis=0), keys[: (b + 1) * 256]))
    for b in range(4):
        rows = slice(b * 256, (b + 1) * 256)
        s = scores[b]
        largest = jnp.max(s, axis=1, keepdims=True)
        e = jnp.exp(s - largest)
        sums = jnp.sum(e, axis=1, keepdims=True)
        o = nn(e.astype(BF), vals[: (b + 1) * 256]) * (1.0 / sums)
        out[rows, :] = jnp.where(first, o[:256], o[256:]).astype(BF)
        one, two, three = three_terms(-(largest + jnp.log(sums)))
        for h in range(2):
            at = slice(h * 256, (h + 1) * 256)
            extra = jnp.where(lane == 3, one[at], jnp.where(lane == 4, two[at], three[at]))
            fq_out[h, rows, :] = jnp.where((lane >= 3) & (lane < 6), extra.astype(BF), fq[rows, :])


def attention_kernel(place, gain, *refs):
    hbm_in, pieces, hbm_out, refs = refs[:6], refs[6:11], refs[11:19], refs[19:]
    held, made, refs = refs[:6], refs[6:13], refs[13:]
    piece_sems, in_sems, out_sems, pair_sems = refs
    x, cos, low, high, fq, fk = held
    normed, weights, q, k, v, att, fq_all = made
    copy = pltpu.make_async_copy
    gets = [copy(hbm_in[0].at[pl.ds(i * 512, 512)], x.at[pl.ds(i * 512, 512)], in_sems.at[i]) for i in range(2)]
    gets += [copy(h, r, in_sems.at[n + 2]) for n, (h, r) in enumerate(zip(hbm_in[1:], held[1:]))]
    puts = [copy(r, h, out_sems.at[n]) for n, (r, h) in enumerate(zip(made[:5], hbm_out))]
    put_out = copy(weights.at[:, pl.ds(3 * HALF, HALF)], hbm_out[7], out_sems.at[7])

    def put_pair(p):
        lanes = pl.ds(pl.multiple_of(p * 128, 128), 128)
        heads = pl.ds(2 * p, 2)
        return (
            copy(att.at[:, lanes], hbm_out[5].at[:, lanes], pair_sems.at[0, p]),
            copy(fq_all.at[heads], hbm_out[6].at[heads], pair_sems.at[1, p]),
        )

    placed = place_pieces(pieces, weights, piece_sems, place)
    for c in gets[:2] + placed + gets[2:]:
        c.start()
    for i in range(2):
        rows = slice(i * 512, (i + 1) * 512)
        gets[i].wait()
        xb = x[rows, :].astype(F32)
        inverse = lax.rsqrt(jnp.mean(xb * xb, axis=1, keepdims=True) + EPS)
        n = (xb * inverse * gain[...]).astype(BF)
        x[rows, :] = n
        normed[:, rows] = n.T
    puts[0].start()
    for c in placed:
        c.wait()
    puts[1].start()
    put_out.start()
    for c in gets[2:]:
        c.wait()
    for i in range(2):
        rows = slice(i * 512, (i + 1) * 512)
        found = nn(x[rows, :], weights[:, :1152])
        tables = cos[rows, :], low[rows, :], high[rows, :]
        v[rows, :] = found[:, 768:].astype(BF)
        for p in range(3):
            at = slice(p * 128, (p + 1) * 128)
            q[rows, at] = (turn_lanes(found[:, at], *tables) * 0.125).astype(BF)
            k_lanes = found[:, HALF + p * 128 : HALF + (p + 1) * 128]
            k[rows, at] = turn_lanes(k_lanes, *tables).astype(BF)
    for c in puts[2:5]:
        c.start()

    def one_pair(p, carry):
        lanes = pl.ds(pl.multiple_of(p * 128, 128), 128)
        views = [r.at[:, lanes] for r in (q, k, v)]
        pair_forward(*views, fq, fk, att.at[:, lanes], fq_all.at[pl.ds(2 * p, 2)])
        for c in put_pair(p):
            c.start()
        return carry

    lax.fori_loop(0, 3, one_pair, 0)
    put_out.wait()
    for c in puts[:5]:
        c.wait()
    for p in range(3):
        for c in put_pair(p):
            c.wait()


def attention(place, gain, x, tables, fq, fk, pieces):
    arrays = (x, *tables, fq, fk)
    half = like((SEQ, HALF), BF)
    outs = [like((D, SEQ), BF), like((D, 2 * D), BF), half, half, half, half, like((6, SEQ, 128), BF)]
    return pl.pallas_call(
        attention_kernel,
        in_specs=[SMEM, full((1, D))] + [HBM] * 11,
        out_specs=[HBM] * 8,
        out_shape=[*outs, like((D, HALF), BF)],
        scratch_shapes=[pltpu.VMEM(a.shape, a.dtype) for a in arrays]
        + [pltpu.VMEM(o.shape, o.dtype) for o in outs]
        + [
            pltpu.SemaphoreType.DMA((5,)),
            pltpu.SemaphoreType.DMA((7,)),
            pltpu.SemaphoreType.DMA((8,)),
            pltpu.SemaphoreType.DMA((2, 3)),
        ],
        compiler_params=params(),
        cost_estimate=cost(10**10, 12 * 2**20),
    )(place, gain, *arrays, *pieces)


def two_terms(v):
    one = v.astype(BF).astype(F32)
    return jnp.concatenate([one, v - one], axis=0).astype(BF)


def folded(v):
    return v[0:8] + v[8:16]


def feed_kernel(place, gain, *refs):
    h_x, h_att, h_other, h_w, h_w_other, h_cot, h_err_e, h_err_s, h_feed = refs[:9]
    start_e, start_s, sum_e, sum_s, left_e, left_s = refs[9:15]
    h_middle, h_grad, h_hid = refs[15:18]
    x, att, other, w_out, w_other, cot, both, down, err_e, err_s = refs[18:28]
    middle, second, turned, hid, grads, grad_low = refs[28:34]
    rows_sem, in_sem, both_sem, down_sem, err_sem, out_sem = refs[34:]
    j = pl.program_id(0)
    copy = pltpu.make_async_copy

    def lanes(n, width, start=0):
        return pl.ds(pl.multiple_of(start + n * width, width), width)

    def get_rows(i):
        rows = pl.ds(i * 512, 512)
        trio = ((h_x, x), (h_att, att), (h_other, other))
        return [copy(h.at[rows], r.at[rows], rows_sem.at[n, i]) for n, (h, r) in enumerate(trio)]

    def get_both(n):
        at = lanes(n, 2 * WIDE)
        return copy(h_feed.at[:, at], both.at[:, at], both_sem.at[n])

    def get_down(n):
        return copy(h_feed.at[:, lanes(n, WIDE, 2 * FF)], down.at[:, lanes(n, WIDE)], down_sem.at[n])

    def get_err(n):
        slot = lax.rem(n, 2)
        return (
            copy(h_err_e.at[0, :, :, lanes(n, WIDE)], err_e.at[slot], err_sem.at[0, slot]),
            copy(h_err_s.at[0, lanes(n, WIDE)], err_s.at[slot], err_sem.at[1, slot]),
        )

    get_w = copy(h_w, w_out, in_sem.at[0])
    get_w_other = copy(h_w_other, w_other, in_sem.at[1])
    get_cot = copy(h_cot, cot, in_sem.at[2])
    put_middle = copy(middle, h_middle, out_sem.at[0])
    put_grad = copy(grad_low, h_grad, out_sem.at[1])
    put_hid = copy(hid, h_hid, out_sem.at[2])

    @pl.when(j == 0)
    def _():
        order = [get_w, get_w_other, *get_rows(0), *get_rows(1), get_both(0), get_cot, get_down(0)]
        for c in order + [*get_err(0)]:
            c.start()
        for n in range(1, WIDES):
            get_both(n).start()
            get_down(n).start()
            if n == 1:
                for c in get_err(n):
                    c.start()
        left_e[...] = jnp.zeros_like(left_e)
        get_w.wait()
        get_w_other.wait()
        for i in range(2):
            rows = slice(i * 512, (i + 1) * 512)
            for c in get_rows(i):
                c.wait()
            m = x[rows, :].astype(F32) + nt(att[rows, :], w_out[...]) + nt(other[rows, :], w_other[...])
            middle[rows, :] = m
            inverse = lax.rsqrt(jnp.mean(m * m, axis=1, keepdims=True) + EPS)
            low = (m * inverse * gain[...]).astype(BF)
            second[rows, :] = low
            turned[:, rows] = low.T
        put_middle.start()

    get_both(j).wait()
    w_both = both.at[:, lanes(j, 2 * WIDE)]
    w_down = down.at[:, lanes(j, WIDE)]
    my_hid = hid.at[:, lanes(j, WIDE)]
    my_grads = grads.at[:, lanes(j, 2 * WIDE)]
    step = FEED_ROWS
    found = []
    for b in range(SEQ // step):
        found.append(nn(second[b * step : (b + 1) * step, :], w_both[...]))

    @pl.when(j == 0)
    def _():
        get_cot.wait()

    get_down(j).wait()
    for b in range(SEQ // step):
        rows = slice(b * step, (b + 1) * step)
        gu, hg = found[b], nn(cot[rows, :], w_down[...])
        g, u = gu[:, :WIDE], gu[:, WIDE:]
        sig = 0.5 * jnp.tanh(0.5 * g) + 0.5
        act = g * sig
        my_hid[rows, :] = (act * u).astype(BF)
        my_grads[rows, :WIDE] = (hg * u * (sig + act * (1.0 - sig))).astype(BF)
        my_grads[rows, WIDE:] = (hg * act).astype(BF)

    @pl.when(j == WIDES - 1)
    def _():
        put_hid.start()
        grad_low[...] = nt(grads[...], both[...]).astype(BF)
        put_grad.start()

    for c in get_err(j):
        c.wait()
    slot = lax.rem(j, 2)
    low = (tn(my_hid[...], cot[...]) + err_s[slot]).astype(BF)
    sum_s[...] = low
    left_s[...] = folded(nt(two_terms(start_s[...]), low))
    made = nn(turned[...], my_grads[...])
    for c in range(2):
        low = (made[:, c * WIDE : (c + 1) * WIDE] + err_e[slot, c]).astype(BF)
        sum_e[c] = low
        left_e[:, c * D : (c + 1) * D] += folded(nt(two_terms(start_e[c]), low))

    @pl.when(j + 2 < WIDES)
    def _():
        for c in get_err(j + 2):
            c.start()

    @pl.when(j == WIDES - 1)
    def _():
        put_middle.wait()
        put_hid.wait()
        put_grad.wait()


FEED_ROWS = 256
FEED_MIB = 56


def feed(place, gain, x, att, other, weights, w_other, cot, err_e, err_s, feed_weights, start_e, start_s):
    arrays = (x, att, other, weights, w_other, cot, err_e, err_s, feed_weights)
    return pl.pallas_call(
        feed_kernel,
        grid=(WIDES,),
        in_specs=[SMEM, full((1, D)), HBM, HBM, ANY, HBM, ANY]
        + [HBM] * 4
        + [pl.BlockSpec((2, RANK, WIDE), lambda j: (0, 0, j)), full((RANK, D))],
        out_specs=[
            pl.BlockSpec((2, D, WIDE), lambda j: (0, 0, j)),
            pl.BlockSpec((WIDE, D), lambda j: (j, 0)),
            full((RANK, 2 * D)),
            pl.BlockSpec((RANK, WIDE), lambda j: (0, j)),
            HBM,
            HBM,
            HBM,
        ],
        out_shape=[
            like((2, D, FF), BF),
            like((FF, D), BF),
            like((RANK, 2 * D), F32),
            like((RANK, FF), F32),
            like((SEQ, D), F32),
            like((SEQ, D), BF),
            like((SEQ, FF), BF),
        ],
        scratch_shapes=[
            pltpu.VMEM((SEQ, D), BF),
            pltpu.VMEM((SEQ, HALF), BF),
            pltpu.VMEM((SEQ, HALF), BF),
            pltpu.VMEM((D, HALF), BF),
            pltpu.VMEM((D, HALF), BF),
            pltpu.VMEM((SEQ, D), BF),
            pltpu.VMEM((D, 2 * FF), BF),
            pltpu.VMEM((D, FF), BF),
            pltpu.VMEM((2, 2, D, WIDE), F32),
            pltpu.VMEM((2, WIDE, D), F32),
            pltpu.VMEM((SEQ, D), F32),
            pltpu.VMEM((SEQ, D), BF),
            pltpu.VMEM((D, SEQ), BF),
            pltpu.VMEM((SEQ, FF), BF),
            pltpu.VMEM((SEQ, 2 * FF), BF),
            pltpu.VMEM((SEQ, D), BF),
            pltpu.SemaphoreType.DMA((3, 2)),
            pltpu.SemaphoreType.DMA((3,)),
            pltpu.SemaphoreType.DMA((WIDES,)),
            pltpu.SemaphoreType.DMA((WIDES,)),
            pltpu.SemaphoreType.DMA((2, 2)),
            pltpu.SemaphoreType.DMA((3,)),
        ],
        compiler_params=params(FEED_MIB),
        cost_estimate=cost(18 * SEQ * D * FF, 40 * 2**20),
    )(place, gain, *arrays, start_e, start_s)


def down_kernel(place, hid, weights, own, send):
    t = place[3]
    for i in range(2):
        part = nt(hid[i * 512 : (i + 1) * 512, :], weights[...])

        @pl.when(t == i)
        def _():
            own[...] = part

        @pl.when(t != i)
        def _():
            send[...] = part.astype(BF)


def down_rows(place, hid, weights):
    return pl.pallas_call(
        down_kernel,
        grid=(1,),
        in_specs=[SMEM, full((SEQ, FF)), pl.BlockSpec((D, FF), lambda j: (0, 2))],
        out_specs=[full((512, D)), full((512, D))],
        out_shape=[like((512, D), F32), like((512, D), BF)],
        compiler_params=params(24),
        cost_estimate=cost(2 * SEQ * D * FF, 8 * 2**20),
    )(place, hid, weights)


def by_eight(v):
    return jnp.sum(v.reshape(-1, 8, v.shape[1]), axis=0)


LEFT_O = slice(3 * D, 3 * D + HALF)
LEFT_E = slice(3 * D + HALF, 5 * D + HALF)
LEFT_S = slice(5 * D + HALF, 5 * D + HALF + FF)
LEFT = 5 * D + HALF + FF


def pair_back(q, k, v, att, grad, fq, fk, cos, low, high, out, dk_acc, dv_acc):
    lane = lax.broadcasted_iota(jnp.int32, (256, 128), 1)
    ones = jnp.where(lax.broadcasted_iota(jnp.int32, (SEQ, 128), 1) < 3, 1.0, 0.0).astype(BF)
    keys = jnp.concatenate([k[...], fk[...]], axis=1)
    vals = jnp.concatenate([v[...], ones], axis=1)
    kt = k[...].T
    dk_acc[...] = jnp.zeros_like(dk_acc)
    dv_acc[...] = jnp.zeros_like(dv_acc)
    for b in range(4):
        rows = slice(b * 256, (b + 1) * 256)
        count = (b + 1) * 256
        qs, gs = both_heads(q[rows, :]), both_heads(grad[rows, :])
        q_rows = [jnp.concatenate([qs[h], fq[h, rows, :]], axis=1) for h in range(2)]
        g_rows = []
        for h in range(2):
            centre = jnp.sum(gs[h].astype(F32) * att[rows, :].astype(F32), axis=1, keepdims=True)
            one, two, three = three_terms(-centre)
            extra = jnp.where(lane == 0, one, jnp.where(lane == 1, two, three))
            fg = jnp.where(lane < 3, extra, 0.0).astype(BF)
            g_rows.append(jnp.concatenate([gs[h], fg], axis=1))
        soft = jnp.exp(nt(keys[:count], jnp.concatenate(q_rows, axis=0)))
        ds = (soft * nt(vals[:count], jnp.concatenate(g_rows, axis=0))).astype(BF)
        dv_acc[:count, :] += nn(soft.astype(BF), jnp.concatenate(gs, axis=0))
        dk_acc[:count, :] += nn(ds, jnp.concatenate(qs, axis=0))
        part = nn(kt[:, :count], ds)
        dq = jnp.concatenate([part[:64, :256], part[64:, 256:]], axis=0).T * 0.125
        out[0][rows, :] = turn_lanes(dq, cos[rows, :], -low[rows, :], -high[rows, :]).astype(BF)
    out[1][...] = turn_lanes(dk_acc[...], cos[...], -low[...], -high[...]).astype(BF)
    out[2][...] = dv_acc[...].astype(BF)


def backward_kernel(place, gain, start_o, start_i, grad_other, *refs):
    hbm_in, hbm_out, refs = refs[:18], refs[18:22], refs[22:]
    gain_sum, left = refs[:2]
    held, made, refs = refs[2:20], refs[20:24], refs[24:]
    att_grad, acc, dk_acc, dv_acc, in_sems, out_sems = refs
    grad, middle, cot, att, w_out, err_o, q, k, v, fq, fk, cos, low, high, turned, err_i, left_e, left_s = held
    middle_grad, sum_o, dproj, sum_i = made
    copy = pltpu.make_async_copy
    gets = []
    for n in range(3):
        for i in range(2):
            rows = pl.ds(i * 512, 512)
            gets.append(copy(hbm_in[n].at[rows], held[n].at[rows], in_sems.at[2 * n + i]))
    for n in range(3, 18):
        gets.append(copy(hbm_in[n], held[n], in_sems.at[n + 3]))
    puts = [copy(m, h, out_sems.at[n]) for n, (m, h) in enumerate(zip(made, hbm_out))]
    for c in gets[0:6:2] + gets[6:8] + gets[1:6:2] + gets[8:]:
        c.start()

    for i in range(2):
        for c in gets[i:6:2]:
            c.wait()
        if i == 0:
            for c in gets[6:8]:
                c.wait()
        rows = slice(i * 512, (i + 1) * 512)
        m = middle[rows, :]
        inverse = lax.rsqrt(jnp.mean(m * m, axis=1, keepdims=True) + EPS)
        unit = m * inverse
        w = grad[rows, :].astype(F32) + grad_other[rows, :].astype(F32)
        a = w * gain[...]
        back = inverse * (a - unit * jnp.mean(a * unit, axis=1, keepdims=True))
        mg = cot[rows, :].astype(F32) + back
        branch = mg.astype(BF)
        att_grad[rows, :] = nn(branch, w_out[...]).astype(BF)
        part = tn(att[rows, :], branch)
        if i == 0:
            acc[...] = part
        else:
            acc[...] += part

        @pl.when(place[3] == i)
        def _():
            middle_grad[...] = mg
            gain_sum[...] = by_eight(w * unit)

    puts[0].start()
    gets[8].wait()
    summed = (acc[...] + err_o[0]).astype(BF)
    sum_o[...] = summed
    puts[1].start()
    left[:, LEFT_O] = folded(nt(two_terms(start_o[...]), summed)).astype(BF)

    for c in gets[9:17]:
        c.wait()

    def one_pair(p, carry):
        lanes = pl.ds(pl.multiple_of(p * 128, 128), 128)
        pair_back(
            *(r.at[:, lanes] for r in (q, k, v, att, att_grad)),
            fq.at[pl.ds(2 * p, 2)],
            fk,
            cos,
            low,
            high,
            [dproj.at[:, pl.ds(pl.multiple_of(c * HALF + p * 128, 128), 128)] for c in range(3)],
            dk_acc,
            dv_acc,
        )
        return carry

    lax.fori_loop(0, 3, one_pair, 0)
    puts[2].start()

    for c in gets[17:]:
        c.wait()
    left[:, LEFT_E] = left_e[...].astype(BF)
    left[:, LEFT_S] = left_s[...].astype(BF)
    found = nn(turned[...], dproj[...])
    for c in range(3):
        summed = (found[:, c * HALF : (c + 1) * HALF] + err_i[0, c]).astype(BF)
        sum_i[c] = summed
        left[:, c * D : (c + 1) * D] = folded(nt(two_terms(start_i[c]), summed)).astype(BF)
    puts[3].start()
    for c in puts:
        c.wait()


BACK_MIB = 60


def backward(place, gain, start_o, start_i, grad_other, *arrays):
    small = (gain, start_o, start_i, grad_other)
    outs = [like((512, D), F32), like((HALF, D), BF), like((SEQ, 3 * HALF), BF), like((3, D, HALF), BF)]
    return pl.pallas_call(
        backward_kernel,
        in_specs=[SMEM] + [full(a.shape) for a in small] + [HBM] * 18,
        out_specs=[HBM] * 4 + [full((8, D)), full((RANK, LEFT))],
        out_shape=outs + [like((8, D), F32), like((RANK, LEFT), BF)],
        scratch_shapes=[pltpu.VMEM(a.shape, a.dtype) for a in arrays]
        + [pltpu.VMEM(o.shape, o.dtype) for o in outs]
        + [
            pltpu.VMEM((SEQ, HALF), BF),
            pltpu.VMEM((HALF, D), F32),
            pltpu.VMEM((SEQ, 128), F32),
            pltpu.VMEM((SEQ, 128), F32),
            pltpu.SemaphoreType.DMA((21,)),
            pltpu.SemaphoreType.DMA((4,)),
        ],
        compiler_params=params(BACK_MIB),
        cost_estimate=cost(20 * 10**9, 30 * 2**20),
    )(place, *small, *arrays)


def first_grad_kernel(place, dproj, weights, own, send):
    for i in range(2):
        part = nt(dproj[i * 512 : (i + 1) * 512, :], weights[...])

        @pl.when(place[3] == i)
        def _():
            own[...] = part

        @pl.when(place[3] != i)
        def _():
            send[...] = part.astype(BF)


def first_grad_rows(place, dproj, weights):
    return pl.pallas_call(
        first_grad_kernel,
        grid=(1,),
        in_specs=[
            SMEM,
            full((SEQ, 3 * HALF)),
            pl.BlockSpec((D, 3 * HALF), lambda i: (0, 0)),
        ],
        out_specs=[full((512, D)), full((512, D))],
        out_shape=[like((512, D), F32), like((512, D), BF)],
        compiler_params=params(24),
        cost_estimate=cost(2 * SEQ * D * 1152, 8 * 2**20),
    )(place, dproj, weights)


def input_grad_kernel(x, gain, middle_grad, own, other, gain_second, out, gains):
    xb = x[...].astype(F32)
    inverse = lax.rsqrt(jnp.mean(xb * xb, axis=1, keepdims=True) + EPS)
    unit = xb * inverse
    w = own[...] + other[...].astype(F32)
    a = w * gain[...]
    back = inverse * (a - unit * jnp.mean(a * unit, axis=1, keepdims=True))
    out[...] = (middle_grad[...] + back).astype(BF)
    gains[:, :D] = by_eight(w * unit)
    gains[:, D:] = gain_second[...]


def input_grad_rows(x, gain, middle_grad, own, other, gain_second):
    shapes = [(512, D), (1, D), (512, D), (512, D), (512, D), (8, D)]
    return pl.pallas_call(
        input_grad_kernel,
        in_specs=[full(s) for s in shapes],
        out_specs=[full((512, D)), full((8, 2 * D))],
        out_shape=[like((512, D), BF), like((8, 2 * D), F32)],
        compiler_params=params(24),
        cost_estimate=cost(10**7, 6 * 2**20),
    )(x, gain, middle_grad, own, other, gain_second)


def orthonormal(factors):
    rest, done = list(factors), [jnp.zeros_like(f) for f in factors]
    for k in range(RANK):
        for m, f in enumerate(factors):
            row = rest[m][k : k + 1]
            row = row * lax.rsqrt(jnp.sum(row * row, axis=1, keepdims=True) + EPS)
            here = lax.broadcasted_iota(jnp.int32, f.shape, 0) == k
            done[m] = jnp.where(here, row, done[m])
            if k < RANK - 1:
                rest[m] = rest[m] - jnp.sum(f * row, axis=1, keepdims=True) * row
    return done


def joined(mine, other, t):
    return jnp.concatenate(
        [jnp.where(t == 0, mine, other), jnp.where(t == 0, other, mine)], axis=1
    )


RIGHT_E = 5 * CHUNK
RIGHT_O = RIGHT_E + 2 * FF
RIGHT_S = RIGHT_O + D
RIGHT_G = RIGHT_S + D
RIGHT = RIGHT_G + 2 * D


def factor_kernel(place, mine, other, gains, h_i, h_o, h_e, h_s, *refs):
    left_i, left_o, left_e, left_s, right = refs[:5]
    sum_i, sum_o, sum_e, sum_s, sems = refs[5:]
    pairs = ((h_i, sum_i), (h_o, sum_o), (h_e, sum_e), (h_s, sum_s))
    copies = [pltpu.make_async_copy(h, v, sems.at[n]) for n, (h, v) in enumerate(pairs)]
    for c in copies:
        c.start()
    t = place[3]
    a, b = mine[...], other[...]
    both = a + b
    factors = [both[:, c * D : (c + 1) * D] for c in range(3)]
    factors.append(joined(a[:, LEFT_O], b[:, LEFT_O], t))
    at = LEFT_E.start
    factors += [both[:, at : at + D], both[:, at + D : at + 2 * D]]
    factors.append(joined(a[:, LEFT_S], b[:, LEFT_S], t))
    found = orthonormal(factors)
    own_o = jnp.where(t == 0, found[3][:, :HALF], found[3][:, HALF:])
    own_s = jnp.where(t == 0, found[6][:, :FF], found[6][:, FF:])
    left_o[...] = own_o
    left_s[...] = own_s
    for c in range(3):
        left_i[c] = found[c]
    for c in range(2):
        left_e[c] = found[4 + c]
    right[:, RIGHT_G:] = gains[...].astype(BF)
    for c in copies:
        c.wait()
    for c in range(3):
        right[:, c * HALF : (c + 1) * HALF] = folded(nn(two_terms(found[c]), sum_i[c])).astype(BF)
    right[:, 3 * HALF : RIGHT_E] = jnp.zeros((RANK, RIGHT_E - 3 * HALF), BF)
    for c in range(2):
        at = RIGHT_E + c * FF
        right[:, at : at + FF] = folded(nn(two_terms(found[4 + c]), sum_e[c])).astype(BF)
    right[:, RIGHT_O : RIGHT_O + D] = folded(nn(two_terms(own_o), sum_o[...])).astype(BF)
    right[:, RIGHT_S : RIGHT_S + D] = folded(nn(two_terms(own_s), sum_s[...])).astype(BF)


def factors_of(place, mine, other, gains, sum_i, sum_o, sum_e, sum_s):
    sums = (sum_i, sum_o, sum_e, sum_s)
    outs = [(3, RANK, D), (RANK, HALF), (2, RANK, D), (RANK, FF)]
    return pl.pallas_call(
        factor_kernel,
        in_specs=[SMEM, full((RANK, LEFT)), full((RANK, LEFT)), full((8, 2 * D))] + [HBM] * 4,
        out_specs=[full(s) for s in outs] + [full((RANK, RIGHT))],
        out_shape=[like(s, F32) for s in outs] + [like((RANK, RIGHT), BF)],
        scratch_shapes=[pltpu.VMEM(s.shape, BF) for s in sums] + [pltpu.SemaphoreType.DMA((4,))],
        compiler_params=params(24),
        cost_estimate=cost(10**8, 10 * 2**20),
    )(place, mine, other, gains, *sums)


def left_terms(v):
    one = v.astype(BF).astype(F32)
    two = v - one
    return jnp.concatenate([one, one, two, two], axis=0).astype(BF)


def right_terms(v):
    one = v.astype(BF).astype(F32)
    two = v - one
    return jnp.concatenate([one, two, one, two], axis=0).astype(BF)


def own_rows(terms, place):
    dp = (place[0] * 4 + place[1]) * 4 + place[2]
    row = lax.broadcasted_iota(jnp.int32, (16, D), 0)
    col = lax.broadcasted_iota(jnp.int32, (16, D), 1)
    pick = jnp.where((row < SHARD) & (col == row + SHARD * dp), 1.0, 0.0).astype(BF)
    return nt(pick, terms).astype(BF)


def moved(old, weight, rate, own, momentum, updated):
    new = momentum_decay * old + own
    momentum[...] = new
    updated[...] = weight - rate * new


LAST = 3


def last_kernel(place, *refs):
    left_i, left_o, left_e, left_s, sums, other, sum_i, sum_o, sum_e, sum_s = refs[:10]
    old_i, old_o, old_e, old_s, w_i, w_o, w_e, w_s, gains, old_g = refs[10:20]
    res_i, res_o, res_e, res_s, mom_i, mom_o, mom_e, mom_s, new_i, new_o, new_e, new_s = refs[20:32]
    right_i, right_o, right_e, right_s, mom_g, new_g = refs[32:38]
    l_i, l_o, l_e, l_s, r_i, r_o, r_e, r_s = refs[38:]
    j = pl.program_id(0)
    scale = 1.0 / 64
    tail = lambda n: (sums[:, RIGHT_O + n * D : RIGHT_O + (n + 1) * D] + other[:, n * D : (n + 1) * D])
    e_rights = [sums[:, RIGHT_E + c * FF : RIGHT_E + (c + 1) * FF] for c in range(2)]
    i_rights = [sums[:, c * HALF : (c + 1) * HALF] for c in range(3)]

    @pl.when(j == 0)
    def _():
        for c in range(2):
            l_e[c * D : (c + 1) * D, :] = left_terms(left_e[c]).T
            r_e[c] = right_terms(e_rights[c] * scale)
        l_s[...] = left_terms(left_s[...]).T
        r_s[...] = right_terms(tail(1) * scale)
        for c in range(3):
            l_i[c * D : (c + 1) * D, :] = left_terms(left_i[c]).T
            r_i[c] = right_terms(i_rights[c] * scale)
        l_o[...] = left_terms(left_o[...]).T
        r_o[...] = right_terms(tail(0) * scale)

    at = lambda n: pl.ds(pl.multiple_of(j * n, n), n)
    for h in range(2):
        rows = pl.ds(pl.multiple_of(j * 512 + h * 256, 256), 256)
        which = (2 * j + h) // 3
        here = slice(h * 256, (h + 1) * 256)
        res_e[here, :] = sum_e[here, :].astype(F32) - nn(l_e[rows, :], r_e[which])
    res_s[0] = sum_s[...].astype(F32) - nn(l_s[at(512), :], r_s[...])
    res_i[0, 0] = sum_i[0].astype(F32) - nn(l_i[at(D), :], r_i[j])
    res_o[0] = sum_o[...].astype(F32) - nn(l_o[at(128), :], r_o[...])

    @pl.when(j == 1)
    def _():
        for c in range(2):
            right_e[c] = e_rights[c] * scale
            own = nn(own_rows(left_terms(left_e[c]), place), r_e[c])[:SHARD]
            moved(old_e[:, c, :], w_e[:, c, :], rate_expand, own, mom_e.at[:, c, :], new_e.at[:, c, :])
        right_s[...] = tail(1) * scale
        own = nn(own_rows(r_s[...], place), left_terms(left_s[...]))[:SHARD]
        moved(old_s[...], w_s[...], rate_shrink, own, mom_s, new_s)
        for c in range(3):
            right_i[c] = i_rights[c] * scale
            own = nn(own_rows(left_terms(left_i[c]), place), r_i[c])[:SHARD]
            moved(old_i[c], w_i[c], rate_inbound, own, mom_i.at[c], new_i.at[c])
        right_o[...] = tail(0) * scale
        own = nn(own_rows(r_o[...], place), left_terms(left_o[...]))[:SHARD]
        moved(old_o[...], w_o[...], rate_outbound, own, mom_o, new_o)
        for n in range(2):
            own = jnp.sum(tail(2 + n), axis=0, keepdims=True)
            row = slice(n, n + 1)
            moved(old_g[row], gains[row], rate_gains, own, mom_g.at[row], new_g.at[row])


def last(place, lefts, sums, other, made, old, w, gains, old_g):
    rows = lambda n, w: pl.BlockSpec((n, w), lambda j: (j, 0))
    sum_i, sum_o, sum_e, sum_s = made
    made = (sum_i, sum_o, sum_e.reshape(2 * D, FF), sum_s)
    small = [*lefts, sums, other]
    states = [*old, *w, gains, old_g]
    state_shapes = [(3, SHARD, HALF), (SHARD, HALF), (SHARD, 2, FF), (SHARD, FF)]
    rest_shapes = [(1, 3, D, HALF), (1, HALF, D), (2 * D, FF), (1, FF, D)]
    tails = [(3, RANK, HALF), (RANK, D), (2, RANK, FF), (RANK, D), (2, D), (2, D)]
    flat = state_shapes * 2 + tails
    outs = pl.pallas_call(
        last_kernel,
        grid=(LAST,),
        in_specs=[SMEM]
        + [full(a.shape) for a in small]
        + [pl.BlockSpec((1, D, HALF), lambda j: (j, 0, 0)), rows(128, D), rows(512, FF), rows(512, D)]
        + [full(a.shape) for a in states],
        out_specs=[
            pl.BlockSpec((1, 1, D, HALF), lambda j: (0, j, 0, 0)),
            pl.BlockSpec((1, 128, D), lambda j: (0, j, 0)),
            rows(512, FF),
            pl.BlockSpec((1, 512, D), lambda j: (0, j, 0)),
        ]
        + [full(s) for s in flat],
        out_shape=[like(s, F32) for s in rest_shapes + flat],
        scratch_shapes=[
            pltpu.VMEM((3 * D, 32), BF),
            pltpu.VMEM((HALF, 32), BF),
            pltpu.VMEM((2 * D, 32), BF),
            pltpu.VMEM((FF, 32), BF),
            pltpu.VMEM((3, 32, HALF), BF),
            pltpu.VMEM((32, D), BF),
            pltpu.VMEM((2, 32, FF), BF),
            pltpu.VMEM((32, D), BF),
        ],
        compiler_params=params(28),
        cost_estimate=cost(10**8, 30 * 2**20),
    )(place, *small, *made, *states)
    return (*outs[:2], outs[2].reshape(1, 2, D, FF), *outs[3:])


def lane_tables(ids):
    zeros = jnp.sum((ids == 0).astype(jnp.int32))
    ones = jnp.sum((ids == 1).astype(jnp.int32))
    before = jnp.where(ids == 0, 0, jnp.where(ids == 1, zeros, zeros + ones))
    places = (jnp.arange(SEQ, dtype=jnp.int32) - before).astype(F32)
    lane = jnp.arange(128, dtype=jnp.int32)
    inverse = rope_base ** (-((lane % 32).astype(F32) * 2.0) / HEAD_DIM)
    angles = places[:, None] * inverse[None, :]
    first = (lane % 64 < 32)[None, :]
    sine = jnp.sin(angles)
    low, high = jnp.where(first, -sine, 0.0), jnp.where(first, 0.0, sine)
    kind = lane[None, :]
    same = ids[:, None] == kind
    fq = jnp.where((kind < 3) & same, 1.0, 0.0).astype(BF)
    fk = jnp.where(kind < 3, jnp.where(same, 0.0, MASKED), jnp.where(kind < 6, 1.0, 0.0))
    return (jnp.cos(angles), low, high), fq, fk.astype(BF)


def both_halves(own, t):
    other = swap(own)
    whole = jnp.zeros((SEQ, D), BF)
    whole = lax.dynamic_update_slice_in_dim(whole, own, t * 512, 0)
    return lax.dynamic_update_slice_in_dim(whole, other, (1 - t) * 512, 0)


def local(
    tokens,
    segment_ids,
    cotangent,
    norm_gains,
    gains_moment,
    inbound,
    outbound,
    expand,
    shrink,
    inbound_moment,
    outbound_moment,
    expand_moment,
    shrink_moment,
    inbound_error,
    outbound_error,
    expand_error,
    shrink_error,
    inbound_start,
    outbound_start,
    expand_start,
    shrink_start,
):
    y, x, z, t = (lax.axis_index(a) for a in DP_TENSOR)
    place = jnp.stack([y, x, z, t]).astype(jnp.int32)

    shard = weight_shard(inbound, outbound.T, jnp.swapaxes(expand, 0, 1), shrink.T)
    shard, segment_ids, tokens, cotangent = lax.optimization_barrier(
        (shard, segment_ids, tokens, cotangent)
    )
    column = [shard, shift(shard, Z, 1), shift(shard, Z, 3), shift(shard, Z, 2)]
    tables, fq, fk = lane_tables(segment_ids)
    column, fq, fk = lax.optimization_barrier((column, fq, fk))
    quarter, feed_rows = rows_of_column(place, column)
    feed_weights = lax.all_gather(feed_rows, (Y, X)).reshape(D, 3 * FF)
    x_all = both_halves(tokens, t)
    quarter = rows_of_plane(quarter)
    cot_all = both_halves(cotangent, t)
    near = shift(quarter, Z, 1), shift(quarter, Z, 3)
    near, x_all, cot_all, tables = lax.optimization_barrier((near, x_all, cot_all, tables))
    far = shift(near[0][:HALF], Z, 1), shift(near[1][HALF:], Z, 3)
    in_pieces = [quarter, *near, *far]

    gain_one, gain_two = norm_gains[0:1], norm_gains[1:2]
    normed, weights, q, k, v, att, fq_all, w_out = attention(
        place, gain_one, x_all, tables, fq, fk, in_pieces
    )
    w_other, att_other = swap(w_out), swap(att)

    start_e, start_s = jnp.swapaxes(expand_start, 1, 2), shrink_start.T
    sum_e, sum_s, left_e, left_s, middle, grad, hid = feed(
        place,
        gain_two,
        x_all,
        att,
        att_other,
        w_out,
        w_other,
        cot_all,
        expand_error,
        shrink_error,
        feed_weights,
        start_e,
        start_s,
    )
    grad_other = swap(grad)
    middle_grad, sum_o, dproj, sum_i, gain_second, left = backward(
        place,
        gain_two,
        outbound_start.T,
        jnp.swapaxes(inbound_start, 1, 2),
        grad_other,
        grad,
        middle,
        cot_all,
        att,
        w_out,
        outbound_error,
        q,
        k,
        v,
        fq_all,
        fk,
        *tables,
        normed,
        inbound_error,
        left_e,
        left_s,
    )

    left, dproj = lax.optimization_barrier((left, dproj))
    terms = ring_terms(left, Z)
    first_own, first_send = first_grad_rows(place, dproj, weights)
    terms, first_own, first_send = lax.optimization_barrier((terms, first_own, first_send))
    terms = ring_terms(rounded(ring_sum(terms)), X)
    first_other = swap(first_send)
    terms, first_other = lax.optimization_barrier((terms, first_other))
    terms = ring_terms(rounded(ring_sum(terms)), Y)
    input_grad, gains = input_grad_rows(
        tokens, gain_one, middle_grad, first_own, first_other, gain_second
    )
    terms, gains = lax.optimization_barrier((terms, gains))
    mine = ring_sum(terms)
    left_i, left_o, left_e, left_s, right = factors_of(
        place, mine, swap(mine), gains, sum_i, sum_o, sum_e, sum_s
    )

    right, hid = lax.optimization_barrier((right, hid))
    terms = ring_terms(right, Z)
    own_out, send_out = down_rows(place, hid, feed_weights)
    terms, own_out, send_out = lax.optimization_barrier((terms, own_out, send_out))
    terms = ring_terms(rounded(ring_sum(terms)), X)
    send_out = swap(send_out)
    terms, send_out = lax.optimization_barrier((terms, send_out))
    terms = ring_terms(rounded(ring_sum(terms)), Y)
    own_middle = lax.dynamic_slice_in_dim(middle, t * 512, 512, 0)
    layer_output = (own_middle + (own_out + send_out.astype(F32))).astype(BF)
    terms, layer_output = lax.optimization_barrier((terms, layer_output))
    sums = ring_sum(terms)
    (
        res_i,
        res_o,
        res_e,
        res_s,
        inbound_momentum,
        outbound_momentum,
        expand_momentum,
        shrink_momentum,
        inbound_updated,
        outbound_updated,
        expand_updated,
        shrink_updated,
        right_i,
        right_o,
        right_e,
        right_s,
        gains_momentum,
        gains_updated,
    ) = last(
        place,
        (left_i, left_o, left_e, left_s),
        sums,
        swap(sums[:, RIGHT_O:]),
        (sum_i, sum_o, sum_e, sum_s),
        (inbound_moment, outbound_moment.T, jnp.swapaxes(expand_moment, 0, 1), shrink_moment.T),
        (inbound, outbound.T, jnp.swapaxes(expand, 0, 1), shrink.T),
        norm_gains,
        gains_moment,
    )
    return (
        layer_output,
        input_grad,
        gains_momentum,
        gains_updated,
        inbound_momentum,
        outbound_momentum.T,
        jnp.swapaxes(expand_momentum, 0, 1),
        shrink_momentum.T,
        inbound_updated,
        outbound_updated.T,
        jnp.swapaxes(expand_updated, 0, 1),
        shrink_updated.T,
        res_i,
        res_o,
        res_e,
        res_s,
        jnp.swapaxes(left_i, 1, 2),
        jnp.swapaxes(right_i, 1, 2),
        left_o.T,
        right_o.T,
        jnp.swapaxes(left_e, 1, 2),
        jnp.swapaxes(right_e, 1, 2),
        left_s.T,
        right_s.T,
    )


def solution(mesh):
    torus = Mesh(mesh.devices.reshape(4, 4, 4, mesh.shape["tensor"]), DP_TENSOR)
    return jax.shard_map(
        local,
        mesh=torus,
        in_specs=(
            P(DP_TENSOR, None),
            P(DP),
            P(DP_TENSOR, None),
            P(),
            P(),
            P(None, DP, T),
            P(T, DP),
            P(None, DP, T),
            P(T, DP),
            P(None, DP, T),
            P(T, DP),
            P(None, DP, T),
            P(T, DP),
            P(DP, None, None, T),
            P(DP, T, None),
            P(DP, None, None, T),
            P(DP, T, None),
            P(None, T, None),
            P(),
            P(None, T, None),
            P(),
        ),
        out_specs=(
            P(DP_TENSOR, None),
            P(DP_TENSOR, None),
            P(),
            P(),
            P(None, DP, T),
            P(T, DP),
            P(None, DP, T),
            P(T, DP),
            P(None, DP, T),
            P(T, DP),
            P(None, DP, T),
            P(T, DP),
            P(DP, None, None, T),
            P(DP, T, None),
            P(DP, None, None, T),
            P(DP, T, None),
            P(),
            P(None, T, None),
            P(T, None),
            P(),
            P(),
            P(None, T, None),
            P(T, None),
            P(),
        ),
        check_vma=False,
    )
```

```python
import jax
import jax.numpy as jnp
from jax import lax
from jax.experimental import pallas as pl
from jax.experimental.pallas import tpu as pltpu
from jax.sharding import Mesh
from jax.sharding import PartitionSpec as P

Y, X, Z, T = "dp_0", "dp_1", "dp_2", "tensor"
DP = (Y, X, Z)
DP_TENSOR = (Y, X, Z, T)
F32, BF = jnp.float32, jnp.bfloat16

SEQ = 1024
D = 768
HEAD_DIM = 64
HALF = 384
FF = 1536
RANK = 8
BLOCK = 256
SHARD = 12
CHUNK = 256
CHUNKS = FF // CHUNK
WIDE = 512
WIDES = FF // WIDE
EPS = 1e-06
MASKED = -1e30

momentum_decay = 0.9
rate_inbound = 0.2
rate_outbound = 6.0
rate_expand = 0.3
rate_shrink = 0.25
rate_gains = 0.0005
rope_base = 10000.0

ANY = pl.BlockSpec(memory_space=pl.ANY)
HBM = pl.BlockSpec(memory_space=pltpu.HBM)
SMEM = pl.BlockSpec(memory_space=pltpu.SMEM)


def nn(a, b):
    return jnp.dot(a, b, preferred_element_type=F32)


def nt(a, b):
    return lax.dot_general(a, b, (((1,), (1,)), ((), ())), preferred_element_type=F32)


def tn(a, b):
    return lax.dot_general(a, b, (((0,), (0,)), ((), ())), preferred_element_type=F32)


def params(mib=56):
    return pltpu.CompilerParams(vmem_limit_bytes=mib * 2**20)


def cost(flops, moved):
    return pl.CostEstimate(flops=flops // 64, bytes_accessed=moved // 64, transcendentals=0)


def full(shape):
    return pl.BlockSpec(shape, lambda *_: (0,) * len(shape))


def like(shape, dtype):
    return jax.ShapeDtypeStruct(shape, dtype)


def shift(v, axis, d):
    n = lax.axis_size(axis)
    return lax.ppermute(v, axis, [(i, (i + d) % n) for i in range(n)])


def swap(v):
    return lax.ppermute(v, T, [(0, 1), (1, 0)])


def rounded(v):
    return lax.reduce_precision(v, exponent_bits=8, mantissa_bits=7)


def ring_terms(v, axis):
    low = v.astype(BF)
    return v, shift(low, axis, 2), shift(low, axis, 1), shift(low, axis, 3)


def ring_sum(terms):
    own, two, one, back = (v.astype(F32) for v in terms)
    return (own + two) + (one + back)


def shard_kernel(inbound, outbound, expand, shrink, out):
    for c in range(3):
        out[:, c * HALF : (c + 1) * HALF] = inbound[c].astype(BF)
    out[:, 1152:1536] = outbound[...].astype(BF)
    for j in range(WIDES):
        for c in range(2):
            at = 1536 + (2 * j + c) * WIDE
            out[:, at : at + WIDE] = expand[:, c, j * WIDE : (j + 1) * WIDE].astype(BF)
    out[:, 4608:] = shrink[...].astype(BF)


def weight_shard(inbound, outbound, expand, shrink):
    return pl.pallas_call(
        shard_kernel,
        out_shape=like((SHARD, 6144), BF),
        compiler_params=params(),
        cost_estimate=cost(10**5, 2**19),
    )(inbound, outbound, expand, shrink)


def column_kernel(place, own, one, back, two, quarter, feed, rows):
    z = place[2]
    pieces = [r[...].astype(F32) for r in (own, one, two, back)]
    for p in range(4):
        away = lax.rem(p + 4 - z, 4)
        piece = jnp.where(
            away == 0,
            pieces[0],
            jnp.where(away == 3, pieces[1], jnp.where(away == 2, pieces[2], pieces[3])),
        )
        rows[p * SHARD : (p + 1) * SHARD, :] = piece
    quarter[...] = rows[:, pl.ds(pl.multiple_of(z * HALF, 128), HALF)].astype(BF)
    feed[...] = rows[:, 1536:].astype(BF)


def rows_of_column(place, pieces):
    widths = (HALF, 3 * FF)
    return pl.pallas_call(
        column_kernel,
        in_specs=[SMEM] + [full(pieces[0].shape)] * 4,
        out_specs=[full((48, w)) for w in widths],
        out_shape=[like((48, w), BF) for w in widths],
        scratch_shapes=[pltpu.VMEM((48, 6144), F32)],
        compiler_params=params(16),
        cost_estimate=cost(10**6, 2**21),
    )(place, *pieces)


def rows_of_plane(v):
    everyone = jnp.broadcast_to(v[None], (16, *v.shape))
    rows = lax.all_to_all(everyone, (Y, X), 0, 0, tiled=True)
    return rows.reshape(16 * v.shape[0], v.shape[1])


def place_pieces(pieces, target, sems, place):
    copies = []
    spots = ((0, 0), (3, 0), (1, 0), (2, 0), (2, HALF))
    for n, (piece, (away, row)) in enumerate(zip(pieces, spots)):
        at = pl.multiple_of(lax.rem(place[2] + away, 4) * HALF, 128)
        spot = target.at[pl.ds(row, piece.shape[0]), pl.ds(at, HALF)]
        copies.append(pltpu.make_async_copy(piece, spot, sems.at[n]))
    return copies


def turn_lanes(v, cos, low, high):
    return v * cos + pltpu.roll(v, 96, 1) * low + pltpu.roll(v, 32, 1) * high


def head_lanes(rows, h):
    lane = lax.broadcasted_iota(jnp.int32, (rows, 128), 1)
    return (lane < 64) if h == 0 else (lane >= 64)


def three_terms(v):
    one = v.astype(BF).astype(F32)
    two = (v - one).astype(BF).astype(F32)
    return one, two, v - one - two


def both_heads(v):
    zero = jnp.zeros((), BF)
    return [jnp.where(head_lanes(v.shape[0], h), v, zero) for h in range(2)]


def pair_forward(q, k, v, fq, fk, out, fq_out):
    keys = jnp.concatenate([k[...], fk[...]], axis=1)
    vals = v[...]
    lane = lax.broadcasted_iota(jnp.int32, (256, 128), 1)
    first = head_lanes(256, 0)
    scores = []
    for b in range(4):
        rows = slice(b * 256, (b + 1) * 256)
        f = fq[rows, :]
        heads = [jnp.concatenate([m, f], axis=1) for m in both_heads(q[rows, :])]
        scores.append(nt(jnp.concatenate(heads, axis=0), keys[: (b + 1) * 256]))
    for b in range(4):
        rows = slice(b * 256, (b + 1) * 256)
        s = scores[b]
        largest = jnp.max(s, axis=1, keepdims=True)
        e = jnp.exp(s - largest)
        sums = jnp.sum(e, axis=1, keepdims=True)
        o = nn(e.astype(BF), vals[: (b + 1) * 256]) * (1.0 / sums)
        out[rows, :] = jnp.where(first, o[:256], o[256:]).astype(BF)
        one, two, three = three_terms(-(largest + jnp.log(sums)))
        for h in range(2):
            at = slice(h * 256, (h + 1) * 256)
            extra = jnp.where(lane == 3, one[at], jnp.where(lane == 4, two[at], three[at]))
            fq_out[h, rows, :] = jnp.where((lane >= 3) & (lane < 6), extra.astype(BF), fq[rows, :])


def attention_kernel(place, gain, *refs):
    hbm_in, pieces, hbm_out, refs = refs[:6], refs[6:11], refs[11:19], refs[19:]
    held, made, refs = refs[:6], refs[6:13], refs[13:]
    piece_sems, in_sems, out_sems, pair_sems = refs
    x, cos, low, high, fq, fk = held
    normed, weights, q, k, v, att, fq_all = made
    copy = pltpu.make_async_copy
    gets = [copy(hbm_in[0].at[pl.ds(i * 512, 512)], x.at[pl.ds(i * 512, 512)], in_sems.at[i]) for i in range(2)]
    gets += [copy(h, r, in_sems.at[n + 2]) for n, (h, r) in enumerate(zip(hbm_in[1:], held[1:]))]
    puts = [copy(r, h, out_sems.at[n]) for n, (r, h) in enumerate(zip(made[:5], hbm_out))]
    put_out = copy(weights.at[:, pl.ds(3 * HALF, HALF)], hbm_out[7], out_sems.at[7])

    def put_pair(p):
        lanes = pl.ds(pl.multiple_of(p * 128, 128), 128)
        heads = pl.ds(2 * p, 2)
        return (
            copy(att.at[:, lanes], hbm_out[5].at[:, lanes], pair_sems.at[0, p]),
            copy(fq_all.at[heads], hbm_out[6].at[heads], pair_sems.at[1, p]),
        )

    placed = place_pieces(pieces, weights, piece_sems, place)
    for c in gets[:2] + placed + gets[2:]:
        c.start()
    for i in range(2):
        rows = slice(i * 512, (i + 1) * 512)
        gets[i].wait()
        xb = x[rows, :].astype(F32)
        inverse = lax.rsqrt(jnp.mean(xb * xb, axis=1, keepdims=True) + EPS)
        n = (xb * inverse * gain[...]).astype(BF)
        x[rows, :] = n
        normed[:, rows] = n.T
    puts[0].start()
    for c in placed:
        c.wait()
    puts[1].start()
    put_out.start()
    for c in gets[2:]:
        c.wait()
    for i in range(2):
        rows = slice(i * 512, (i + 1) * 512)
        found = nn(x[rows, :], weights[:, :1152])
        tables = cos[rows, :], low[rows, :], high[rows, :]
        v[rows, :] = found[:, 768:].astype(BF)
        for p in range(3):
            at = slice(p * 128, (p + 1) * 128)
            q[rows, at] = (turn_lanes(found[:, at], *tables) * 0.125).astype(BF)
            k_lanes = found[:, HALF + p * 128 : HALF + (p + 1) * 128]
            k[rows, at] = turn_lanes(k_lanes, *tables).astype(BF)
    for c in puts[2:5]:
        c.start()

    def one_pair(p, carry):
        lanes = pl.ds(pl.multiple_of(p * 128, 128), 128)
        views = [r.at[:, lanes] for r in (q, k, v)]
        pair_forward(*views, fq, fk, att.at[:, lanes], fq_all.at[pl.ds(2 * p, 2)])
        for c in put_pair(p):
            c.start()
        return carry

    lax.fori_loop(0, 3, one_pair, 0)
    put_out.wait()
    for c in puts[:5]:
        c.wait()
    for p in range(3):
        for c in put_pair(p):
            c.wait()


def attention(place, gain, x, tables, fq, fk, pieces):
    arrays = (x, *tables, fq, fk)
    half = like((SEQ, HALF), BF)
    outs = [like((D, SEQ), BF), like((D, 2 * D), BF), half, half, half, half, like((6, SEQ, 128), BF)]
    return pl.pallas_call(
        attention_kernel,
        in_specs=[SMEM, full((1, D))] + [HBM] * 11,
        out_specs=[HBM] * 8,
        out_shape=[*outs, like((D, HALF), BF)],
        scratch_shapes=[pltpu.VMEM(a.shape, a.dtype) for a in arrays]
        + [pltpu.VMEM(o.shape, o.dtype) for o in outs]
        + [
            pltpu.SemaphoreType.DMA((5,)),
            pltpu.SemaphoreType.DMA((7,)),
            pltpu.SemaphoreType.DMA((8,)),
            pltpu.SemaphoreType.DMA((2, 3)),
        ],
        compiler_params=params(),
        cost_estimate=cost(10**10, 12 * 2**20),
    )(place, gain, *arrays, *pieces)


def two_terms(v):
    one = v.astype(BF).astype(F32)
    return jnp.concatenate([one, v - one], axis=0).astype(BF)


def folded(v):
    return v[0:8] + v[8:16]


def feed_kernel(place, gain, *refs):
    h_x, h_att, h_other, h_w, h_w_other, h_cot, h_err_e, h_err_s, h_feed = refs[:9]
    start_e, start_s, sum_e, sum_s, left_e, left_s = refs[9:15]
    h_middle, h_grad, h_hid = refs[15:18]
    x, att, other, w_out, w_other, cot, both, down, err_e, err_s = refs[18:28]
    middle, second, turned, hid, grads, grad_low = refs[28:34]
    rows_sem, in_sem, both_sem, down_sem, err_sem, out_sem = refs[34:]
    j = pl.program_id(0)
    copy = pltpu.make_async_copy

    def lanes(n, width, start=0):
        return pl.ds(pl.multiple_of(start + n * width, width), width)

    def get_rows(i):
        rows = pl.ds(i * 512, 512)
        trio = ((h_x, x), (h_att, att), (h_other, other))
        return [copy(h.at[rows], r.at[rows], rows_sem.at[n, i]) for n, (h, r) in enumerate(trio)]

    def get_both(n):
        at = lanes(n, 2 * WIDE)
        return copy(h_feed.at[:, at], both.at[:, at], both_sem.at[n])

    def get_down(n):
        return copy(h_feed.at[:, lanes(n, WIDE, 2 * FF)], down.at[:, lanes(n, WIDE)], down_sem.at[n])

    def get_err(n):
        slot = lax.rem(n, 2)
        return (
            copy(h_err_e.at[0, :, :, lanes(n, WIDE)], err_e.at[slot], err_sem.at[0, slot]),
            copy(h_err_s.at[0, lanes(n, WIDE)], err_s.at[slot], err_sem.at[1, slot]),
        )

    get_w = copy(h_w, w_out, in_sem.at[0])
    get_w_other = copy(h_w_other, w_other, in_sem.at[1])
    get_cot = copy(h_cot, cot, in_sem.at[2])
    put_middle = copy(middle, h_middle, out_sem.at[0])
    put_grad = copy(grad_low, h_grad, out_sem.at[1])
    put_hid = copy(hid, h_hid, out_sem.at[2])

    @pl.when(j == 0)
    def _():
        order = [get_w, get_w_other, *get_rows(0), *get_rows(1), get_both(0), get_cot, get_down(0)]
        for c in order + [*get_err(0)]:
            c.start()
        for n in range(1, WIDES):
            get_both(n).start()
            get_down(n).start()
            if n == 1:
                for c in get_err(n):
                    c.start()
        left_e[...] = jnp.zeros_like(left_e)
        get_w.wait()
        get_w_other.wait()
        for i in range(2):
            rows = slice(i * 512, (i + 1) * 512)
            for c in get_rows(i):
                c.wait()
            m = x[rows, :].astype(F32) + nt(att[rows, :], w_out[...]) + nt(other[rows, :], w_other[...])
            middle[rows, :] = m
            inverse = lax.rsqrt(jnp.mean(m * m, axis=1, keepdims=True) + EPS)
            low = (m * inverse * gain[...]).astype(BF)
            second[rows, :] = low
            turned[:, rows] = low.T
        put_middle.start()

    get_both(j).wait()
    w_both = both.at[:, lanes(j, 2 * WIDE)]
    w_down = down.at[:, lanes(j, WIDE)]
    my_hid = hid.at[:, lanes(j, WIDE)]
    my_grads = grads.at[:, lanes(j, 2 * WIDE)]
    step = FEED_ROWS
    found = []
    for b in range(SEQ // step):
        found.append(nn(second[b * step : (b + 1) * step, :], w_both[...]))

    @pl.when(j == 0)
    def _():
        get_cot.wait()

    get_down(j).wait()
    for b in range(SEQ // step):
        rows = slice(b * step, (b + 1) * step)
        gu, hg = found[b], nn(cot[rows, :], w_down[...])
        g, u = gu[:, :WIDE], gu[:, WIDE:]
        sig = 0.5 * jnp.tanh(0.5 * g) + 0.5
        act = g * sig
        my_hid[rows, :] = (act * u).astype(BF)
        my_grads[rows, :WIDE] = (hg * u * (sig + act * (1.0 - sig))).astype(BF)
        my_grads[rows, WIDE:] = (hg * act).astype(BF)

    @pl.when(j == WIDES - 1)
    def _():
        put_hid.start()
        grad_low[...] = nt(grads[...], both[...]).astype(BF)
        put_grad.start()

    for c in get_err(j):
        c.wait()
    slot = lax.rem(j, 2)
    low = (tn(my_hid[...], cot[...]) + err_s[slot]).astype(BF)
    sum_s[...] = low
    left_s[...] = folded(nt(two_terms(start_s[...]), low))
    made = nn(turned[...], my_grads[...])
    for c in range(2):
        low = (made[:, c * WIDE : (c + 1) * WIDE] + err_e[slot, c]).astype(BF)
        sum_e[c] = low
        left_e[:, c * D : (c + 1) * D] += folded(nt(two_terms(start_e[c]), low))

    @pl.when(j + 2 < WIDES)
    def _():
        for c in get_err(j + 2):
            c.start()

    @pl.when(j == WIDES - 1)
    def _():
        put_middle.wait()
        put_hid.wait()
        put_grad.wait()


FEED_ROWS = 256
FEED_MIB = 56


def feed(place, gain, x, att, other, weights, w_other, cot, err_e, err_s, feed_weights, start_e, start_s):
    arrays = (x, att, other, weights, w_other, cot, err_e, err_s, feed_weights)
    return pl.pallas_call(
        feed_kernel,
        grid=(WIDES,),
        in_specs=[SMEM, full((1, D)), HBM, HBM, ANY, HBM, ANY]
        + [HBM] * 4
        + [pl.BlockSpec((2, RANK, WIDE), lambda j: (0, 0, j)), full((RANK, D))],
        out_specs=[
            pl.BlockSpec((2, D, WIDE), lambda j: (0, 0, j)),
            pl.BlockSpec((WIDE, D), lambda j: (j, 0)),
            full((RANK, 2 * D)),
            pl.BlockSpec((RANK, WIDE), lambda j: (0, j)),
            HBM,
            HBM,
            HBM,
        ],
        out_shape=[
            like((2, D, FF), BF),
            like((FF, D), BF),
            like((RANK, 2 * D), F32),
            like((RANK, FF), F32),
            like((SEQ, D), F32),
            like((SEQ, D), BF),
            like((SEQ, FF), BF),
        ],
        scratch_shapes=[
            pltpu.VMEM((SEQ, D), BF),
            pltpu.VMEM((SEQ, HALF), BF),
            pltpu.VMEM((SEQ, HALF), BF),
            pltpu.VMEM((D, HALF), BF),
            pltpu.VMEM((D, HALF), BF),
            pltpu.VMEM((SEQ, D), BF),
            pltpu.VMEM((D, 2 * FF), BF),
            pltpu.VMEM((D, FF), BF),
            pltpu.VMEM((2, 2, D, WIDE), F32),
            pltpu.VMEM((2, WIDE, D), F32),
            pltpu.VMEM((SEQ, D), F32),
            pltpu.VMEM((SEQ, D), BF),
            pltpu.VMEM((D, SEQ), BF),
            pltpu.VMEM((SEQ, FF), BF),
            pltpu.VMEM((SEQ, 2 * FF), BF),
            pltpu.VMEM((SEQ, D), BF),
            pltpu.SemaphoreType.DMA((3, 2)),
            pltpu.SemaphoreType.DMA((3,)),
            pltpu.SemaphoreType.DMA((WIDES,)),
            pltpu.SemaphoreType.DMA((WIDES,)),
            pltpu.SemaphoreType.DMA((2, 2)),
            pltpu.SemaphoreType.DMA((3,)),
        ],
        compiler_params=params(FEED_MIB),
        cost_estimate=cost(18 * SEQ * D * FF, 40 * 2**20),
    )(place, gain, *arrays, start_e, start_s)


def down_kernel(place, hid, weights, own, send):
    t = place[3]
    for i in range(2):
        part = nt(hid[i * 512 : (i + 1) * 512, :], weights[...])

        @pl.when(t == i)
        def _():
            own[...] = part

        @pl.when(t != i)
        def _():
            send[...] = part.astype(BF)


def down_rows(place, hid, weights):
    return pl.pallas_call(
        down_kernel,
        grid=(1,),
        in_specs=[SMEM, full((SEQ, FF)), pl.BlockSpec((D, FF), lambda j: (0, 2))],
        out_specs=[full((512, D)), full((512, D))],
        out_shape=[like((512, D), F32), like((512, D), BF)],
        compiler_params=params(24),
        cost_estimate=cost(2 * SEQ * D * FF, 8 * 2**20),
    )(place, hid, weights)


def by_eight(v):
    return jnp.sum(v.reshape(-1, 8, v.shape[1]), axis=0)


LEFT_O = slice(3 * D, 3 * D + HALF)
LEFT_E = slice(3 * D + HALF, 5 * D + HALF)
LEFT_S = slice(5 * D + HALF, 5 * D + HALF + FF)
LEFT = 5 * D + HALF + FF


def pair_back(q, k, v, att, grad, fq, fk, cos, low, high, out, dk_acc, dv_acc):
    lane = lax.broadcasted_iota(jnp.int32, (256, 128), 1)
    ones = jnp.where(lax.broadcasted_iota(jnp.int32, (SEQ, 128), 1) < 3, 1.0, 0.0).astype(BF)
    keys = jnp.concatenate([k[...], fk[...]], axis=1)
    vals = jnp.concatenate([v[...], ones], axis=1)
    kt = k[...].T
    dk_acc[...] = jnp.zeros_like(dk_acc)
    dv_acc[...] = jnp.zeros_like(dv_acc)
    for b in range(4):
        rows = slice(b * 256, (b + 1) * 256)
        count = (b + 1) * 256
        qs, gs = both_heads(q[rows, :]), both_heads(grad[rows, :])
        q_rows = [jnp.concatenate([qs[h], fq[h, rows, :]], axis=1) for h in range(2)]
        g_rows = []
        for h in range(2):
            centre = jnp.sum(gs[h].astype(F32) * att[rows, :].astype(F32), axis=1, keepdims=True)
            one, two, three = three_terms(-centre)
            extra = jnp.where(lane == 0, one, jnp.where(lane == 1, two, three))
            fg = jnp.where(lane < 3, extra, 0.0).astype(BF)
            g_rows.append(jnp.concatenate([gs[h], fg], axis=1))
        soft = jnp.exp(nt(keys[:count], jnp.concatenate(q_rows, axis=0)))
        ds = (soft * nt(vals[:count], jnp.concatenate(g_rows, axis=0))).astype(BF)
        dv_acc[:count, :] += nn(soft.astype(BF), jnp.concatenate(gs, axis=0))
        dk_acc[:count, :] += nn(ds, jnp.concatenate(qs, axis=0))
        part = nn(kt[:, :count], ds)
        dq = jnp.concatenate([part[:64, :256], part[64:, 256:]], axis=0).T * 0.125
        out[0][rows, :] = turn_lanes(dq, cos[rows, :], -low[rows, :], -high[rows, :]).astype(BF)
    out[1][...] = turn_lanes(dk_acc[...], cos[...], -low[...], -high[...]).astype(BF)
    out[2][...] = dv_acc[...].astype(BF)


def backward_kernel(place, gain, start_o, start_i, grad_other, *refs):
    hbm_in, hbm_out, refs = refs[:18], refs[18:22], refs[22:]
    gain_sum, left = refs[:2]
    held, made, refs = refs[2:20], refs[20:24], refs[24:]
    att_grad, acc, dk_acc, dv_acc, in_sems, out_sems = refs
    grad, middle, cot, att, w_out, err_o, q, k, v, fq, fk, cos, low, high, turned, err_i, left_e, left_s = held
    middle_grad, sum_o, dproj, sum_i = made
    copy = pltpu.make_async_copy
    gets = []
    for n in range(3):
        for i in range(2):
            rows = pl.ds(i * 512, 512)
            gets.append(copy(hbm_in[n].at[rows], held[n].at[rows], in_sems.at[2 * n + i]))
    for n in range(3, 18):
        gets.append(copy(hbm_in[n], held[n], in_sems.at[n + 3]))
    puts = [copy(m, h, out_sems.at[n]) for n, (m, h) in enumerate(zip(made, hbm_out))]
    for c in gets[0:6:2] + gets[6:8] + gets[1:6:2] + gets[8:]:
        c.start()

    for i in range(2):
        for c in gets[i:6:2]:
            c.wait()
        if i == 0:
            for c in gets[6:8]:
                c.wait()
        rows = slice(i * 512, (i + 1) * 512)
        m = middle[rows, :]
        inverse = lax.rsqrt(jnp.mean(m * m, axis=1, keepdims=True) + EPS)
        unit = m * inverse
        w = grad[rows, :].astype(F32) + grad_other[rows, :].astype(F32)
        a = w * gain[...]
        back = inverse * (a - unit * jnp.mean(a * unit, axis=1, keepdims=True))
        mg = cot[rows, :].astype(F32) + back
        branch = mg.astype(BF)
        att_grad[rows, :] = nn(branch, w_out[...]).astype(BF)
        part = tn(att[rows, :], branch)
        if i == 0:
            acc[...] = part
        else:
            acc[...] += part

        @pl.when(place[3] == i)
        def _():
            middle_grad[...] = mg
            gain_sum[...] = by_eight(w * unit)

    puts[0].start()
    gets[8].wait()
    summed = (acc[...] + err_o[0]).astype(BF)
    sum_o[...] = summed
    puts[1].start()
    left[:, LEFT_O] = folded(nt(two_terms(start_o[...]), summed)).astype(BF)

    for c in gets[9:17]:
        c.wait()

    def one_pair(p, carry):
        lanes = pl.ds(pl.multiple_of(p * 128, 128), 128)
        pair_back(
            *(r.at[:, lanes] for r in (q, k, v, att, att_grad)),
            fq.at[pl.ds(2 * p, 2)],
            fk,
            cos,
            low,
            high,
            [dproj.at[:, pl.ds(pl.multiple_of(c * HALF + p * 128, 128), 128)] for c in range(3)],
            dk_acc,
            dv_acc,
        )
        return carry

    lax.fori_loop(0, 3, one_pair, 0)
    puts[2].start()

    for c in gets[17:]:
        c.wait()
    left[:, LEFT_E] = left_e[...].astype(BF)
    left[:, LEFT_S] = left_s[...].astype(BF)
    found = nn(turned[...], dproj[...])
    for c in range(3):
        summed = (found[:, c * HALF : (c + 1) * HALF] + err_i[0, c]).astype(BF)
        sum_i[c] = summed
        left[:, c * D : (c + 1) * D] = folded(nt(two_terms(start_i[c]), summed)).astype(BF)
    puts[3].start()
    for c in puts:
        c.wait()


BACK_MIB = 60


def backward(place, gain, start_o, start_i, grad_other, *arrays):
    small = (gain, start_o, start_i, grad_other)
    outs = [like((512, D), F32), like((HALF, D), BF), like((SEQ, 3 * HALF), BF), like((3, D, HALF), BF)]
    return pl.pallas_call(
        backward_kernel,
        in_specs=[SMEM] + [full(a.shape) for a in small] + [HBM] * 18,
        out_specs=[HBM] * 4 + [full((8, D)), full((RANK, LEFT))],
        out_shape=outs + [like((8, D), F32), like((RANK, LEFT), BF)],
        scratch_shapes=[pltpu.VMEM(a.shape, a.dtype) for a in arrays]
        + [pltpu.VMEM(o.shape, o.dtype) for o in outs]
        + [
            pltpu.VMEM((SEQ, HALF), BF),
            pltpu.VMEM((HALF, D), F32),
            pltpu.VMEM((SEQ, 128), F32),
            pltpu.VMEM((SEQ, 128), F32),
            pltpu.SemaphoreType.DMA((21,)),
            pltpu.SemaphoreType.DMA((4,)),
        ],
        compiler_params=params(BACK_MIB),
        cost_estimate=cost(20 * 10**9, 30 * 2**20),
    )(place, *small, *arrays)


def first_grad_kernel(place, dproj, weights, own, send):
    for i in range(2):
        part = nt(dproj[i * 512 : (i + 1) * 512, :], weights[...])

        @pl.when(place[3] == i)
        def _():
            own[...] = part

        @pl.when(place[3] != i)
        def _():
            send[...] = part.astype(BF)


def first_grad_rows(place, dproj, weights):
    return pl.pallas_call(
        first_grad_kernel,
        grid=(1,),
        in_specs=[
            SMEM,
            full((SEQ, 3 * HALF)),
            pl.BlockSpec((D, 3 * HALF), lambda i: (0, 0)),
        ],
        out_specs=[full((512, D)), full((512, D))],
        out_shape=[like((512, D), F32), like((512, D), BF)],
        compiler_params=params(24),
        cost_estimate=cost(2 * SEQ * D * 1152, 8 * 2**20),
    )(place, dproj, weights)


def input_grad_kernel(x, gain, middle_grad, own, other, gain_second, out, gains):
    xb = x[...].astype(F32)
    inverse = lax.rsqrt(jnp.mean(xb * xb, axis=1, keepdims=True) + EPS)
    unit = xb * inverse
    w = own[...] + other[...].astype(F32)
    a = w * gain[...]
    back = inverse * (a - unit * jnp.mean(a * unit, axis=1, keepdims=True))
    out[...] = (middle_grad[...] + back).astype(BF)
    gains[:, :D] = by_eight(w * unit)
    gains[:, D:] = gain_second[...]


def input_grad_rows(x, gain, middle_grad, own, other, gain_second):
    shapes = [(512, D), (1, D), (512, D), (512, D), (512, D), (8, D)]
    return pl.pallas_call(
        input_grad_kernel,
        in_specs=[full(s) for s in shapes],
        out_specs=[full((512, D)), full((8, 2 * D))],
        out_shape=[like((512, D), BF), like((8, 2 * D), F32)],
        compiler_params=params(24),
        cost_estimate=cost(10**7, 6 * 2**20),
    )(x, gain, middle_grad, own, other, gain_second)


def orthonormal(factors):
    rest, done = list(factors), [jnp.zeros_like(f) for f in factors]
    for k in range(RANK):
        for m, f in enumerate(factors):
            row = rest[m][k : k + 1]
            row = row * lax.rsqrt(jnp.sum(row * row, axis=1, keepdims=True) + EPS)
            here = lax.broadcasted_iota(jnp.int32, f.shape, 0) == k
            done[m] = jnp.where(here, row, done[m])
            if k < RANK - 1:
                rest[m] = rest[m] - jnp.sum(f * row, axis=1, keepdims=True) * row
    return done


def joined(mine, other, t):
    return jnp.concatenate(
        [jnp.where(t == 0, mine, other), jnp.where(t == 0, other, mine)], axis=1
    )


RIGHT_E = 5 * CHUNK
RIGHT_O = RIGHT_E + 2 * FF
RIGHT_S = RIGHT_O + D
RIGHT_G = RIGHT_S + D
RIGHT = RIGHT_G + 256


def factor_kernel(place, mine, other, gains, h_i, h_o, h_e, h_s, *refs):
    left_i, left_o, left_e, left_s, right = refs[:5]
    sum_i, sum_o, sum_e, sum_s, sems = refs[5:]
    pairs = ((h_i, sum_i), (h_o, sum_o), (h_e, sum_e), (h_s, sum_s))
    copies = [pltpu.make_async_copy(h, v, sems.at[n]) for n, (h, v) in enumerate(pairs)]
    for c in copies:
        c.start()
    t = place[3]
    a, b = mine[...], other[...]
    both = a + b
    factors = [both[:, c * D : (c + 1) * D] for c in range(3)]
    factors.append(joined(a[:, LEFT_O], b[:, LEFT_O], t))
    at = LEFT_E.start
    factors += [both[:, at : at + D], both[:, at + D : at + 2 * D]]
    factors.append(joined(a[:, LEFT_S], b[:, LEFT_S], t))
    found = orthonormal(factors)
    own_o = jnp.where(t == 0, found[3][:, :HALF], found[3][:, HALF:])
    own_s = jnp.where(t == 0, found[6][:, :FF], found[6][:, FF:])
    left_o[...] = own_o
    left_s[...] = own_s
    for c in range(3):
        left_i[c] = found[c]
    for c in range(2):
        left_e[c] = found[4 + c]
    total = jnp.sum(gains[...], axis=0, keepdims=True)
    parts = [total[:, n * 128 : (n + 1) * 128] for n in range(12)]
    parts += [jnp.zeros((1, 128), F32)] * 4
    for n in range(2):
        packed = jnp.concatenate(parts[n * 8 : (n + 1) * 8], axis=0)
        right[:, RIGHT_G + n * 128 : RIGHT_G + (n + 1) * 128] = packed.astype(BF)
    for c in copies:
        c.wait()
    for c in range(3):
        right[:, c * HALF : (c + 1) * HALF] = folded(nn(two_terms(found[c]), sum_i[c])).astype(BF)
    right[:, 3 * HALF : RIGHT_E] = jnp.zeros((RANK, RIGHT_E - 3 * HALF), BF)
    for c in range(2):
        at = RIGHT_E + c * FF
        right[:, at : at + FF] = folded(nn(two_terms(found[4 + c]), sum_e[c])).astype(BF)
    right[:, RIGHT_O : RIGHT_O + D] = folded(nn(two_terms(own_o), sum_o[...])).astype(BF)
    right[:, RIGHT_S : RIGHT_S + D] = folded(nn(two_terms(own_s), sum_s[...])).astype(BF)


def factors_of(place, mine, other, gains, sum_i, sum_o, sum_e, sum_s):
    sums = (sum_i, sum_o, sum_e, sum_s)
    outs = [(3, RANK, D), (RANK, HALF), (2, RANK, D), (RANK, FF)]
    return pl.pallas_call(
        factor_kernel,
        in_specs=[SMEM, full((RANK, LEFT)), full((RANK, LEFT)), full((8, 2 * D))] + [HBM] * 4,
        out_specs=[full(s) for s in outs] + [full((RANK, RIGHT))],
        out_shape=[like(s, F32) for s in outs] + [like((RANK, RIGHT), BF)],
        scratch_shapes=[pltpu.VMEM(s.shape, BF) for s in sums] + [pltpu.SemaphoreType.DMA((4,))],
        compiler_params=params(24),
        cost_estimate=cost(10**8, 10 * 2**20),
    )(place, mine, other, gains, *sums)


def left_terms(v):
    one = v.astype(BF).astype(F32)
    two = v - one
    return jnp.concatenate([one, one, two, two], axis=0).astype(BF)


def right_terms(v):
    one = v.astype(BF).astype(F32)
    two = v - one
    return jnp.concatenate([one, two, one, two], axis=0).astype(BF)


def own_rows(terms, place):
    dp = (place[0] * 4 + place[1]) * 4 + place[2]
    row = lax.broadcasted_iota(jnp.int32, (16, D), 0)
    col = lax.broadcasted_iota(jnp.int32, (16, D), 1)
    pick = jnp.where((row < SHARD) & (col == row + SHARD * dp), 1.0, 0.0).astype(BF)
    return nt(pick, terms).astype(BF)


def moved(old, weight, rate, own, momentum, updated):
    new = momentum_decay * old + own
    momentum[...] = new
    updated[...] = weight - rate * new


LAST = 3


def last_kernel(place, *refs):
    left_i, left_o, left_e, left_s, sums, other, sum_i, sum_o, sum_e, sum_s = refs[:10]
    old_i, old_o, old_e, old_s, w_i, w_o, w_e, w_s, gains, old_g = refs[10:20]
    res_i, res_o, res_e, res_s, mom_i, mom_o, mom_e, mom_s, new_i, new_o, new_e, new_s = refs[20:32]
    right_i, right_o, right_e, right_s, mom_g, new_g = refs[32:38]
    l_i, l_o, l_e, l_s, r_i, r_o, r_e, r_s = refs[38:]
    j = pl.program_id(0)
    scale = 1.0 / 64
    tail = lambda n: (sums[:, RIGHT_O + n * D : RIGHT_O + (n + 1) * D] + other[:, n * D : (n + 1) * D])
    e_rights = [sums[:, RIGHT_E + c * FF : RIGHT_E + (c + 1) * FF] for c in range(2)]
    i_rights = [sums[:, c * HALF : (c + 1) * HALF] for c in range(3)]

    @pl.when(j == 0)
    def _():
        for c in range(2):
            l_e[c * D : (c + 1) * D, :] = left_terms(left_e[c]).T
            r_e[c] = right_terms(e_rights[c] * scale)
        l_s[...] = left_terms(left_s[...]).T
        r_s[...] = right_terms(tail(1) * scale)
        for c in range(3):
            l_i[c * D : (c + 1) * D, :] = left_terms(left_i[c]).T
            r_i[c] = right_terms(i_rights[c] * scale)
        l_o[...] = left_terms(left_o[...]).T
        r_o[...] = right_terms(tail(0) * scale)

    at = lambda n: pl.ds(pl.multiple_of(j * n, n), n)
    for h in range(2):
        rows = pl.ds(pl.multiple_of(j * 512 + h * 256, 256), 256)
        which = (2 * j + h) // 3
        here = slice(h * 256, (h + 1) * 256)
        res_e[here, :] = sum_e[here, :].astype(F32) - nn(l_e[rows, :], r_e[which])
    res_s[0] = sum_s[...].astype(F32) - nn(l_s[at(512), :], r_s[...])
    res_i[0, 0] = sum_i[0].astype(F32) - nn(l_i[at(D), :], r_i[j])
    res_o[0] = sum_o[...].astype(F32) - nn(l_o[at(128), :], r_o[...])

    @pl.when(j == 1)
    def _():
        for c in range(2):
            right_e[c] = e_rights[c] * scale
            own = nn(own_rows(left_terms(left_e[c]), place), r_e[c])[:SHARD]
            moved(old_e[:, c, :], w_e[:, c, :], rate_expand, own, mom_e.at[:, c, :], new_e.at[:, c, :])
        right_s[...] = tail(1) * scale
        own = nn(own_rows(r_s[...], place), left_terms(left_s[...]))[:SHARD]
        moved(old_s[...], w_s[...], rate_shrink, own, mom_s, new_s)
        for c in range(3):
            right_i[c] = i_rights[c] * scale
            own = nn(own_rows(left_terms(left_i[c]), place), r_i[c])[:SHARD]
            moved(old_i[c], w_i[c], rate_inbound, own, mom_i.at[c], new_i.at[c])
        right_o[...] = tail(0) * scale
        own = nn(own_rows(r_o[...], place), left_terms(left_o[...]))[:SHARD]
        moved(old_o[...], w_o[...], rate_outbound, own, mom_o, new_o)
        both = sums[:, RIGHT_G:] + other[:, RIGHT_G - RIGHT_O :]
        parts = [both[n % 8 : n % 8 + 1, n // 8 * 128 : (n // 8 + 1) * 128] for n in range(12)]
        for n in range(2):
            own = jnp.concatenate(parts[n * 6 : (n + 1) * 6], axis=1)
            row = slice(n, n + 1)
            moved(old_g[row], gains[row], rate_gains, own, mom_g.at[row], new_g.at[row])


def last(place, lefts, sums, other, made, old, w, gains, old_g):
    rows = lambda n, w: pl.BlockSpec((n, w), lambda j: (j, 0))
    sum_i, sum_o, sum_e, sum_s = made
    made = (sum_i, sum_o, sum_e.reshape(2 * D, FF), sum_s)
    small = [*lefts, sums, other]
    states = [*old, *w, gains, old_g]
    state_shapes = [(3, SHARD, HALF), (SHARD, HALF), (SHARD, 2, FF), (SHARD, FF)]
    rest_shapes = [(1, 3, D, HALF), (1, HALF, D), (2 * D, FF), (1, FF, D)]
    tails = [(3, RANK, HALF), (RANK, D), (2, RANK, FF), (RANK, D), (2, D), (2, D)]
    flat = state_shapes * 2 + tails
    outs = pl.pallas_call(
        last_kernel,
        grid=(LAST,),
        in_specs=[SMEM]
        + [full(a.shape) for a in small]
        + [pl.BlockSpec((1, D, HALF), lambda j: (j, 0, 0)), rows(128, D), rows(512, FF), rows(512, D)]
        + [full(a.shape) for a in states],
        out_specs=[
            pl.BlockSpec((1, 1, D, HALF), lambda j: (0, j, 0, 0)),
            pl.BlockSpec((1, 128, D), lambda j: (0, j, 0)),
            rows(512, FF),
            pl.BlockSpec((1, 512, D), lambda j: (0, j, 0)),
        ]
        + [full(s) for s in flat],
        out_shape=[like(s, F32) for s in rest_shapes + flat],
        scratch_shapes=[
            pltpu.VMEM((3 * D, 32), BF),
            pltpu.VMEM((HALF, 32), BF),
            pltpu.VMEM((2 * D, 32), BF),
            pltpu.VMEM((FF, 32), BF),
            pltpu.VMEM((3, 32, HALF), BF),
            pltpu.VMEM((32, D), BF),
            pltpu.VMEM((2, 32, FF), BF),
            pltpu.VMEM((32, D), BF),
        ],
        compiler_params=params(28),
        cost_estimate=cost(10**8, 30 * 2**20),
    )(place, *small, *made, *states)
    return (*outs[:2], outs[2].reshape(1, 2, D, FF), *outs[3:])


def lane_tables(ids):
    zeros = jnp.sum((ids == 0).astype(jnp.int32))
    ones = jnp.sum((ids == 1).astype(jnp.int32))
    before = jnp.where(ids == 0, 0, jnp.where(ids == 1, zeros, zeros + ones))
    places = (jnp.arange(SEQ, dtype=jnp.int32) - before).astype(F32)
    lane = jnp.arange(128, dtype=jnp.int32)
    inverse = rope_base ** (-((lane % 32).astype(F32) * 2.0) / HEAD_DIM)
    angles = places[:, None] * inverse[None, :]
    first = (lane % 64 < 32)[None, :]
    sine = jnp.sin(angles)
    low, high = jnp.where(first, -sine, 0.0), jnp.where(first, 0.0, sine)
    kind = lane[None, :]
    same = ids[:, None] == kind
    fq = jnp.where((kind < 3) & same, 1.0, 0.0).astype(BF)
    fk = jnp.where(kind < 3, jnp.where(same, 0.0, MASKED), jnp.where(kind < 6, 1.0, 0.0))
    return (jnp.cos(angles), low, high), fq, fk.astype(BF)


def both_halves(own, t):
    other = swap(own)
    whole = jnp.zeros((SEQ, D), BF)
    whole = lax.dynamic_update_slice_in_dim(whole, own, t * 512, 0)
    return lax.dynamic_update_slice_in_dim(whole, other, (1 - t) * 512, 0)


def local(
    tokens,
    segment_ids,
    cotangent,
    norm_gains,
    gains_moment,
    inbound,
    outbound,
    expand,
    shrink,
    inbound_moment,
    outbound_moment,
    expand_moment,
    shrink_moment,
    inbound_error,
    outbound_error,
    expand_error,
    shrink_error,
    inbound_start,
    outbound_start,
    expand_start,
    shrink_start,
):
    y, x, z, t = (lax.axis_index(a) for a in DP_TENSOR)
    place = jnp.stack([y, x, z, t]).astype(jnp.int32)

    shard = weight_shard(inbound, outbound.T, jnp.swapaxes(expand, 0, 1), shrink.T)
    shard, segment_ids, tokens, cotangent = lax.optimization_barrier(
        (shard, segment_ids, tokens, cotangent)
    )
    column = [shard, shift(shard, Z, 1), shift(shard, Z, 3), shift(shard, Z, 2)]
    tables, fq, fk = lane_tables(segment_ids)
    column, fq, fk = lax.optimization_barrier((column, fq, fk))
    quarter, feed_rows = rows_of_column(place, column)
    feed_weights = lax.all_gather(feed_rows, (Y, X)).reshape(D, 3 * FF)
    x_all = both_halves(tokens, t)
    quarter = rows_of_plane(quarter)
    cot_all = both_halves(cotangent, t)
    near = shift(quarter, Z, 1), shift(quarter, Z, 3)
    near, x_all, cot_all, tables = lax.optimization_barrier((near, x_all, cot_all, tables))
    far = shift(near[0][:HALF], Z, 1), shift(near[1][HALF:], Z, 3)
    in_pieces = [quarter, *near, *far]

    gain_one, gain_two = norm_gains[0:1], norm_gains[1:2]
    normed, weights, q, k, v, att, fq_all, w_out = attention(
        place, gain_one, x_all, tables, fq, fk, in_pieces
    )
    w_other, att_other = swap(w_out), swap(att)

    start_e, start_s = jnp.swapaxes(expand_start, 1, 2), shrink_start.T
    sum_e, sum_s, left_e, left_s, middle, grad, hid = feed(
        place,
        gain_two,
        x_all,
        att,
        att_other,
        w_out,
        w_other,
        cot_all,
        expand_error,
        shrink_error,
        feed_weights,
        start_e,
        start_s,
    )
    grad_other = swap(grad)
    middle_grad, sum_o, dproj, sum_i, gain_second, left = backward(
        place,
        gain_two,
        outbound_start.T,
        jnp.swapaxes(inbound_start, 1, 2),
        grad_other,
        grad,
        middle,
        cot_all,
        att,
        w_out,
        outbound_error,
        q,
        k,
        v,
        fq_all,
        fk,
        *tables,
        normed,
        inbound_error,
        left_e,
        left_s,
    )

    left, dproj = lax.optimization_barrier((left, dproj))
    terms = ring_terms(left, Z)
    first_own, first_send = first_grad_rows(place, dproj, weights)
    terms, first_own, first_send = lax.optimization_barrier((terms, first_own, first_send))
    terms = ring_terms(rounded(ring_sum(terms)), X)
    first_other = swap(first_send)
    terms, first_other = lax.optimization_barrier((terms, first_other))
    terms = ring_terms(rounded(ring_sum(terms)), Y)
    input_grad, gains = input_grad_rows(
        tokens, gain_one, middle_grad, first_own, first_other, gain_second
    )
    terms, gains = lax.optimization_barrier((terms, gains))
    mine = ring_sum(terms)
    left_i, left_o, left_e, left_s, right = factors_of(
        place, mine, swap(mine), gains, sum_i, sum_o, sum_e, sum_s
    )

    right, hid = lax.optimization_barrier((right, hid))
    terms = ring_terms(right, Z)
    own_out, send_out = down_rows(place, hid, feed_weights)
    terms, own_out, send_out = lax.optimization_barrier((terms, own_out, send_out))
    terms = ring_terms(rounded(ring_sum(terms)), X)
    send_out = swap(send_out)
    terms, send_out = lax.optimization_barrier((terms, send_out))
    terms = ring_terms(rounded(ring_sum(terms)), Y)
    own_middle = lax.dynamic_slice_in_dim(middle, t * 512, 512, 0)
    layer_output = (own_middle + (own_out + send_out.astype(F32))).astype(BF)
    terms, layer_output = lax.optimization_barrier((terms, layer_output))
    sums = ring_sum(terms)
    (
        res_i,
        res_o,
        res_e,
        res_s,
        inbound_momentum,
        outbound_momentum,
        expand_momentum,
        shrink_momentum,
        inbound_updated,
        outbound_updated,
        expand_updated,
        shrink_updated,
        right_i,
        right_o,
        right_e,
        right_s,
        gains_momentum,
        gains_updated,
    ) = last(
        place,
        (left_i, left_o, left_e, left_s),
        sums,
        swap(sums[:, RIGHT_O:]),
        (sum_i, sum_o, sum_e, sum_s),
        (inbound_moment, outbound_moment.T, jnp.swapaxes(expand_moment, 0, 1), shrink_moment.T),
        (inbound, outbound.T, jnp.swapaxes(expand, 0, 1), shrink.T),
        norm_gains,
        gains_moment,
    )
    return (
        layer_output,
        input_grad,
        gains_momentum,
        gains_updated,
        inbound_momentum,
        outbound_momentum.T,
        jnp.swapaxes(expand_momentum, 0, 1),
        shrink_momentum.T,
        inbound_updated,
        outbound_updated.T,
        jnp.swapaxes(expand_updated, 0, 1),
        shrink_updated.T,
        res_i,
        res_o,
        res_e,
        res_s,
        jnp.swapaxes(left_i, 1, 2),
        jnp.swapaxes(right_i, 1, 2),
        left_o.T,
        right_o.T,
        jnp.swapaxes(left_e, 1, 2),
        jnp.swapaxes(right_e, 1, 2),
        left_s.T,
        right_s.T,
    )


def solution(mesh):
    torus = Mesh(mesh.devices.reshape(4, 4, 4, mesh.shape["tensor"]), DP_TENSOR)
    return jax.shard_map(
        local,
        mesh=torus,
        in_specs=(
            P(DP_TENSOR, None),
            P(DP),
            P(DP_TENSOR, None),
            P(),
            P(),
            P(None, DP, T),
            P(T, DP),
            P(None, DP, T),
            P(T, DP),
            P(None, DP, T),
            P(T, DP),
            P(None, DP, T),
            P(T, DP),
            P(DP, None, None, T),
            P(DP, T, None),
            P(DP, None, None, T),
            P(DP, T, None),
            P(None, T, None),
            P(),
            P(None, T, None),
            P(),
        ),
        out_specs=(
            P(DP_TENSOR, None),
            P(DP_TENSOR, None),
            P(),
            P(),
            P(None, DP, T),
            P(T, DP),
            P(None, DP, T),
            P(T, DP),
            P(None, DP, T),
            P(T, DP),
            P(None, DP, T),
            P(T, DP),
            P(DP, None, None, T),
            P(DP, T, None),
            P(DP, None, None, T),
            P(DP, T, None),
            P(),
            P(None, T, None),
            P(T, None),
            P(),
            P(),
            P(None, T, None),
            P(T, None),
            P(),
        ),
        check_vma=False,
    )
```
